32 devices in a mesh: dp: 8 (over y, x, core), mp: 4 (over z).
Axes of the slice: x: 2, y: 2, z: 4, core: 2. Of those that a mesh axis runs over, the one named last changes fastest.
Arguments:
- tokens: bfloat16 [4096, 768], P(('dp', 'mp'))
- cotangent: bfloat16 [4096, 768], P(('dp', 'mp')), may hold values from -6 to 6
- seq_starts: int32 [8, 8], P('dp'), may hold values from 0 to 511, as said below
- attn_weight: float32 [4, 768, 768], replicated
- up_weight: float32 [768, 3072], P(None, 'mp')
- down_weight: float32 [3072, 768], P('mp')
- vec_params: float32 [4, 768], replicated
- attn_stats: float32 [4, 2, 768], replicated
- ffn_narrow_stats: float32 [2, 768], replicated
- ffn_wide_stats: float32 [2, 3072], P(None, 'mp')
- vec_moment: float32 [4, 768], replicated
Outputs:
- block_out: float32 [4096, 768], P(('dp', 'mp'))
- tokens_grad: float32 [4096, 768], P(('dp', 'mp'))
- attn_grad: float32 [4, 768, 768], P(None, 'mp')
- attn_row_stats: float32 [4, 768], P(None, 'mp')
- attn_col_stats: float32 [4, 768], replicated
- attn_new: float32 [4, 768, 768], P(None, 'mp')
- attn_new_low: bfloat16 [4, 768, 768], P(None, 'mp')
- up_grad: float32 [768, 3072], P(None, 'mp')
- down_grad: float32 [3072, 768], P('mp')
- ffn_narrow_new: float32 [2, 768], replicated
- ffn_wide_new: float32 [2, 3072], P(None, 'mp')
- up_new: float32 [768, 3072], P(None, 'mp')
- down_new: float32 [3072, 768], P('mp')
- up_new_low: bfloat16 [768, 3072], P(None, 'mp')
- down_new_low: bfloat16 [3072, 768], P('mp')
- vec_grad: float32 [4, 768], replicated
- vec_moment_new: float32 [4, 768], replicated
- vec_new: float32 [4, 768], replicated
The draws below stay inside these ranges and needn't reach their ends.
Inputs may be any that keep to these rules, and one draw needn't show every extreme that they name: `seq_starts`: each row rises strictly from 0; its sequences fill the pack's 512 tokens. One sequence of each pack, at a place drawn from the seed, is at least 386 tokens long; the others have 1 to 18 tokens. In one pack, drawn from the seed, the last sequence is a single token.
All inputs are finite; a program needn't handle non-finite values.
Results may differ from the reference program's by a relative error of at most 0.0094.
Values may be sent and summed in bfloat16 or wider, within the bound.
No kernel may reach another device: no remote copies, remote signals or barrier semaphores. Data moves between devices by JAX's collectives and lax.ppermute only.
A program may use at most 192 MiB of HBM per device.

```python
import math
import jax
import jax.numpy as jnp
from jax import lax

D = 768
HEADS = 12
FF = 3072
SPAN = 64
STEP = 10
SEQS = 8
GROUP = 512
TOKENS = 4096
SHORT_MAX = 18


def old_ratio():
    decay = 1.0 - float(STEP) ** (-0.8)
    return (1.0 - decay) / decay


def log_factor(key, shape, lower, upper):
    return jnp.exp(jax.random.uniform(key, shape, jnp.float32, math.log(lower), math.log(upper)))


def draw_tokens(key, part):
    key = jax.random.fold_in(key, 11)
    ramp = jnp.linspace(0.6, 1.5, D)
    values = jax.random.normal(key, (TOKENS, D), jnp.float32)
    return (values * ramp[None, :]).astype(jnp.bfloat16)


def draw_seq_starts(key, part):
    key = jax.random.fold_in(key, 3)
    short_key, slot_key, other_key, pack_key = jax.random.split(key, 4)
    pack_count = TOKENS // GROUP
    positions = jnp.arange(SEQS)[None, :]
    shorts = jax.random.randint(short_key, (pack_count, SEQS), 1, SHORT_MAX + 1)
    slots = jax.random.randint(slot_key, (pack_count, 1), 0, SEQS)
    other_slots = jax.random.randint(other_key, (pack_count, 1), 0, SEQS - 1)
    special = jax.random.randint(pack_key, (), 0, pack_count)
    is_special = jnp.arange(pack_count)[:, None] == special
    slots = jnp.where(is_special, other_slots, slots)
    shorts = jnp.where(is_special & (positions == SEQS - 1), 1, shorts)
    is_long = positions == slots
    short_total = jnp.sum(jnp.where(is_long, 0, shorts), axis=1, keepdims=True)
    lengths = jnp.where(is_long, GROUP - short_total, shorts)
    return (jnp.cumsum(lengths, axis=1) - lengths).astype(jnp.int32)


def draw_attn_weight(key, part):
    key = jax.random.fold_in(key, 7)
    ramp = jnp.linspace(0.6, 1.5, D)
    values = jax.random.normal(key, (4, D, D), jnp.float32)
    factors = jnp.array([1.0, 1.0, 1.0, 8.0], jnp.float32) * D ** (-0.5)
    return values * ramp[None, :, None] * ramp[None, None, :] * factors[:, None, None]


def draw_up_weight(key, part):
    key = jax.random.fold_in(key, 13)
    ramp = jnp.linspace(0.6, 1.5, FF)
    values = jax.random.normal(key, (D, FF), jnp.float32)
    return values * ramp[None, :] * D ** (-0.5)


def draw_down_weight(key, part):
    key = jax.random.fold_in(key, 17)
    ramp = jnp.linspace(0.6, 1.5, FF)
    values = jax.random.normal(key, (FF, D), jnp.float32)
    return values * ramp[:, None] * FF ** (-0.5)


def draw_vec_params(key, part):
    key = jax.random.fold_in(key, 19)
    noise = jax.random.uniform(key, (4, D), jnp.float32, -1.0, 1.0)
    gains = jnp.linspace(0.8, 1.2, D)[None, :] * (1.0 + 0.15 * noise)
    is_gain = (jnp.arange(4) % 2 == 0)[:, None]
    return jnp.where(is_gain, gains, 0.5 * noise)


def draw_attn_stats(key, part):
    key = jax.random.fold_in(key, 23)
    base = 0.25 * TOKENS * old_ratio()
    ramp = jnp.exp(jnp.linspace(math.log(1.5), math.log(0.3), D))
    return base * log_factor(key, (4, 2, D), 0.5, 1.5) * ramp[None, None, :]


def draw_ffn_narrow_stats(key, part):
    key = jax.random.fold_in(key, 29)
    base = 0.25 * TOKENS * old_ratio()
    return base * log_factor(key, (2, D), 0.5, 1.5)


def draw_ffn_wide_stats(key, part):
    key = jax.random.fold_in(key, 31)
    base = 0.25 * TOKENS * old_ratio()
    ramp = jnp.exp(jnp.linspace(math.log(1.5), math.log(0.1), FF))
    return base * log_factor(key, (2, FF), 0.5, 1.5) * ramp[None, :]


def draw_vec_moment(key, part):
    key = jax.random.fold_in(key, 37)
    base = 1.0 * TOKENS * old_ratio()
    return base * log_factor(key, (4, D), 0.3, 1.5)


def shard_levels(stream_key, shape, pieces, least, high):
    level, own = 1.0, jax.random.fold_in(stream_key, 6)
    for dim, blocks in pieces:
        steps = jnp.exp(jax.random.uniform(jax.random.fold_in(own, dim), (blocks,), jnp.float32, least / len(pieces), high / len(pieces)))
        level = level * jnp.repeat(steps, shape[dim] // blocks).reshape([-1 if axis == dim else 1 for axis in range(len(shape))])
    return level


def bell_draw(stream_key, shape, scale, reach, cuts=(), kind=jnp.bfloat16):
    level = shard_levels(stream_key, shape, cuts, -0.22, 0.18) if cuts else 1.0
    values = jax.random.normal(stream_key, shape, jnp.float32) * scale * level
    return jnp.minimum(jnp.maximum(values, -reach), reach).astype(kind)


def setup_inputs(seed: int = 0) -> dict:
    arg_keys = jax.random.split(jax.random.key(seed), 12)
    return {
        "tokens": draw_tokens(jax.random.fold_in(arg_keys[11], 71), 0),
        "cotangent": bell_draw(arg_keys[1], (TOKENS, D), 1.0, 6.0, ((0, 32),)),
        "seq_starts": draw_seq_starts(jax.random.fold_in(arg_keys[11], 71), 0),
        "attn_weight": draw_attn_weight(jax.random.fold_in(arg_keys[11], 71), 0),
        "up_weight": draw_up_weight(jax.random.fold_in(arg_keys[11], 71), 0),
        "down_weight": draw_down_weight(jax.random.fold_in(arg_keys[11], 71), 0),
        "vec_params": draw_vec_params(jax.random.fold_in(arg_keys[11], 71), 0),
        "attn_stats": draw_attn_stats(jax.random.fold_in(arg_keys[11], 71), 0),
        "ffn_narrow_stats": draw_ffn_narrow_stats(jax.random.fold_in(arg_keys[11], 71), 0),
        "ffn_wide_stats": draw_ffn_wide_stats(jax.random.fold_in(arg_keys[11], 71), 0),
        "vec_moment": draw_vec_moment(jax.random.fold_in(arg_keys[11], 71), 0),
    }


@jax.custom_vjp
def low(v):
    return lax.optimization_barrier(v.astype(jnp.bfloat16)).astype(jnp.float32)

@jax.custom_vjp
def low_back(v):
    return v

def low_keep(v):
    return (low(v), None)

def low_pass(kept, grad):
    return (grad,)

def back_keep(v):
    return (v, None)

def back_low(kept, grad):
    return (low(grad),)
low.defvjp(low_keep, low_pass)
low_back.defvjp(back_keep, back_low)
norm_eps = 1e-05
tiny_square = 1e-30
learn_rate = 0.3
clip_limit = 1.0

def layer_norm(inputs, gains, shifts):
    center_mean = lax.optimization_barrier(jnp.mean(inputs, axis=-1, keepdims=True))
    centered = inputs - center_mean
    variance = lax.optimization_barrier(jnp.mean(centered * centered, axis=-1, keepdims=True))
    return centered * lax.rsqrt(variance + norm_eps) * gains + shifts

def exact_gelu(values):
    return jax.nn.gelu(values, approximate=False)

def seq_layout(starts, token_count):
    indices = jnp.arange(token_count, dtype=jnp.int32)
    seq_ids = lax.optimization_barrier(jnp.sum((indices[:, None] >= starts[None, :]).astype(jnp.int32), axis=1)) - 1
    finish = jnp.concatenate([starts[1:], jnp.full((1,), token_count, jnp.int32)])
    choose_seq = (seq_ids[:, None] == jnp.arange(starts.shape[0], dtype=jnp.int32)[None, :]).astype(jnp.int32)
    begins = lax.optimization_barrier(jnp.sum(choose_seq * starts[None, :], axis=1))
    lengths = lax.optimization_barrier(jnp.sum(choose_seq * (finish - starts)[None, :], axis=1))
    angles = 0.5 * math.pi * (indices - begins).astype(jnp.float32) / lengths.astype(jnp.float32)
    return (seq_ids, angles)

def chain_combine(earlier, later_part):
    flags = later_part[0]
    return (earlier[0] * flags, flags[:, None, None, None] * earlier[1] + later_part[1], flags[:, None, None] * earlier[2] + later_part[2])

def linear_core(query, key_rows, value_rows, seq_ids, angles, head_count, span_len):
    token_count, width = query.shape
    head_size = width // head_count
    blocks = token_count // span_len
    highest = lax.Precision.HIGHEST
    cosine = jnp.cos(angles)[:, None, None]
    sine = jnp.sin(angles)[:, None, None]
    query_feat = jax.nn.softplus(query).reshape(token_count, head_count, head_size)
    key_feat = jax.nn.softplus(key_rows).reshape(token_count, head_count, head_size)
    query_full = jnp.concatenate([query_feat * cosine, query_feat * sine], axis=2).reshape(blocks, span_len, head_count, 2 * head_size)
    key_full = jnp.concatenate([key_feat * cosine, key_feat * sine], axis=2).reshape(blocks, span_len, head_count, 2 * head_size)
    value_blocks = value_rows.reshape(blocks, span_len, head_count, head_size)
    block_ids = seq_ids.reshape(blocks, span_len)
    last_ids = block_ids[:, -1]
    before_ids = jnp.concatenate([jnp.full((1,), -1, jnp.int32), last_ids[:-1]])
    places = jnp.arange(span_len)
    allowed = (block_ids[:, :, None] == block_ids[:, None, :]) & (places[:, None] >= places[None, :])[None]
    scores = jnp.einsum('bthf,buhf->bhtu', query_full, key_full, precision=highest)
    scores = scores * allowed[:, None].astype(scores.dtype)
    own_flags = (block_ids == last_ids[:, None]).astype(scores.dtype)
    key_own = key_full * own_flags[:, :, None, None]
    span_terms = jnp.einsum('buhf,buhd->bhfd', key_own, value_blocks, precision=highest)
    span_sums = lax.optimization_barrier(jnp.sum(key_own, axis=1))
    keep_flags = (last_ids == before_ids).astype(scores.dtype)
    scanned = lax.associative_scan(chain_combine, (keep_flags, span_terms, span_sums))
    state_in = jnp.concatenate([jnp.zeros_like(scanned[1][:1]), scanned[1][:-1]], axis=0)
    total_in = jnp.concatenate([jnp.zeros_like(scanned[2][:1]), scanned[2][:-1]], axis=0)
    use_state = (block_ids == before_ids[:, None]).astype(scores.dtype)
    numerator = jnp.einsum('bhtu,buhd->bthd', scores, value_blocks, precision=highest)
    numerator = numerator + use_state[:, :, None, None] * jnp.einsum('bthf,bhfd->bthd', query_full, state_in, precision=highest)
    denominator = jnp.einsum('bhtu->bth', scores)
    denominator = denominator + use_state[:, :, None] * jnp.einsum('bthf,bhf->bth', query_full, total_in, precision=highest)
    return (numerator / denominator[:, :, :, None]).reshape(token_count, width)

def block(inputs, starts, attn, up_mat, down_mat, vecs):
    highest = lax.Precision.HIGHEST
    seq_ids, angles = seq_layout(starts, inputs.shape[0])
    query = low_back(jnp.dot(inputs, low(attn[0]), precision=highest))
    key_rows = low_back(jnp.dot(inputs, low(attn[1]), precision=highest))
    value_rows = low_back(jnp.dot(inputs, low(attn[2]), precision=highest))
    mixed = linear_core(query, key_rows, value_rows, seq_ids, angles, HEADS, SPAN)
    attn_out = low_back(jnp.dot(low(mixed), low(attn[3]), precision=highest))
    normed_first = layer_norm(inputs + attn_out, vecs[0], vecs[1])
    pre_act = low_back(jnp.dot(low(normed_first), low(up_mat), precision=highest))
    hidden = low(exact_gelu(pre_act))
    branch = low_back(jnp.dot(hidden, low(down_mat), precision=highest))
    return layer_norm(normed_first + branch, vecs[2], vecs[3])

def factored_update(weight, grad, rows_old, cols_old):
    decay = 1.0 - float(STEP) ** (-0.8)
    square = grad * grad + tiny_square
    rows_new = decay * rows_old + (1.0 - decay) * lax.optimization_barrier(jnp.mean(square, axis=-1))
    cols_new = decay * cols_old + (1.0 - decay) * lax.optimization_barrier(jnp.mean(square, axis=-2))
    scale = rows_new[..., :, None] * cols_new[..., None, :] / lax.optimization_barrier(jnp.mean(rows_new, axis=-1))[..., None, None]
    scaled = grad * lax.rsqrt(scale)
    clip_factor = jnp.maximum(1.0, jnp.sqrt(lax.optimization_barrier(jnp.mean(scaled * scaled, axis=(-2, -1)))) / clip_limit)[..., None, None]
    spread = jnp.sqrt(lax.optimization_barrier(jnp.mean(weight * weight, axis=(-2, -1))))[..., None, None]
    return (rows_new, cols_new, weight - learn_rate * spread * scaled / clip_factor)

def vector_update(params, grads, moment):
    decay = 1.0 - float(STEP) ** (-0.8)
    new_moment = decay * moment + (1.0 - decay) * (grads * grads + tiny_square)
    scaled = grads * lax.rsqrt(new_moment)
    clip_factor = jnp.maximum(1.0, jnp.sqrt(lax.optimization_barrier(jnp.mean(scaled * scaled, axis=1, keepdims=True))) / clip_limit)
    spread = jnp.sqrt(lax.optimization_barrier(jnp.mean(params * params, axis=1, keepdims=True)))
    return (new_moment, params - learn_rate * spread * scaled / clip_factor)

def reference(tokens, cotangent, seq_starts, attn_weight, up_weight, down_weight, vec_params, attn_stats, ffn_narrow_stats, ffn_wide_stats, vec_moment):
    pack_count = seq_starts.shape[0]
    packs = tokens.astype(jnp.float32).reshape(pack_count, -1, D)
    pack_cots = cotangent.astype(jnp.float32).reshape(pack_count, -1, D)

    def one_pack(totals, item):
        pack_in, pack_cot, starts = item

        def run(inputs, attn, up_mat, down_mat, vecs):
            return block(inputs, starts, attn, up_mat, down_mat, vecs)
        result, pullback = jax.vjp(run, pack_in, attn_weight, up_weight, down_weight, vec_params)
        grads = pullback(pack_cot)
        totals = tuple((total + grad for total, grad in zip(totals, grads[1:])))
        return (totals, (result, grads[0]))
    zeros = (jnp.zeros_like(attn_weight), jnp.zeros_like(up_weight), jnp.zeros_like(down_weight), jnp.zeros_like(vec_params))
    totals, (results, input_grads) = lax.scan(one_pack, zeros, (packs, pack_cots, seq_starts))
    attn_grad, up_grad, down_grad, vec_grad = totals
    attn_rows, attn_cols, attn_new = factored_update(attn_weight, attn_grad, attn_stats[:, 0], attn_stats[:, 1])
    up_rows, up_cols, up_new = factored_update(up_weight, up_grad, ffn_narrow_stats[0], ffn_wide_stats[0])
    down_rows, down_cols, down_new = factored_update(down_weight, down_grad, ffn_wide_stats[1], ffn_narrow_stats[1])
    vec_moment_new, vec_new = vector_update(vec_params, vec_grad, vec_moment)
    return (results.reshape(-1, D), input_grads.reshape(-1, D), attn_grad, attn_rows, attn_cols, attn_new, attn_new.astype(jnp.bfloat16), up_grad, down_grad, jnp.stack([up_rows, down_cols]), jnp.stack([up_cols, down_rows]), up_new, down_new, up_new.astype(jnp.bfloat16), down_new.astype(jnp.bfloat16), vec_grad, vec_moment_new, vec_new)
```

```python
import functools
import math

import jax
import jax.numpy as jnp
from jax import lax
from jax.experimental import pallas as pl
from jax.experimental.pallas import tpu as pltpu
from jax.sharding import PartitionSpec as P

HEADS = 12
STEP = 10

norm_eps = 1e-05
tiny_square = 1e-30
learn_rate = 0.3
clip_limit = 1.0
decay = 1.0 - float(STEP) ** (-0.8)

f32 = jnp.float32
bf16 = jnp.bfloat16

NN = (((1,), (0,)), ((), ()))
NT = (((1,), (1,)), ((), ()))
TN = (((0,), (0,)), ((), ()))


def mm(a, b, dims=NN):
    return lax.dot_general(a, b, dims, preferred_element_type=f32)


def params(mib):
    return pltpu.CompilerParams(vmem_limit_bytes=mib * 1024 * 1024)


def sds(shape, dtype):
    return jax.ShapeDtypeStruct(shape, dtype)


def in_hbm(array):
    return pltpu.with_memory_space_constraint(array, pltpu.HBM)


STAGED = 8
EVEN_A = (0, 4, 2, 6)
EVEN_B = (0, 2, 4, 6)
VEC_ROWS = 16


def chunk_rows(index, name, rows):
    return pl.ds(pl.multiple_of((index ^ name) * rows, rows), rows)


def write_pieces(index, half_a, half_b, keep, send, rows):
    for half, names, base in ((half_a, EVEN_A, 0), (half_b, EVEN_B, 4 * rows)):
        for n, name in enumerate(names):
            here = slice(base + n * rows, base + (n + 1) * rows)
            keep[here, :] = half[chunk_rows(index, name, rows), :]
            send[here, :] = half[chunk_rows(index, name | 1, rows), :].astype(send.dtype)


def read_pieces(index, even, odd, half_a, half_b, rows):
    for half, names, base in ((half_a, EVEN_A, 0), (half_b, EVEN_B, 4 * rows)):
        for n, name in enumerate(names):
            here = slice(base + n * rows, base + (n + 1) * rows)
            half[chunk_rows(index, name, rows), :] = even[here, :].astype(half.dtype)
            half[chunk_rows(index, name | 1, rows), :] = odd[here, :].astype(half.dtype)


def two_parts(values):
    high = values.astype(bf16)
    return high, (values - high.astype(f32)).astype(bf16)


def joined(block):
    return block[0:4, :].astype(f32) + block[4:8, :].astype(f32)


def fold_first_kernel(rows, keep, received, *refs):
    keep_a, send_a, keep_b, send_b = refs[-4:]
    total = keep[...] + received[0 : 8 * rows, :].astype(f32)
    keep_a[...] = total[0 : 2 * rows]
    send_a[0 : 2 * rows, :] = total[2 * rows : 4 * rows].astype(bf16)
    keep_b[...] = total[4 * rows : 6 * rows]
    send_b[...] = total[6 * rows : 8 * rows].astype(bf16)
    if len(refs) > 4:
        vec, vec_out = refs[0:2]
        fold_vec(vec, received[8 * rows :, :], vec_out, send_a, 2 * rows)


def fold_vec(vec, received, vec_out, send, place):
    total = vec[0:4, :] + joined(received)
    high, low = two_parts(total)
    vec_out[0:4, :] = high.astype(f32) + low.astype(f32)
    vec_out[4:8, :] = jnp.zeros_like(total)
    if send is not None:
        tail = jnp.concatenate([high.astype(f32), low.astype(f32)], axis=0)
        send[place : place + VEC_ROWS, :] = jnp.concatenate([tail, jnp.zeros_like(tail)], axis=0).astype(bf16)


def fold_second_kernel(rows, keep_a, received_a, keep_b, received_b, *refs):
    next_a, send_a, next_b, send_b = refs[-4:]
    total = keep_a[...] + received_a[0 : 2 * rows, :].astype(f32)
    next_a[...] = total[0:rows]
    send_a[0:rows, :] = total[rows : 2 * rows].astype(bf16)
    total = keep_b[...] + received_b[...].astype(f32)
    next_b[...] = total[0:rows]
    send_b[...] = total[rows : 2 * rows].astype(bf16)
    if len(refs) > 4:
        vec, vec_out = refs[0:2]
        fold_vec(vec, received_a[2 * rows :, :], vec_out, send_a, rows)


def fold_third_kernel(rows, keep_a, received_a, keep_b, received_b, *refs):
    last_a, last_b = refs[-2:]
    last_a[...] = (keep_a[...] + received_a[0:rows, :].astype(f32)).astype(bf16)
    last_b[...] = (keep_b[...] + received_b[...].astype(f32)).astype(bf16)
    if len(refs) > 2:
        vec, vec_out = refs[0:2]
        fold_vec(vec, received_a[rows:, :], vec_out, None, 0)


def fold_call(kernel, name, rows, inputs, vec, outs):
    width = inputs[0].shape[1]
    extra_in, extra_out = ([], []) if vec is None else ([vec], [sds((8, width), f32)])
    return pl.pallas_call(
        functools.partial(kernel, rows),
        out_shape=extra_out + [sds((r, width), t) for r, t in outs],
        compiler_params=params(8),
        name=name,
    )(*inputs, *extra_in)


def fold_first(rows, keep, received, vec=None):
    tail = 0 if vec is None else VEC_ROWS
    outs = [(2 * rows, f32), (2 * rows + tail, bf16), (2 * rows, f32), (2 * rows, bf16)]
    return fold_call(fold_first_kernel, "fold_first", rows, (keep, received), vec, outs)


def fold_second(rows, keep_a, received_a, keep_b, received_b, vec=None):
    tail = 0 if vec is None else VEC_ROWS
    outs = [(rows, f32), (rows + tail, bf16), (rows, f32), (rows, bf16)]
    return fold_call(fold_second_kernel, "fold_second", rows, (keep_a, received_a, keep_b, received_b), vec, outs)


def fold_third(rows, keep_a, received_a, keep_b, received_b, vec=None):
    outs = [(rows, bf16), (rows, bf16)]
    return fold_call(fold_third_kernel, "fold_third", rows, (keep_a, received_a, keep_b, received_b), vec, outs)


def across(block, bit):
    return lax.ppermute(block, "dp", [(i, i ^ bit) for i in range(STAGED)])


def prepare_kernel(seqs, tokens_pack, starts, attn, up, down, attn_low, up_low, down_low, mask, mask_t, squares):
    step = pl.program_id(0)

    @pl.when(step == 0)
    def _():
        squares[...] = jnp.zeros_like(squares)

    for k in range(4):
        block = attn[k]
        attn_low[k] = block.astype(bf16)
        squares[k : k + 1, :] += jnp.sum(block * block, axis=0, keepdims=True)
    for k, (source, target) in enumerate(((up, up_low), (down, down_low))):
        block = source[...]
        target[...] = block.astype(bf16)
        squares[4 + k : 5 + k, :] += jnp.sum(block * block, axis=0, keepdims=True)

    def layout(index):
        seq = jnp.zeros_like(index)
        begin = jnp.zeros_like(index)
        length = jnp.ones_like(index)
        for s in range(seqs):
            start = starts[0, s]
            finish = starts[0, s + 1] if s + 1 < seqs else tokens_pack
            inside = index >= start
            seq = jnp.where(inside, s, seq)
            begin = jnp.where(inside, start, begin)
            length = jnp.where(inside, finish - start, length)
        angle = 0.5 * math.pi * (index - begin).astype(f32) / length.astype(f32)
        return seq, jnp.cos(angle), jnp.sin(angle)

    rows = mask.shape[0]
    row = lax.broadcasted_iota(jnp.int32, (rows, 128), 0) + step * rows
    col = lax.broadcasted_iota(jnp.int32, (8, tokens_pack), 1)
    row_seq, row_cos, row_sin = (a[:, 0:1] for a in layout(row))
    col_seq, col_cos, col_sin = (a[0:1, :] for a in layout(col))
    same = row_seq == col_seq
    value = row_cos * col_cos + row_sin * col_sin
    row, col = row[:, 0:1], col[0:1, :]
    mask[...] = jnp.where(same & (col <= row), value, 0.0)
    mask_t[...] = jnp.where(same & (row <= col), value, 0.0)


def prepare(seq_starts, attn_weight, up_weight, down_weight, tokens_pack):
    steps = 8
    seqs = seq_starts.shape[1]
    heads4, width, _ = attn_weight.shape
    hidden = up_weight.shape[1]
    a_rows, u_rows, d_rows, m_rows = width // steps, width // steps, hidden // steps, tokens_pack // steps
    return pl.pallas_call(
        functools.partial(prepare_kernel, seqs, tokens_pack),
        grid=(steps,),
        in_specs=[
            pl.BlockSpec(memory_space=pltpu.SMEM),
            pl.BlockSpec((4, a_rows, width), lambda i: (0, i, 0)),
            pl.BlockSpec((u_rows, hidden), lambda i: (i, 0)),
            pl.BlockSpec((d_rows, width), lambda i: (i, 0)),
        ],
        out_specs=[
            pl.BlockSpec((4, a_rows, width), lambda i: (0, i, 0)),
            pl.BlockSpec((u_rows, hidden), lambda i: (i, 0)),
            pl.BlockSpec((d_rows, width), lambda i: (i, 0)),
            pl.BlockSpec((m_rows, tokens_pack), lambda i: (i, 0)),
            pl.BlockSpec((m_rows, tokens_pack), lambda i: (i, 0)),
            pl.BlockSpec((8, width), lambda i: (0, 0)),
        ],
        out_shape=[
            sds((4, width, width), bf16),
            sds((width, hidden), bf16),
            sds((hidden, width), bf16),
            sds((tokens_pack, tokens_pack), f32),
            sds((tokens_pack, tokens_pack), f32),
            sds((8, width), f32),
        ],
        compiler_params=params(16),
        cost_estimate=pl.CostEstimate(flops=10_000_000, bytes_accessed=22_000_000, transcendentals=0),
        name="prepare",
    )(seq_starts, in_hbm(attn_weight), in_hbm(up_weight), in_hbm(down_weight))


def half_lanes(width):
    return lax.broadcasted_iota(jnp.int32, (1, width), 1) < width // 2


def norm_parts(values):
    centered = values - jnp.mean(values, axis=-1, keepdims=True)
    spread = lax.rsqrt(jnp.mean(centered * centered, axis=-1, keepdims=True) + norm_eps)
    return centered * spread, spread


def norm_back(grad, unit, spread, gain):
    scaled = grad * gain
    return spread * (
        scaled
        - jnp.mean(scaled, axis=-1, keepdims=True)
        - unit * jnp.mean(scaled * unit, axis=-1, keepdims=True)
    )


def causal_blocks(tokens, size):
    return [(i, min(size, tokens - i)) for i in range(0, tokens, size)]


def forward_kernel(
    local,
    x0,
    x1,
    x2,
    x3,
    attn_low,
    up_low,
    down_low,
    mask,
    vec,
    x_all,
    query_feat,
    key_feat,
    value_low,
    query_slope,
    key_slope,
    mixed_low,
    inverse,
    own_sum,
    own_first,
    first_low,
    slope,
    hidden_low,
    part0,
    part1,
    part2,
    part3,
    branch,
):
    rank = lax.axis_index("mp")
    tokens, width = x_all.shape
    ranks = tokens // local

    def place(k):
        return pl.ds(pl.multiple_of(lax.rem(rank + k, ranks) * local, local), local)

    for k, block in enumerate((x0, x1, x2, x3)):
        x_all[place(ranks - k), :] = block[...]

    piece = 256
    for c in range(0, width, piece):
        cols = slice(c, c + piece)
        for which, feat, grad in ((0, query_feat, query_slope), (1, key_feat, key_slope)):
            raw = mm(x_all[...], attn_low[which, :, cols])
            feat[:, cols] = jax.nn.softplus(raw).astype(bf16)
            grad[:, cols] = jax.nn.sigmoid(raw).astype(bf16)
        value_low[:, cols] = mm(x_all[...], attn_low[2, :, cols]).astype(bf16)

    pair = 2 * (width // HEADS)
    first_half = half_lanes(pair)
    for c in range(0, width, pair):
        cols = slice(c, c + pair)
        keys = key_feat[:, cols]
        values = value_low[:, cols]
        zero = jnp.zeros_like(keys)
        one = jnp.ones_like(values)
        for i, rows in causal_blocks(tokens, 256):
            here = slice(i, i + rows)
            upto = i + rows
            queries = query_feat[here, cols]
            results = []
            for own in (first_half, ~first_half):
                scores = mm(queries, jnp.where(own, keys[:upto], zero[:upto]), NT)
                scores = (scores * mask[here, :upto]).astype(bf16)
                results.append(mm(scores, jnp.where(own, values[:upto], one[:upto])))
            numerator = jnp.where(first_half, results[0], results[1])
            denominator = pltpu.roll(jnp.where(first_half, results[1], results[0]), pair // 2, 1)
            inv = 1.0 / denominator
            inverse[here, cols] = inv
            mixed_low[here, cols] = (numerator * inv).astype(bf16)

    for i, rows in causal_blocks(tokens, 256):
        here = slice(i, i + rows)
        summed = x_all[here, :].astype(f32) + mm(mixed_low[here, :], attn_low[3])
        branch[here, :] = summed
        unit, _ = norm_parts(summed)
        first_low[here, :] = (unit * vec[0:1, :] + vec[1:2, :]).astype(bf16)
    own_sum[...] = branch[place(0), :]
    unit, _ = norm_parts(own_sum[...])
    own_first[...] = unit * vec[0:1, :] + vec[1:2, :]

    hidden_count = up_low.shape[1]
    for c in range(0, hidden_count, piece):
        cols = slice(c, c + piece)
        pre = mm(first_low[...], up_low[:, cols])
        cdf = 0.5 * (1.0 + lax.erf(pre * math.sqrt(0.5)))
        hidden_low[:, cols] = (pre * cdf).astype(bf16)
        slope[:, cols] = cdf + pre * (jnp.exp(-0.5 * pre * pre) * (1.0 / math.sqrt(2.0 * math.pi)))

    branch[...] = mm(hidden_low[...], down_low[...])
    for k, part in enumerate((part0, part1, part2, part3)):
        part[...] = branch[place(k), :].astype(part.dtype)


def forward(blocks, attn_low, up_low, down_low, mask, vec):
    local, width = blocks[0].shape
    tokens = mask.shape[0]
    hidden = up_low.shape[1]
    return pl.pallas_call(
        functools.partial(forward_kernel, local),
        out_shape=[sds((tokens, width), bf16)] * 7
        + [sds((tokens, width), f32), sds((local, width), f32), sds((local, width), f32)]
        + [sds((tokens, width), bf16), sds((tokens, hidden), f32), sds((tokens, hidden), bf16)]
        + [sds((local, width), f32)]
        + [sds((local, width), bf16)] * 3,
        scratch_shapes=[pltpu.VMEM((tokens, width), f32)],
        compiler_params=params(16),
        cost_estimate=pl.CostEstimate(flops=8_000_000_000, bytes_accessed=20_000_000, transcendentals=2_000_000),
        name="forward",
    )(*blocks, attn_low, up_low, down_low, mask, vec)


def middle_kernel(part0, part1, part2, part3, own_first, cotangent, vec, block_out, d_second, d_branch, sums):
    branch = part0[...] + part1[...].astype(f32) + part2[...].astype(f32) + part3[...].astype(f32)
    unit, spread = norm_parts(own_first[...] + branch)
    gain = vec[2:3, :]
    block_out[...] = unit * gain + vec[3:4, :]
    grad = cotangent[...].astype(f32)
    inner = norm_back(grad, unit, spread, gain)
    d_second[...] = inner
    d_branch[...] = inner.astype(bf16)
    sums[...] = jnp.zeros_like(sums)
    sums[2:3, :] = jnp.sum(grad * unit, axis=0, keepdims=True)
    sums[3:4, :] = jnp.sum(grad, axis=0, keepdims=True)


def middle(parts, own_first, cotangent, vec):
    local, width = own_first.shape
    return pl.pallas_call(
        middle_kernel,
        out_shape=[sds((local, width), f32), sds((local, width), f32), sds((local, width), bf16), sds((8, width), f32)],
        compiler_params=params(16),
        name="middle",
    )(*parts, own_first, cotangent, vec)


def feed_back_kernel(
    local, d0, d1, d2, d3, slope, up_low, down_low, d_branch, d_pre, part0, part1, part2, part3, total
):
    rank = lax.axis_index("mp")
    tokens, width = d_branch.shape
    ranks = tokens // local

    def place(k):
        return pl.ds(pl.multiple_of(lax.rem(rank + k, ranks) * local, local), local)

    for k, block in enumerate((d0, d1, d2, d3)):
        d_branch[place(ranks - k), :] = block[...]
    piece = 256
    for c in range(0, d_pre.shape[1], piece):
        cols = slice(c, c + piece)
        d_pre[:, cols] = (mm(d_branch[...], down_low[cols, :], NT) * slope[:, cols]).astype(bf16)
    total[...] = mm(d_pre[...], up_low[...], NT)
    for k, part in enumerate((part0, part1, part2, part3)):
        part[...] = total[place(k), :].astype(part.dtype)


def feed_back(blocks, slope, up_low, down_low):
    local, width = blocks[0].shape
    tokens, hidden = slope.shape
    return pl.pallas_call(
        functools.partial(feed_back_kernel, local),
        out_shape=[sds((tokens, width), bf16), sds((tokens, hidden), bf16), sds((local, width), f32)]
        + [sds((local, width), bf16)] * 3,
        scratch_shapes=[pltpu.VMEM((tokens, width), f32)],
        compiler_params=params(16),
        cost_estimate=pl.CostEstimate(flops=1_200_000_000, bytes_accessed=9_000_000, transcendentals=0),
        name="feed_back",
    )(*blocks, slope, up_low, down_low)


def feed_grads_kernel(index, first_low, d_pre, hidden_low, d_branch, keep, send, up_grad, down_grad):
    up_grad[...] = mm(first_low[...], d_pre[...], TN)
    down_grad[...] = mm(hidden_low[...], d_branch[...], TN)
    write_pieces(index[0], up_grad, down_grad, keep, send, up_grad.shape[0] // STAGED)


def feed_grads(index, first_low, d_pre, hidden_low, d_branch):
    width, hidden = first_low.shape[1], d_pre.shape[1]
    half = (width + hidden) // 2
    return pl.pallas_call(
        feed_grads_kernel,
        in_specs=[pl.BlockSpec(memory_space=pltpu.SMEM)] + [pl.BlockSpec(memory_space=pltpu.VMEM)] * 4,
        out_shape=[sds((half, width), f32), sds((half, width), bf16)],
        scratch_shapes=[pltpu.VMEM((width, hidden), f32), pltpu.VMEM((hidden, width), f32)],
        compiler_params=params(16),
        cost_estimate=pl.CostEstimate(flops=1_200_000_000, bytes_accessed=9_000_000, transcendentals=0),
        name="feed_grads",
    )(index, first_low, d_pre, hidden_low, d_branch)


def first_back_kernel(part0, part1, part2, part3, d_second, own_sum, sums_in, vec, d_resid, d_attn, sums):
    grad = d_second[...] + part0[...] + part1[...].astype(f32) + part2[...].astype(f32) + part3[...].astype(f32)
    unit, spread = norm_parts(own_sum[...])
    inner = norm_back(grad, unit, spread, vec[0:1, :])
    d_resid[...] = inner
    d_attn[...] = inner.astype(bf16)
    sums[...] = sums_in[...]
    sums[0:1, :] = jnp.sum(grad * unit, axis=0, keepdims=True)
    sums[1:2, :] = jnp.sum(grad, axis=0, keepdims=True)


def first_back(parts, d_second, own_sum, sums, vec):
    local, width = own_sum.shape
    return pl.pallas_call(
        first_back_kernel,
        out_shape=[sds((local, width), f32), sds((local, width), bf16), sds((8, width), f32)],
        compiler_params=params(16),
        name="first_back",
    )(*parts, d_second, own_sum, sums, vec)


def mix_back_kernel(
    local,
    index,
    a0,
    a1,
    a2,
    a3,
    attn_low,
    query_feat,
    key_feat,
    value_low,
    query_slope,
    key_slope,
    mixed_low,
    inverse,
    mask,
    mask_t,
    d_resid,
    x_slice,
    mixed_slice,
    sums,
    tokens_grad,
    vec,
    keep,
    send,
    attn_grad,
    d_attn,
    d_query,
    d_key,
    d_value,
):
    rank = lax.axis_index("mp")
    tokens, width = d_attn.shape
    ranks = tokens // local
    own_width = x_slice.shape[0]

    def place(k):
        return pl.ds(pl.multiple_of(lax.rem(rank + k, ranks) * local, local), local)

    for k, block in enumerate((a0, a1, a2, a3)):
        d_attn[place(ranks - k), :] = block[...]

    pair = 2 * (width // HEADS)
    first_half = half_lanes(pair)
    spans = causal_blocks(tokens, 256)
    for c in range(0, width, pair):
        cols = slice(c, c + pair)
        d_mixed = mm(d_attn[...], attn_low[3, cols, :], NT) * inverse[:, cols]
        d_num = d_mixed.astype(bf16)
        d_den = (d_mixed * mixed_low[:, cols].astype(f32)).astype(bf16)
        queries = query_feat[:, cols]
        keys = key_feat[:, cols]
        values = value_low[:, cols]
        left = jnp.concatenate([d_num, d_den], axis=1)
        zero = jnp.zeros_like(keys)
        minus = jnp.full_like(values, -1)
        grad_query = [jnp.zeros((rows, pair), f32) for _, rows in spans]
        grad_key = [jnp.zeros((rows, pair), f32) for _, rows in spans]
        grad_value = [jnp.zeros((rows, pair), f32) for _, rows in spans]
        for own in (first_half, ~first_half):
            own_query = jnp.where(own, queries, zero)
            own_key = jnp.where(own, keys, zero)
            own_num = jnp.where(own, d_num, zero)
            right = jnp.concatenate([jnp.where(own, values, zero), jnp.where(own, minus, zero)], axis=1)
            for n, (i, rows) in enumerate(spans):
                here = slice(i, i + rows)
                upto = i + rows
                d_scores = mm(left[here], right[:upto], NT)
                d_scores = (d_scores * mask[here, :upto]).astype(bf16)
                grad_query[n] += mm(d_scores, own_key[:upto])
                scores_t = mm(own_key[here], queries[i:], NT)
                scores_t = (scores_t * mask_t[here, i:]).astype(bf16)
                grad_value[n] += mm(scores_t, own_num[i:])
                d_scores_t = mm(right[here], left[i:], NT)
                d_scores_t = (d_scores_t * mask_t[here, i:]).astype(bf16)
                grad_key[n] += mm(d_scores_t, own_query[i:])
        for n, (i, rows) in enumerate(spans):
            here = slice(i, i + rows)
            d_query[here, cols] = (grad_query[n] * query_slope[here, cols].astype(f32)).astype(bf16)
            d_key[here, cols] = (grad_key[n] * key_slope[here, cols].astype(f32)).astype(bf16)
            d_value[here, cols] = grad_value[n].astype(bf16)

    mine = place(0)
    tokens_grad[...] = (
        d_resid[...]
        + mm(d_query[mine, :], attn_low[0], NT)
        + mm(d_key[mine, :], attn_low[1], NT)
        + mm(d_value[mine, :], attn_low[2], NT)
    )
    for k, grad in enumerate((d_query, d_key, d_value)):
        attn_grad[k * own_width : (k + 1) * own_width, :] = mm(x_slice[...], grad[...])
    attn_grad[3 * own_width : 4 * own_width, :] = mm(mixed_slice[...], d_attn[...])
    rows = 2 * own_width // STAGED
    write_pieces(
        index[0], attn_grad.at[0 : 2 * own_width], attn_grad.at[2 * own_width : 4 * own_width], keep, send, rows
    )
    high, low = two_parts(sums[0:4, :])
    both = jnp.concatenate([high.astype(f32), low.astype(f32)], axis=0)
    send[8 * rows :, :] = jnp.concatenate([both, jnp.zeros_like(both)], axis=0).astype(bf16)
    vec[0:4, :] = both[0:4] + both[4:8]
    vec[4:8, :] = jnp.zeros_like(both[0:4])


def mix_back(
    index, blocks, attn_low, feats, mixed_low, inverse, mask, mask_t, d_resid, x_slice, mixed_slice, sums
):
    local, width = blocks[0].shape
    tokens = mask.shape[0]
    own_width = x_slice.shape[0]
    return pl.pallas_call(
        functools.partial(mix_back_kernel, local),
        in_specs=[pl.BlockSpec(memory_space=pltpu.SMEM)] + [pl.BlockSpec(memory_space=pltpu.VMEM)] * 18,
        out_shape=[
            sds((local, width), f32),
            sds((8, width), f32),
            sds((2 * own_width, width), f32),
            sds((2 * own_width + VEC_ROWS, width), bf16),
        ],
        scratch_shapes=[pltpu.VMEM((4 * own_width, width), f32)] + [pltpu.VMEM((tokens, width), bf16)] * 4,
        compiler_params=params(16),
        cost_estimate=pl.CostEstimate(flops=10_000_000_000, bytes_accessed=18_000_000, transcendentals=0),
        name="mix_back",
    )(index, *blocks, attn_low, *feats, mixed_low, inverse, mask, mask_t, d_resid, x_slice, mixed_slice, sums)


def as_row(column):
    return jnp.transpose(jnp.broadcast_to(column, (column.shape[0], 128)))[0:1, :]


def as_column(row):
    return jnp.transpose(jnp.broadcast_to(row, (128, row.shape[1])))[:, 0:1]


def attn_stats_kernel(index, even, odd, vec, rows_old, grad_out, rows_new, shares, total):
    own_width, width = grad_out.shape[1:]
    half = 2 * own_width
    read_pieces(index[0], even, odd, total.at[0:half], total.at[half : 2 * half], half // STAGED)
    for k in range(4):
        grad = total[k * own_width : (k + 1) * own_width, :]
        grad_out[k] = grad
        square = grad * grad
        rows = decay * as_column(rows_old[k : k + 1, :]) + (1.0 - decay) * jnp.mean(
            square + tiny_square, axis=1, keepdims=True
        )
        rows_new[k : k + 1, :] = as_row(rows)
        shares[k : k + 1, :] = jnp.sum(square + tiny_square, axis=0, keepdims=True)
        shares[4 + k : 5 + k, :] = jnp.sum(square / rows, axis=0, keepdims=True)
        shares[8 + k : 9 + k, :] = jnp.broadcast_to(jnp.sum(rows, axis=0, keepdims=True), (1, width))
    shares[12:16, :] = vec[0:4, :]


def attn_stats_call(index, even, odd, vec, rows_old):
    own_width = rows_old.shape[1]
    width = even.shape[1]
    return pl.pallas_call(
        attn_stats_kernel,
        in_specs=[pl.BlockSpec(memory_space=pltpu.SMEM)] + [pl.BlockSpec(memory_space=pltpu.VMEM)] * 4,
        out_shape=[sds((4, own_width, width), f32), sds((4, own_width), f32), sds((16, width), f32)],
        scratch_shapes=[pltpu.VMEM((4 * own_width, width), f32)],
        compiler_params=params(16),
        name="attn_stats",
    )(index, even, odd, vec, rows_old)


def feed_stats_kernel(index, even, odd, wide_old, squares, up_grad, down_grad, wide_new, shares):
    width, hidden = up_grad.shape
    read_pieces(index[0], even, odd, up_grad, down_grad, width // STAGED)
    grad = up_grad[...]
    square = grad * grad
    columns = decay * wide_old[0:1, :] + (1.0 - decay) * jnp.mean(square + tiny_square, axis=0, keepdims=True)
    wide_new[0:1, :] = columns
    shares[0:1, :] = as_row(jnp.sum(square + tiny_square, axis=1, keepdims=True))
    shares[1:2, :] = as_row(jnp.sum(square / columns, axis=1, keepdims=True))
    grad = down_grad[...]
    square = grad * grad
    rows = decay * as_column(wide_old[1:2, :]) + (1.0 - decay) * jnp.mean(
        square + tiny_square, axis=1, keepdims=True
    )
    wide_new[1:2, :] = as_row(rows)
    shares[2:3, :] = jnp.sum(square + tiny_square, axis=0, keepdims=True)
    shares[3:4, :] = jnp.sum(square / rows, axis=0, keepdims=True)
    shares[4:5, :] = jnp.broadcast_to(jnp.sum(rows, axis=0, keepdims=True), (1, width))
    for k in range(2):
        shares[5 + k : 6 + k, :] = jnp.broadcast_to(
            jnp.sum(squares[4 + k : 5 + k, :], axis=1, keepdims=True), (1, width)
        )
    shares[7:8, :] = jnp.zeros((1, width), f32)


def feed_stats(index, even, odd, wide_old, squares):
    width, hidden = even.shape[1], wide_old.shape[1]
    return pl.pallas_call(
        feed_stats_kernel,
        in_specs=[pl.BlockSpec(memory_space=pltpu.SMEM)] + [pl.BlockSpec(memory_space=pltpu.VMEM)] * 4,
        out_shape=[sds((width, hidden), f32), sds((hidden, width), f32), sds((2, hidden), f32), sds((8, width), f32)],
        compiler_params=params(16),
        name="feed_stats",
    )(index, even, odd, wide_old, squares)


def add_shares(shares, slots):
    rank = lax.axis_index("mp")
    ranks = len(shares)
    rows = shares[0].shape[0]
    for k, share in enumerate(shares):
        slots[pl.ds(pl.multiple_of(lax.rem(rank + ranks - k, ranks) * rows, rows), rows), :] = share[...]
    total = slots[0:rows, :]
    for k in range(1, ranks):
        total += slots[k * rows : (k + 1) * rows, :]
    return total


def attn_update_kernel(
    rank,
    grad,
    weight,
    rows_new,
    cols_old,
    squares,
    share0,
    share1,
    share2,
    share3,
    vec,
    vec_moment,
    new,
    new_low,
    cols_new,
    vec_grad,
    vec_moment_new,
    vec_new,
    factors,
    columns,
    slots,
):
    step = pl.program_id(0)
    width = grad.shape[2]
    entries = float(width * width)

    @pl.when(step == 0)
    def _():
        total = add_shares((share0, share1, share2, share3), slots)
        cols = decay * cols_old[...] + (1.0 - decay) * total[0:4, :] / width
        cols_new[...] = cols
        mean_rows = total[8:12, :] / width
        scaled = jnp.sum(total[4:8, :] / cols, axis=1, keepdims=True) * mean_rows
        clip = jnp.maximum(1.0, jnp.sqrt(scaled / entries) / clip_limit)
        spread = jnp.sqrt(jnp.sum(squares[0:4, :], axis=1, keepdims=True) / entries)
        factors[0:4, :] = learn_rate * spread / clip
        factors[4:8, :] = mean_rows
        for k in range(4):
            columns[:, k : k + 1] = as_column(rows_new[k : k + 1, :])
        grads = total[12:16, :]
        vec_grad[...] = grads
        moment = decay * vec_moment[...] + (1.0 - decay) * (grads * grads + tiny_square)
        vec_moment_new[...] = moment
        scaled = grads * lax.rsqrt(moment)
        clip = jnp.maximum(1.0, jnp.sqrt(jnp.mean(scaled * scaled, axis=1, keepdims=True)) / clip_limit)
        held = vec[...]
        spread = jnp.sqrt(jnp.mean(held * held, axis=1, keepdims=True))
        vec_new[...] = held - learn_rate * spread * scaled / clip

    for k in range(4):

        @pl.when(step == k)
        def _():
            scale = columns[:, k : k + 1] * cols_new[k : k + 1, :] / factors[4 + k : 5 + k, :]
            value = weight[0] - factors[k : k + 1, :] * (grad[0] * lax.rsqrt(scale))
            new[0] = value
            new_low[0] = value.astype(bf16)


def attn_update(rank, grad, weight, rows_new, cols_old, squares, shares, vec, vec_moment):
    _, own_width, width = grad.shape

    def whole(shape):
        return pl.BlockSpec(shape, lambda i, r: (0,) * len(shape))

    spec = pl.BlockSpec((1, own_width, width), lambda i, r: (i, 0, 0))
    return pl.pallas_call(
        attn_update_kernel,
        grid_spec=pltpu.PrefetchScalarGridSpec(
            num_scalar_prefetch=1,
            grid=(4,),
            in_specs=[
                spec,
                pl.BlockSpec((1, own_width, width), lambda i, r: (i, r[0], 0)),
                whole((4, own_width)),
                whole((4, width)),
                whole((8, width)),
            ]
            + [whole((16, width))] * 4
            + [whole((4, width)), whole((4, width))],
            out_specs=[spec, spec, whole((4, width)), whole((4, width)), whole((4, width)), whole((4, width))],
            scratch_shapes=[
                pltpu.VMEM((8, width), f32),
                pltpu.VMEM((own_width, 8), f32),
                pltpu.VMEM((16 * len(shares), width), f32),
            ],
        ),
        out_shape=[sds((4, own_width, width), f32), sds((4, own_width, width), bf16)] + [sds((4, width), f32)] * 4,
        compiler_params=params(16),
        name="attn_update",
    )(rank, grad, in_hbm(weight), rows_new, cols_old, squares, *shares, vec, vec_moment)


def feed_update_kernel(
    hidden_all,
    up_grad,
    down_grad,
    up_weight,
    down_weight,
    wide_new,
    narrow_old,
    share0,
    share1,
    share2,
    share3,
    up_new,
    up_new_low,
    down_new,
    down_new_low,
    narrow_new,
    factors,
    columns,
    slots,
):
    step = pl.program_id(0)
    width = narrow_old.shape[1]
    block = up_grad.shape[0]
    entries = float(width * hidden_all)

    @pl.when(step == 0)
    def _():
        total = add_shares((share0, share1, share2, share3), slots)
        rows = decay * narrow_old[0:1, :] + (1.0 - decay) * total[0:1, :] / hidden_all
        narrow_new[0:1, :] = rows
        mean_up = jnp.mean(rows, axis=1, keepdims=True)
        scaled = jnp.sum(total[1:2, :] / rows, axis=1, keepdims=True) * mean_up
        clip = jnp.maximum(1.0, jnp.sqrt(scaled / entries) / clip_limit)
        factors[0:1, :] = learn_rate * jnp.sqrt(total[5:6, :] / entries) / clip
        factors[1:2, :] = jnp.broadcast_to(mean_up, (1, width))
        cols = decay * narrow_old[1:2, :] + (1.0 - decay) * total[2:3, :] / hidden_all
        narrow_new[1:2, :] = cols
        mean_down = total[4:5, :] / hidden_all
        scaled = jnp.sum(total[3:4, :] / cols, axis=1, keepdims=True) * mean_down
        clip = jnp.maximum(1.0, jnp.sqrt(scaled / entries) / clip_limit)
        factors[2:3, :] = learn_rate * jnp.sqrt(total[6:7, :] / entries) / clip
        factors[3:4, :] = mean_down
        columns[:, 0:1] = as_column(rows)
        columns[:, 1:2] = as_column(wide_new[1:2, :])

    here = pl.ds(pl.multiple_of(step * block, block), block)
    scale = columns[here, 0:1] * wide_new[0:1, :] / factors[1:2, 0:1]
    value = up_weight[...] - factors[0:1, 0:1] * (up_grad[...] * lax.rsqrt(scale))
    up_new[...] = value
    up_new_low[...] = value.astype(bf16)
    scale = columns[here, 1:2] * narrow_new[1:2, :] / factors[3:4, 0:1]
    value = down_weight[...] - factors[2:3, 0:1] * (down_grad[...] * lax.rsqrt(scale))
    down_new[...] = value
    down_new_low[...] = value.astype(bf16)


def feed_update(up_grad, down_grad, up_weight, down_weight, wide_new, narrow_old, shares, hidden_all):
    steps = 4
    width, hidden = up_grad.shape

    def whole(shape):
        return pl.BlockSpec(shape, lambda i: (0,) * len(shape))

    up_spec = pl.BlockSpec((width // steps, hidden), lambda i: (i, 0))
    down_spec = pl.BlockSpec((hidden // steps, width), lambda i: (i, 0))
    return pl.pallas_call(
        functools.partial(feed_update_kernel, hidden_all),
        grid=(steps,),
        in_specs=[up_spec, down_spec, up_spec, down_spec, whole((2, hidden)), whole((2, width))]
        + [whole((8, width))] * 4,
        out_specs=[up_spec, up_spec, down_spec, down_spec, whole((2, width))],
        scratch_shapes=[
            pltpu.VMEM((8, width), f32),
            pltpu.VMEM((width, 8), f32),
            pltpu.VMEM((8 * len(shares), width), f32),
        ],
        out_shape=[
            sds((width, hidden), f32),
            sds((width, hidden), bf16),
            sds((hidden, width), f32),
            sds((hidden, width), bf16),
            sds((2, width), f32),
        ],
        compiler_params=params(16),
        name="feed_update",
    )(up_grad, down_grad, in_hbm(up_weight), in_hbm(down_weight), wide_new, narrow_old, *shares)


def to_next(block, shift, ranks):
    return lax.ppermute(block, "mp", [(i, (i + shift) % ranks) for i in range(ranks)])


def spread_out(block, ranks):
    return [block] + [to_next(block, k, ranks) for k in range(1, ranks)]


def exchange(parts, ranks):
    return [parts[0]] + [to_next(parts[k], k, ranks) for k in range(1, ranks)]


def on_device(
    tokens,
    cotangent,
    seq_starts,
    attn_weight,
    up_weight,
    down_weight,
    vec_params,
    attn_stats,
    ffn_narrow_stats,
    ffn_wide_stats,
    vec_moment,
):
    ranks = lax.axis_size("mp")
    rank = lax.axis_index("mp")
    local, width = tokens.shape
    own_width = width // ranks
    hidden_all = up_weight.shape[1] * ranks

    blocks = spread_out(tokens, ranks)
    attn_low, up_low, down_low, mask, mask_t, squares = prepare(
        seq_starts, attn_weight, up_weight, down_weight, local * ranks
    )
    (
        x_all,
        query_feat,
        key_feat,
        value_low,
        query_slope,
        key_slope,
        mixed_low,
        inverse,
        own_sum,
        own_first,
        first_low,
        slope,
        hidden_low,
        *parts,
    ) = forward(blocks, attn_low, up_low, down_low, mask, vec_params)
    parts = exchange(parts, ranks)
    block_out, d_second, d_branch, sums = middle(parts, own_first, cotangent, vec_params)
    d_branch, d_pre, *parts = feed_back(spread_out(d_branch, ranks), slope, up_low, down_low)
    staged = lax.axis_size("dp") == STAGED
    index = (lax.axis_index("dp") if staged else jnp.int32(0)).reshape(1)
    feed_rows = up_weight.shape[0] // STAGED
    attn_rows = 2 * own_width // STAGED

    parts = exchange(parts, ranks)
    feed_keep, feed_send = feed_grads(index, first_low, d_pre, hidden_low, d_branch)
    if staged:
        received = across(feed_send, 1)
        feed_keep_a, send_a, feed_keep_b, send_b = fold_first(feed_rows, feed_keep, received)
        parts, send_a, send_b = lax.optimization_barrier((parts, send_a, send_b))
        feed_got_a, feed_got_b = across(send_a, 2), across(send_b, 4)
    d_resid, d_attn, sums = first_back(parts, d_second, own_sum, sums, vec_params)
    blocks = spread_out(d_attn, ranks)
    if staged:
        feed_keep_a, send_a, feed_keep_b, send_b = fold_second(
            feed_rows, feed_keep_a, feed_got_a, feed_keep_b, feed_got_b
        )
        feed_got_a, feed_got_b = across(send_a, 4), across(send_b, 2)
        feed_a, feed_b = fold_third(feed_rows, feed_keep_a, feed_got_a, feed_keep_b, feed_got_b)
        blocks, feed_a, feed_b = lax.optimization_barrier((blocks, feed_a, feed_b))
        feed_a4, feed_b2 = across(feed_a, 4), across(feed_b, 2)
    x_slice = lax.dynamic_slice_in_dim(x_all, rank * own_width, own_width, 1).T
    mixed_slice = lax.dynamic_slice_in_dim(mixed_low, rank * own_width, own_width, 1).T
    tokens_grad, vec_part, attn_keep, attn_send = mix_back(
        index,
        blocks,
        attn_low,
        (query_feat, key_feat, value_low, query_slope, key_slope),
        mixed_low,
        inverse,
        mask,
        mask_t,
        d_resid,
        x_slice,
        mixed_slice,
        sums,
    )
    if staged:
        received = across(attn_send, 1)
        feed_a04 = jnp.concatenate([feed_a, feed_a4])
        feed_b02 = jnp.concatenate([feed_b, feed_b2])
        feed_a26, feed_b46 = across(feed_a04, 2), across(feed_b02, 4)
        vec_part, attn_keep_a, send_a, attn_keep_b, send_b = fold_first(attn_rows, attn_keep, received, vec_part)
        got_a, got_b = across(send_a, 2), across(send_b, 4)
        feed_even = jnp.concatenate([feed_a04, feed_a26, feed_b02, feed_b46])
        feed_odd = across(feed_even, 1)
        vec_part, attn_keep_a, send_a, attn_keep_b, send_b = fold_second(
            attn_rows, attn_keep_a, got_a, attn_keep_b, got_b, vec_part
        )
        got_a, got_b = across(send_a, 4), across(send_b, 2)
        vec_part, attn_a, attn_b = fold_third(attn_rows, attn_keep_a, got_a, attn_keep_b, got_b, vec_part)
        attn_a = jnp.concatenate([attn_a, across(attn_a, 4)])
        attn_b = jnp.concatenate([attn_b, across(attn_b, 2)])
        attn_even = jnp.concatenate([attn_a, across(attn_a, 2), attn_b, across(attn_b, 4)])
        attn_odd = across(attn_even, 1)
    else:
        feed_even, feed_odd, attn_even, attn_odd, vec_part = lax.psum(
            (feed_keep, feed_send.astype(f32), attn_keep, attn_send[: 8 * attn_rows].astype(f32), vec_part), "dp"
        )
    up_grad, down_grad, wide_new, feed_shares = feed_stats(index, feed_even, feed_odd, ffn_wide_stats, squares)
    feed_shares = spread_out(feed_shares, ranks)
    rows_old = lax.dynamic_slice_in_dim(attn_stats[:, 0], rank * own_width, own_width, 1)
    attn_grad, attn_rows_new, attn_shares = attn_stats_call(index, attn_even, attn_odd, vec_part, rows_old)
    attn_shares = spread_out(attn_shares, ranks)
    up_new, up_new_low, down_new, down_new_low, narrow_new = feed_update(
        up_grad, down_grad, up_weight, down_weight, wide_new, ffn_narrow_stats, feed_shares, hidden_all
    )
    attn_new, attn_new_low, attn_cols, vec_grad, vec_moment_new, vec_new = attn_update(
        rank.reshape(1), attn_grad, attn_weight, attn_rows_new, attn_stats[:, 1], squares, attn_shares, vec_params,
        vec_moment,
    )
    return (
        block_out,
        tokens_grad,
        attn_grad,
        attn_rows_new,
        attn_cols,
        attn_new,
        attn_new_low,
        up_grad,
        down_grad,
        narrow_new,
        wide_new,
        up_new,
        down_new,
        up_new_low,
        down_new_low,
        vec_grad,
        vec_moment_new,
        vec_new,
    )


def solution(mesh):
    in_specs = (
        P(("dp", "mp"), None),
        P(("dp", "mp"), None),
        P("dp", None),
        P(),
        P(None, "mp"),
        P("mp", None),
        P(),
        P(),
        P(),
        P(None, "mp"),
        P(),
    )
    out_specs = (
        P(("dp", "mp"), None),
        P(("dp", "mp"), None),
        P(None, "mp", None),
        P(None, "mp"),
        P(),
        P(None, "mp", None),
        P(None, "mp", None),
        P(None, "mp"),
        P("mp", None),
        P(),
        P(None, "mp"),
        P(None, "mp"),
        P("mp", None),
        P(None, "mp"),
        P("mp", None),
        P(),
        P(),
        P(),
    )
    return jax.shard_map(
        on_device, mesh=mesh, in_specs=in_specs, out_specs=out_specs, check_vma=False
    )
```

```python
import functools
import math

import jax
import jax.numpy as jnp
from jax import lax
from jax.experimental import pallas as pl
from jax.experimental.pallas import tpu as pltpu
from jax.sharding import PartitionSpec as P

HEADS = 12
STEP = 10

norm_eps = 1e-05
tiny_square = 1e-30
learn_rate = 0.3
clip_limit = 1.0
decay = 1.0 - float(STEP) ** (-0.8)

f32 = jnp.float32
bf16 = jnp.bfloat16

NN = (((1,), (0,)), ((), ()))
NT = (((1,), (1,)), ((), ()))
TN = (((0,), (0,)), ((), ()))


def mm(a, b, dims=NN):
    return lax.dot_general(a, b, dims, preferred_element_type=f32)


def params(mib):
    return pltpu.CompilerParams(vmem_limit_bytes=mib * 1024 * 1024)


def sds(shape, dtype):
    return jax.ShapeDtypeStruct(shape, dtype)


def in_hbm(array):
    return pltpu.with_memory_space_constraint(array, pltpu.HBM)


def in_vmem(array):
    return pltpu.with_memory_space_constraint(array, pltpu.VMEM)


def all_vmem(arrays):
    return [in_vmem(array) for array in arrays]


def near(shape, dtype):
    return pltpu.VMEM(shape, dtype)


NO_COST = pl.CostEstimate(flops=0, bytes_accessed=0, transcendentals=0)


def holding(kernel, count, held):
    def body(*refs):
        for ref in refs[count : count + held]:
            pltpu.touch(ref)
        kernel(*refs[:count], *refs[count + held :])

    return body


STAGED = 8
VEC_ROWS = 16
SHIFTS = (0, 2, 1, 3)
SUM_SHIFTS = (0, 1, 2, 3)


def half_rows(count, mine):
    rows = count // 2
    side = lax.rem(lax.axis_index("dp"), 2) if lax.axis_size("dp") == STAGED else 0
    return pl.ds(pl.multiple_of((side if mine else 1 - side) * rows, rows), rows)


def write_halves(total, keep, send):
    rows = total.shape[0] // 2
    keep[...] = total[half_rows(total.shape[0], True), :]
    send[0:rows, :] = total[half_rows(total.shape[0], False), :].astype(send.dtype)


def read_halves(mine, other, total):
    total[half_rows(total.shape[0], True), :] = mine[...].astype(total.dtype)
    total[half_rows(total.shape[0], False), :] = other[...].astype(total.dtype)


def two_parts(values):
    high = values.astype(bf16).astype(f32)
    low = (values - high).astype(bf16).astype(f32)
    both = jnp.concatenate([high, low], axis=0)
    return high + low, jnp.concatenate([both, jnp.zeros_like(both)], axis=0).astype(bf16)


def joined(block):
    return block[0:4, :].astype(f32) + block[4:8, :].astype(f32)


def add_vec(vec, block, vec_out, send=None):
    held, packed = two_parts(vec[0:4, :] + joined(block))
    vec_out[0:4, :] = held
    vec_out[4:8, :] = jnp.zeros_like(held)
    if send is not None:
        send[...] = packed


def fold_first_kernel(keep, received, *refs):
    send_a, send_b = refs[-2:]
    rows = keep.shape[0] // 2
    send_a[0:rows, :] = (keep[0:rows, :] + received[0:rows, :].astype(f32)).astype(bf16)
    send_b[...] = (keep[rows : 2 * rows, :] + received[rows : 2 * rows, :].astype(f32)).astype(bf16)
    if len(refs) > 2:
        add_vec(refs[0], received[2 * rows :, :], refs[1], send_a.at[rows:, :])


def fold_second_kernel(own_a, got_a, own_b, got_b, *refs):
    send_a, send_b = refs[-2:]
    rows = own_b.shape[0]
    send_a[0:rows, :] = (own_a[0:rows, :].astype(f32) + got_a[0:rows, :].astype(f32)).astype(bf16)
    send_b[...] = (own_b[...].astype(f32) + got_b[...].astype(f32)).astype(bf16)
    if len(refs) > 2:
        add_vec(refs[0], got_a[rows:, :], refs[1], send_a.at[rows:, :])


def fold_last_kernel(own_a, got_a, own_b, got_b, *refs):
    total = refs[-1]
    rows = own_b.shape[0]
    total[0:rows, :] = (own_a[0:rows, :].astype(f32) + got_a[0:rows, :].astype(f32)).astype(bf16)
    total[rows:, :] = (own_b[...].astype(f32) + got_b[...].astype(f32)).astype(bf16)
    if len(refs) > 1:
        add_vec(refs[0], got_a[rows:, :], refs[1])


def fold_call(kernel, name, inputs, vec, outs):
    width = inputs[0].shape[1]
    extra_in, extra_out = ([in_vmem(vec)], [near((8, width), f32)]) if vec is not None else ([], [])
    return pl.pallas_call(
        kernel,
        out_shape=extra_out + [near((rows, width), bf16) for rows in outs],
        compiler_params=params(8),
        cost_estimate=NO_COST,
        name=name,
    )(in_vmem(inputs[0]), *inputs[1:], *extra_in)


def fold_first(keep, received, vec=None):
    rows = keep.shape[0] // 2
    return fold_call(
        fold_first_kernel, "fold_first", (keep, received), vec, (rows if vec is None else rows + VEC_ROWS, rows)
    )


def fold_second(own_a, got_a, own_b, got_b, vec=None):
    return fold_call(
        fold_second_kernel, "fold_second", (own_a, got_a, own_b, got_b), vec, (own_a.shape[0], own_b.shape[0])
    )


def fold_last(own_a, got_a, own_b, got_b, vec=None):
    return fold_call(fold_last_kernel, "fold_last", (own_a, got_a, own_b, got_b), vec, (2 * own_b.shape[0],))


def fold_feed_kernel(*refs):
    own, got, (send_a, send_b) = refs[0:4], refs[4:8], refs[8:]
    rows = own[0].shape[0]
    for n, (block, other) in enumerate(zip(own, got)):
        send = (send_a, send_b)[n % 2]
        place = n // 2 * rows
        send[place : place + rows, :] = (block[...].astype(f32) + other[...].astype(f32)).astype(bf16)


def fold_feed(own, got):
    rows, width = own[0].shape
    return pl.pallas_call(
        fold_feed_kernel,
        out_shape=[near((2 * rows, width), bf16)] * 2,
        compiler_params=params(8),
        cost_estimate=NO_COST,
        name="fold_feed",
    )(*all_vmem(own), *got)


def fold_feed_last_kernel(own_a, got_a, own_b, got_b, total):
    rows = own_a.shape[0] // 2
    for n, (block, other) in enumerate(((own_a, got_a), (own_b, got_b))):
        for part in range(2):
            here = slice(part * rows, (part + 1) * rows)
            place = (2 * part + n) * rows
            total[place : place + rows, :] = (block[here, :].astype(f32) + other[here, :].astype(f32)).astype(bf16)


def fold_feed_last(own_a, got_a, own_b, got_b):
    rows, width = own_a.shape
    return pl.pallas_call(
        fold_feed_last_kernel,
        out_shape=near((2 * rows, width), bf16),
        compiler_params=params(8),
        cost_estimate=NO_COST,
        name="fold_feed_last",
    )(in_vmem(own_a), got_a, in_vmem(own_b), got_b)


def across(block, bit):
    return lax.ppermute(block, "dp", [(i, i ^ bit) for i in range(STAGED)])


def prepare_kernel(seqs, tokens_pack, starts, attn, up, down, attn_low, up_low, down_low, mask, mask_t, squares):
    step = pl.program_id(0)

    @pl.when(step == 0)
    def _():
        squares[...] = jnp.zeros_like(squares)

    for k in range(4):
        block = attn[k]
        attn_low[k] = block.astype(bf16)
        squares[k : k + 1, :] += jnp.sum(block * block, axis=0, keepdims=True)
    for k, (source, target) in enumerate(((up, up_low), (down, down_low))):
        block = source[...]
        target[...] = block.astype(bf16)
        squares[4 + k : 5 + k, :] += jnp.sum(block * block, axis=0, keepdims=True)

    def layout(index):
        seq = jnp.zeros_like(index)
        begin = jnp.zeros_like(index)
        length = jnp.ones_like(index)
        for s in range(seqs):
            start = starts[0, s]
            finish = starts[0, s + 1] if s + 1 < seqs else tokens_pack
            inside = index >= start
            seq = jnp.where(inside, s, seq)
            begin = jnp.where(inside, start, begin)
            length = jnp.where(inside, finish - start, length)
        angle = 0.5 * math.pi * (index - begin).astype(f32) / length.astype(f32)
        return seq, jnp.cos(angle), jnp.sin(angle)

    rows = mask.shape[0]
    row = lax.broadcasted_iota(jnp.int32, (rows, 128), 0) + step * rows
    col = lax.broadcasted_iota(jnp.int32, (8, tokens_pack), 1)
    row_seq, row_cos, row_sin = (a[:, 0:1] for a in layout(row))
    col_seq, col_cos, col_sin = (a[0:1, :] for a in layout(col))
    same = row_seq == col_seq
    value = row_cos * col_cos + row_sin * col_sin
    row, col = row[:, 0:1], col[0:1, :]
    mask[...] = jnp.where(same & (col <= row), value, 0.0)
    mask_t[...] = jnp.where(same & (row <= col), value, 0.0)


def prepare(seq_starts, attn_weight, up_weight, down_weight, tokens_pack):
    steps = 8
    seqs = seq_starts.shape[1]
    heads4, width, _ = attn_weight.shape
    hidden = up_weight.shape[1]
    a_rows, u_rows, d_rows, m_rows = width // steps, width // steps, hidden // steps, tokens_pack // steps
    return pl.pallas_call(
        functools.partial(prepare_kernel, seqs, tokens_pack),
        grid=(steps,),
        in_specs=[
            pl.BlockSpec(memory_space=pltpu.SMEM),
            pl.BlockSpec((4, a_rows, width), lambda i: (0, i, 0)),
            pl.BlockSpec((u_rows, hidden), lambda i: (i, 0)),
            pl.BlockSpec((d_rows, width), lambda i: (i, 0)),
        ],
        out_specs=[
            pl.BlockSpec((4, a_rows, width), lambda i: (0, i, 0)),
            pl.BlockSpec((u_rows, hidden), lambda i: (i, 0)),
            pl.BlockSpec((d_rows, width), lambda i: (i, 0)),
            pl.BlockSpec((m_rows, tokens_pack), lambda i: (i, 0)),
            pl.BlockSpec((m_rows, tokens_pack), lambda i: (i, 0)),
            pl.BlockSpec((8, width), lambda i: (0, 0)),
        ],
        out_shape=[
            near((4, width, width), bf16),
            near((width, hidden), bf16),
            near((hidden, width), bf16),
            near((tokens_pack, tokens_pack), f32),
            near((tokens_pack, tokens_pack), f32),
            near((8, width), f32),
        ],
        compiler_params=params(24),
        cost_estimate=pl.CostEstimate(flops=10_000_000, bytes_accessed=22_000_000, transcendentals=0),
        name="prepare",
    )(seq_starts, in_hbm(attn_weight), in_hbm(up_weight), in_hbm(down_weight))


def half_lanes(width):
    return lax.broadcasted_iota(jnp.int32, (1, width), 1) < width // 2


def norm_parts(values):
    centered = values - jnp.mean(values, axis=-1, keepdims=True)
    spread = lax.rsqrt(jnp.mean(centered * centered, axis=-1, keepdims=True) + norm_eps)
    return centered * spread, spread


def norm_back(grad, unit, spread, gain):
    scaled = grad * gain
    return spread * (
        scaled
        - jnp.mean(scaled, axis=-1, keepdims=True)
        - unit * jnp.mean(scaled * unit, axis=-1, keepdims=True)
    )


def causal_blocks(tokens, size):
    return [(i, min(size, tokens - i)) for i in range(0, tokens, size)]


def forward_kernel(
    local,
    x0,
    x1,
    x2,
    x3,
    attn_low,
    up_low,
    down_low,
    mask,
    vec,
    x_all,
    query_feat,
    key_feat,
    value_low,
    mixed_low,
    inverse,
    own_sum,
    own_first,
    first_low,
    pre_act,
    hidden_low,
    part0,
    part1,
    part2,
    part3,
    branch,
):
    rank = lax.axis_index("mp")
    tokens, width = x_all.shape
    ranks = tokens // local

    def place(k):
        return pl.ds(pl.multiple_of(lax.rem(rank + k, ranks) * local, local), local)

    for k, block in zip(SHIFTS, (x0, x1, x2, x3)):
        x_all[place(ranks - k), :] = block[...]

    piece = 256
    for c in range(0, width, piece):
        cols = slice(c, c + piece)
        for which, feat in ((0, query_feat), (1, key_feat)):
            raw = mm(x_all[...], attn_low[which, :, cols])
            feat[:, cols] = jax.nn.softplus(raw).astype(bf16)
        value_low[:, cols] = mm(x_all[...], attn_low[2, :, cols]).astype(bf16)

    pair = 2 * (width // HEADS)
    first_half = half_lanes(pair)
    for c in range(0, width, pair):
        cols = slice(c, c + pair)
        keys = key_feat[:, cols]
        values = value_low[:, cols]
        zero = jnp.zeros_like(keys)
        one = jnp.ones_like(values)
        sides = (first_half, ~first_half)
        own_keys = [jnp.where(own, keys, zero) for own in sides]
        own_values = [
            jnp.concatenate([jnp.where(own, values, zero), jnp.where(own, one, zero)], axis=1) for own in sides
        ]
        for i, rows in causal_blocks(tokens, 256):
            here = slice(i, i + rows)
            upto = i + rows
            queries = query_feat[here, cols]
            weights = []
            for side in range(2):
                scores = mm(queries, own_keys[side][:upto], NT)
                weights.append((scores * mask[here, :upto]).astype(bf16))
            both = mm(
                jnp.concatenate(weights, axis=1),
                jnp.concatenate([block[:upto] for block in own_values], axis=0),
            )
            inv = 1.0 / both[:, pair:]
            inverse[here, cols] = inv
            mixed_low[here, cols] = (both[:, :pair] * inv).astype(bf16)

    for i, rows in causal_blocks(tokens, 256):
        here = slice(i, i + rows)
        summed = x_all[here, :].astype(f32) + mm(mixed_low[here, :], attn_low[3])
        branch[here, :] = summed
        unit, _ = norm_parts(summed)
        first_low[here, :] = (unit * vec[0:1, :] + vec[1:2, :]).astype(bf16)
    own_sum[...] = branch[place(0), :]
    unit, _ = norm_parts(own_sum[...])
    own_first[...] = unit * vec[0:1, :] + vec[1:2, :]

    hidden_count = up_low.shape[1]
    for c in range(0, hidden_count, piece):
        cols = slice(c, c + piece)
        pre = mm(first_low[...], up_low[:, cols])
        cdf = 0.5 * (1.0 + lax.erf(pre * math.sqrt(0.5)))
        hidden_low[:, cols] = (pre * cdf).astype(bf16)
        pre_act[:, cols] = pre

    branch[...] = mm(hidden_low[...], down_low[...])
    for k, part in zip(SUM_SHIFTS, (part0, part1, part2, part3)):
        part[...] = branch[place(k), :].astype(part.dtype)


def forward(blocks, attn_low, up_low, down_low, mask, vec):
    local, width = blocks[0].shape
    tokens = mask.shape[0]
    hidden = up_low.shape[1]
    return pl.pallas_call(
        functools.partial(forward_kernel, local),
        out_shape=[near((tokens, width), bf16)] * 5
        + [near((tokens, width), f32), near((local, width), f32), near((local, width), f32)]
        + [near((tokens, width), bf16), near((tokens, hidden), f32), near((tokens, hidden), bf16)]
        + [near((local, width), f32)]
        + [near((local, width), bf16)] * 3,
        scratch_shapes=[pltpu.VMEM((tokens, width), f32)],
        compiler_params=params(16),
        cost_estimate=pl.CostEstimate(flops=8_000_000_000, bytes_accessed=20_000_000, transcendentals=2_000_000),
        name="forward",
    )(*blocks, *all_vmem((attn_low, up_low, down_low, mask)), vec)


def slopes_kernel(query_feat, key_feat, mask_t, pre_act, weights_t, query_slope, key_slope, slope):
    tokens, width = query_feat.shape
    piece = 256
    for c in range(0, width, piece):
        cols = slice(c, c + piece)
        for feat, grad in ((query_feat, query_slope), (key_feat, key_slope)):
            value = feat[:, cols].astype(f32)
            small = value * (1.0 - value * (0.5 - value * (1.0 / 6.0)))
            grad[:, cols] = jnp.where(value < 0.02, small, 1.0 - jnp.exp(-value)).astype(bf16)
    for c in range(0, pre_act.shape[1], piece):
        cols = slice(c, c + piece)
        pre = pre_act[:, cols]
        cdf = 0.5 * (1.0 + lax.erf(pre * math.sqrt(0.5)))
        slope[:, cols] = cdf + pre * (jnp.exp(-0.5 * pre * pre) * (1.0 / math.sqrt(2.0 * math.pi)))
    pair = 2 * (width // HEADS)
    first_half = half_lanes(pair)
    for head in range(HEADS):
        cols = slice(head // 2 * pair, (head // 2 + 1) * pair)
        own = first_half if head % 2 == 0 else ~first_half
        for i, rows in causal_blocks(tokens, 256):
            here = slice(i, i + rows)
            keys = key_feat[here, cols]
            scores = mm(jnp.where(own, keys, jnp.zeros_like(keys)), query_feat[i:, cols], NT)
            weights_t[head * tokens + i : head * tokens + i + rows, i:] = (scores * mask_t[here, i:]).astype(bf16)


def slopes(query_feat, key_feat, mask_t, pre_act):
    tokens, width = query_feat.shape
    return pl.pallas_call(
        slopes_kernel,
        out_shape=[near((HEADS * tokens, tokens), bf16)]
        + [near((tokens, width), bf16)] * 2
        + [near(pre_act.shape, f32)],
        compiler_params=params(16),
        cost_estimate=NO_COST,
        name="slopes",
    )(*all_vmem((query_feat, key_feat, mask_t, pre_act)))


def middle_kernel(part0, part1, part2, part3, own_first, cotangent, vec, block_out, d_second, sums, *d_branch):
    branch = part0[...] + part1[...].astype(f32) + part2[...].astype(f32) + part3[...].astype(f32)
    unit, spread = norm_parts(own_first[...] + branch)
    gain = vec[2:3, :]
    block_out[...] = unit * gain + vec[3:4, :]
    grad = cotangent[...].astype(f32)
    inner = norm_back(grad, unit, spread, gain)
    d_second[...] = inner
    for copy in d_branch:
        copy[...] = inner.astype(bf16)
    sums[...] = jnp.zeros_like(sums)
    sums[2:3, :] = jnp.sum(grad * unit, axis=0, keepdims=True)
    sums[3:4, :] = jnp.sum(grad, axis=0, keepdims=True)


def middle(parts, own_first, cotangent, vec, held):
    local, width = own_first.shape
    return pl.pallas_call(
        holding(middle_kernel, 7, len(held)),
        out_shape=[sds((local, width), f32), near((local, width), f32), near((8, width), f32)]
        + [near((local, width), bf16)] * 4,
        compiler_params=params(8),
        name="middle",
    )(in_vmem(parts[0]), *parts[1:], in_vmem(own_first), cotangent, vec, *all_vmem(held))


def feed_back_kernel(
    local, d0, d1, d2, d3, slope, up_low, down_low, d_branch, d_pre, part0, part1, part2, part3, total
):
    rank = lax.axis_index("mp")
    tokens, width = d_branch.shape
    ranks = tokens // local

    def place(k):
        return pl.ds(pl.multiple_of(lax.rem(rank + k, ranks) * local, local), local)

    for k, block in zip(SHIFTS, (d0, d1, d2, d3)):
        d_branch[place(ranks - k), :] = block[...]
    piece = 256
    for c in range(0, d_pre.shape[1], piece):
        cols = slice(c, c + piece)
        d_pre[:, cols] = (mm(d_branch[...], down_low[cols, :], NT) * slope[:, cols]).astype(bf16)
    total[...] = mm(d_pre[...], up_low[...], NT)
    for k, part in zip(SUM_SHIFTS, (part0, part1, part2, part3)):
        part[...] = total[place(k), :].astype(part.dtype)


def feed_back(blocks, slope, up_low, down_low, held):
    local, width = blocks[0].shape
    tokens, hidden = slope.shape
    return pl.pallas_call(
        holding(functools.partial(feed_back_kernel, local), 7, len(held)),
        out_shape=[near((tokens, width), bf16), near((tokens, hidden), bf16), near((local, width), f32)]
        + [near((local, width), bf16)] * 3,
        scratch_shapes=[pltpu.VMEM((tokens, width), f32)],
        compiler_params=params(16),
        cost_estimate=pl.CostEstimate(flops=1_200_000_000, bytes_accessed=9_000_000, transcendentals=0),
        name="feed_back",
    )(in_vmem(blocks[0]), *blocks[1:], *all_vmem((slope, up_low, down_low, *held)))


def feed_grads_kernel(first_low, d_pre, hidden_low, d_branch, keep_up, keep_down, send_up, send_down):
    for left, right, keep, send in (
        (first_low, d_pre, keep_up, send_up),
        (hidden_low, d_branch, keep_down, send_down),
    ):
        keep[...] = mm(left[:, half_rows(left.shape[1], True)], right[...], TN)
        send[...] = mm(left[:, half_rows(left.shape[1], False)], right[...], TN).astype(bf16)


def feed_grads(first_low, d_pre, hidden_low, d_branch):
    width, hidden = first_low.shape[1], d_pre.shape[1]
    return pl.pallas_call(
        feed_grads_kernel,
        out_shape=[near((width // 2, hidden), f32), near((hidden // 2, width), f32)]
        + [near((width // 2, hidden), bf16), near((hidden // 2, width), bf16)],
        compiler_params=params(16),
        cost_estimate=NO_COST,
        name="feed_grads",
    )(*all_vmem((first_low, d_pre, hidden_low, d_branch)))


def first_back_kernel(part0, part1, part2, part3, d_second, own_sum, sums_in, vec, d_resid, sums, *d_attn):
    grad = d_second[...] + part0[...] + part1[...].astype(f32) + part2[...].astype(f32) + part3[...].astype(f32)
    unit, spread = norm_parts(own_sum[...])
    inner = norm_back(grad, unit, spread, vec[0:1, :])
    d_resid[...] = inner
    for copy in d_attn:
        copy[...] = inner.astype(bf16)
    sums[...] = sums_in[...]
    sums[0:1, :] = jnp.sum(grad * unit, axis=0, keepdims=True)
    sums[1:2, :] = jnp.sum(grad, axis=0, keepdims=True)


def first_back(parts, d_second, own_sum, sums, vec, held):
    local, width = own_sum.shape
    return pl.pallas_call(
        holding(first_back_kernel, 8, len(held)),
        out_shape=[near((local, width), f32), near((8, width), f32)] + [near((local, width), bf16)] * 4,
        compiler_params=params(8),
        name="first_back",
    )(in_vmem(parts[0]), *parts[1:], *all_vmem((d_second, own_sum, sums)), vec, *all_vmem(held))


def own_columns_kernel(x_all, mixed_low, x_slice, mixed_slice, turned):
    rows = x_slice.shape[0]
    mine = pl.ds(pl.multiple_of(lax.axis_index("mp") * rows, rows), rows)
    for source, target in ((x_all, x_slice), (mixed_low, mixed_slice)):
        turned[...] = jnp.transpose(source[...])
        target[...] = turned[mine, :]


def own_columns(x_all, mixed_low, own_width):
    tokens, width = x_all.shape
    return pl.pallas_call(
        own_columns_kernel,
        out_shape=[near((own_width, tokens), bf16)] * 2,
        scratch_shapes=[pltpu.VMEM((width, tokens), bf16)],
        compiler_params=params(8),
        cost_estimate=NO_COST,
        name="own_columns",
    )(*all_vmem((x_all, mixed_low)))


def mix_heads(
    start, d_num, d_den, query_feat, key_feat, value_low, query_slope, key_slope, weights_t, mask, mask_t, d_query, d_key,
    d_value,
):
    tokens, width = query_feat.shape
    pair = 2 * (width // HEADS)
    first_half = half_lanes(pair)
    spans = causal_blocks(tokens, 256)
    for c in range(start, start + width // 2, pair):
        cols = slice(c, c + pair)
        queries = query_feat[:, cols]
        keys = key_feat[:, cols]
        values = value_low[:, cols]
        nums = d_num[:, cols]
        left = jnp.concatenate([nums, d_den[:, cols]], axis=1)
        zero = jnp.zeros_like(keys)
        minus = jnp.full_like(values, -1)
        grad_query = [jnp.zeros((rows, pair), f32) for _, rows in spans]
        grad_key = [jnp.zeros((rows, pair), f32) for _, rows in spans]
        grad_value = [jnp.zeros((rows, pair), f32) for _, rows in spans]
        for half, own in enumerate((first_half, ~first_half)):
            base = (2 * (c // pair) + half) * tokens
            own_query = jnp.where(own, queries, zero)
            own_key = jnp.where(own, keys, zero)
            own_num = jnp.where(own, nums, zero)
            right = jnp.concatenate([jnp.where(own, values, zero), jnp.where(own, minus, zero)], axis=1)
            for n, (i, rows) in enumerate(spans):
                here = slice(i, i + rows)
                upto = i + rows
                d_scores = mm(left[here], right[:upto], NT)
                d_scores = (d_scores * mask[here, :upto]).astype(bf16)
                grad_query[n] += mm(d_scores, own_key[:upto])
                grad_value[n] += mm(weights_t[base + i : base + i + rows, i:], own_num[i:])
                d_scores_t = mm(right[here], left[i:], NT)
                d_scores_t = (d_scores_t * mask_t[here, i:]).astype(bf16)
                grad_key[n] += mm(d_scores_t, own_query[i:])
        out = slice(c - start, c - start + pair)
        for n, (i, rows) in enumerate(spans):
            here = slice(i, i + rows)
            d_query[here, out] = (grad_query[n] * query_slope[here, cols].astype(f32)).astype(bf16)
            d_key[here, out] = (grad_key[n] * key_slope[here, cols].astype(f32)).astype(bf16)
            d_value[here, out] = grad_value[n].astype(bf16)


def mix_first_kernel(
    local,
    a0,
    a1,
    a2,
    a3,
    attn_low,
    mixed_low,
    inverse,
    query_feat,
    key_feat,
    value_low,
    query_slope,
    key_slope,
    weights_t,
    mask,
    mask_t,
    d_attn,
    d_num,
    d_den,
    d_query,
    d_key,
    d_value,
):
    rank = lax.axis_index("mp")
    tokens, width = d_attn.shape
    ranks = tokens // local
    for k, block in zip(SHIFTS, (a0, a1, a2, a3)):
        here = pl.ds(pl.multiple_of(lax.rem(rank + ranks - k, ranks) * local, local), local)
        d_attn[here, :] = block[...]
    piece = 256
    for c in range(0, width, piece):
        cols = slice(c, c + piece)
        d_mixed = mm(d_attn[...], attn_low[3, cols, :], NT) * inverse[:, cols]
        d_num[:, cols] = d_mixed.astype(bf16)
        d_den[:, cols] = (d_mixed * mixed_low[:, cols].astype(f32)).astype(bf16)
    mix_heads(
        0, d_num, d_den, query_feat, key_feat, value_low, query_slope, key_slope, weights_t, mask, mask_t, d_query,
        d_key, d_value,
    )


def mix_first(blocks, attn_low, mixed_low, inverse, feats):
    local, width = blocks[0].shape
    tokens = mixed_low.shape[0]
    return pl.pallas_call(
        functools.partial(mix_first_kernel, local),
        out_shape=[near((tokens, width), bf16)] * 3 + [near((tokens, width // 2), bf16)] * 3,
        compiler_params=params(16),
        cost_estimate=pl.CostEstimate(flops=6_000_000_000, bytes_accessed=18_000_000, transcendentals=0),
        name="mix_first",
    )(in_vmem(blocks[0]), *blocks[1:], *all_vmem((attn_low, mixed_low, inverse, *feats)))


def mix_second_kernel(
    d_attn,
    d_num,
    d_den,
    first_query,
    first_key,
    first_value,
    attn_low,
    query_feat,
    key_feat,
    value_low,
    query_slope,
    key_slope,
    weights_t,
    mask,
    mask_t,
    x_slice,
    mixed_slice,
    sums,
    d_query,
    d_key,
    d_value,
    vec,
    keep,
    send,
    attn_grad,
):
    width = d_attn.shape[1]
    own_width = x_slice.shape[0]
    half = width // 2
    for source, target in ((first_query, d_query), (first_key, d_key), (first_value, d_value)):
        target[:, 0:half] = source[...]
    mix_heads(
        half, d_num, d_den, query_feat, key_feat, value_low, query_slope, key_slope, weights_t, mask, mask_t,
        d_query.at[:, half:width], d_key.at[:, half:width], d_value.at[:, half:width],
    )
    for k, grad in enumerate((d_query, d_key, d_value)):
        attn_grad[k * own_width : (k + 1) * own_width, :] = mm(x_slice[...], grad[...])
    attn_grad[3 * own_width : 4 * own_width, :] = mm(mixed_slice[...], d_attn[...])
    write_halves(attn_grad, keep, send)
    held, packed = two_parts(sums[0:4, :])
    send[2 * own_width :, :] = packed
    vec[0:4, :] = held
    vec[4:8, :] = jnp.zeros_like(held)


def mix_second(first, attn_low, feats, x_slice, mixed_slice, sums):
    tokens, width = first[0].shape
    own_width = x_slice.shape[0]
    return pl.pallas_call(
        mix_second_kernel,
        out_shape=[near((tokens, width), bf16)] * 3
        + [
            near((8, width), f32),
            near((2 * own_width, width), f32),
            near((2 * own_width + VEC_ROWS, width), bf16),
        ],
        scratch_shapes=[pltpu.VMEM((4 * own_width, width), f32)],
        compiler_params=params(16),
        cost_estimate=pl.CostEstimate(flops=6_000_000_000, bytes_accessed=18_000_000, transcendentals=0),
        name="mix_second",
    )(*all_vmem((*first, attn_low, *feats, x_slice, mixed_slice, sums)))


def tokens_back_kernel(
    d_query, d_key, d_value, attn_low, d_resid, attn_weight, up_weight, down_weight, tokens_grad, own_attn, own_up, own_down,
    sems,
):
    local, own_width = d_resid.shape[0], own_attn.shape[1]
    rank = lax.axis_index("mp")
    columns = pl.ds(pl.multiple_of(rank * own_width, own_width), own_width)
    copies = [
        pltpu.make_async_copy(attn_weight.at[:, columns, :], own_attn, sems.at[0]),
        pltpu.make_async_copy(up_weight, own_up, sems.at[1]),
        pltpu.make_async_copy(down_weight, own_down, sems.at[2]),
    ]
    for copy in copies:
        copy.start()
    mine = pl.ds(pl.multiple_of(rank * local, local), local)
    tokens_grad[...] = (
        d_resid[...]
        + mm(d_query[mine, :], attn_low[0], NT)
        + mm(d_key[mine, :], attn_low[1], NT)
        + mm(d_value[mine, :], attn_low[2], NT)
    )
    for copy in copies:
        copy.wait()


def tokens_back(d_query, d_key, d_value, attn_low, d_resid, attn_weight, up_weight, down_weight, own_width):
    return pl.pallas_call(
        tokens_back_kernel,
        in_specs=[pl.BlockSpec(memory_space=pltpu.VMEM)] * 5 + [pl.BlockSpec(memory_space=pl.ANY)] * 3,
        out_shape=[
            sds(d_resid.shape, f32),
            near((4, own_width, d_resid.shape[1]), f32),
            near(up_weight.shape, f32),
            near(down_weight.shape, f32),
        ],
        scratch_shapes=[pltpu.SemaphoreType.DMA((3,))],
        compiler_params=params(16),
        cost_estimate=NO_COST,
        name="tokens_back",
    )(
        *all_vmem((d_query, d_key, d_value, attn_low, d_resid)), in_hbm(attn_weight), in_hbm(up_weight),
        in_hbm(down_weight),
    )


def as_row(column):
    return jnp.transpose(jnp.broadcast_to(column, (column.shape[0], 128)))[0:1, :]


def as_column(row):
    return jnp.transpose(jnp.broadcast_to(row, (128, row.shape[1])))[:, 0:1]


SHARE_ROWS = 24


def lane_scalars(values, width):
    lane = lax.broadcasted_iota(jnp.int32, (1, width), 1)
    row = jnp.zeros((1, width), f32)
    for k, value in enumerate(values):
        row = jnp.where(lane == k, value, row)
    return row


def lane_scalar(row, k):
    lane = lax.broadcasted_iota(jnp.int32, row.shape, 1)
    return jnp.sum(jnp.where(lane == k, row, 0.0), axis=1, keepdims=True)


def attn_stats_kernel(even, odd, vec, stats, feed_shares, total, rows_new, shares, columns, rows16):
    own_width, width = total.shape[0] // 4, total.shape[1]
    mine = pl.ds(pl.multiple_of(lax.axis_index("mp") * own_width, own_width), own_width)
    read_halves(even, odd, total)
    scalars = []
    for k in range(4):
        grad = total[k * own_width : (k + 1) * own_width, :]
        square = grad * grad
        columns[...] = as_column(stats[k, 0:1, :])
        rows = decay * columns[mine, :] + (1.0 - decay) * jnp.mean(square + tiny_square, axis=1, keepdims=True)
        rows_new[k : k + 1, :] = as_row(rows)
        rows16[k : k + 1, :] = jnp.sum(square + tiny_square, axis=0, keepdims=True)
        rows16[4 + k : 5 + k, :] = jnp.sum(square * (1.0 / rows), axis=0, keepdims=True)
        scalars.append(jnp.sum(rows, axis=0, keepdims=True))
    rows16[8:12, :] = vec[0:4, :]
    rows16[12:16, :] = feed_shares[0:4, :]
    shares[0:16, :] = rows16[...].astype(bf16)
    row = lane_scalars(scalars, width) + feed_shares[4:5, :]
    high = row.astype(bf16).astype(f32)
    low = (row - high).astype(bf16).astype(f32)
    shares[16:24, :] = jnp.concatenate([high, low, jnp.zeros((6, width), f32)], axis=0).astype(bf16)


def attn_stats_call(even, odd, vec, stats, feed_shares, own_width):
    width = even.shape[1]
    return pl.pallas_call(
        attn_stats_kernel,
        out_shape=[near((4 * own_width, width), f32), near((4, own_width), f32), near((SHARE_ROWS, width), bf16)],
        scratch_shapes=[pltpu.VMEM((width, 1), f32), pltpu.VMEM((16, width), f32)],
        compiler_params=params(16),
        name="attn_stats",
    )(in_vmem(even), odd, in_vmem(vec), stats, in_vmem(feed_shares))


def attn_out_kernel(total, rows, grad_out, rows_out):
    own_width = grad_out.shape[1]
    for k in range(4):
        grad_out[k] = total[k * own_width : (k + 1) * own_width, :]
    rows_out[...] = rows[...]


def attn_out(total, rows):
    own_width, width = rows.shape[1], total.shape[1]
    return pl.pallas_call(
        attn_out_kernel,
        out_shape=[sds((4, own_width, width), f32), sds((4, own_width), f32)],
        compiler_params=params(8),
        cost_estimate=NO_COST,
        name="attn_out",
    )(*all_vmem((total, rows)))


def feed_stats_kernel(mine, other, wide_old, squares, up_grad_out, down_grad_out, wide_out, grads, wide_new, shares):
    width, hidden = up_grad_out.shape
    for part, rows in enumerate((width, hidden)):
        half = slice(part * width // 2, (part * width + rows) // 2)
        read_halves(mine.at[half], other.at[half], grads.at[part * width : part * width + rows])
    grad = grads[0:width, :]
    up_grad_out[...] = grad
    square = grad * grad
    columns = decay * wide_old[0:1, :] + (1.0 - decay) * jnp.mean(square + tiny_square, axis=0, keepdims=True)
    wide_new[0:1, :] = columns
    shares[0:1, :] = as_row(jnp.sum(square + tiny_square, axis=1, keepdims=True))
    shares[1:2, :] = as_row(jnp.sum(square * (1.0 / columns), axis=1, keepdims=True))
    grad = grads[width:, :]
    down_grad_out[...] = grad
    square = grad * grad
    rows = decay * as_column(wide_old[1:2, :]) + (1.0 - decay) * jnp.mean(
        square + tiny_square, axis=1, keepdims=True
    )
    wide_new[1:2, :] = as_row(rows)
    wide_out[...] = wide_new[...]
    shares[2:3, :] = jnp.sum(square + tiny_square, axis=0, keepdims=True)
    shares[3:4, :] = jnp.sum(square * (1.0 / rows), axis=0, keepdims=True)
    scalars = [jnp.sum(rows, axis=0, keepdims=True)]
    for k in range(2):
        scalars.append(jnp.sum(squares[4 + k : 5 + k, :], axis=1, keepdims=True))
    shares[4:5, :] = lane_scalars([0.0] * 4 + scalars, width)
    shares[5:8, :] = jnp.zeros((3, width), f32)


def feed_stats(even, odd, wide_old, squares):
    width, hidden = squares.shape[1], wide_old.shape[1]
    return pl.pallas_call(
        feed_stats_kernel,
        out_shape=[
            sds((width, hidden), f32),
            sds((hidden, width), f32),
            sds((2, hidden), f32),
            near((width + hidden, width), f32),
            near((2, hidden), f32),
            near((8, width), f32),
        ],
        compiler_params=params(16),
        cost_estimate=NO_COST,
        name="feed_stats",
    )(in_vmem(even), odd, wide_old, in_vmem(squares))


def add_shares(shares, slots):
    rank = lax.axis_index("mp")
    ranks = len(shares)
    rows = shares[0].shape[0]
    for k, share in zip(SHIFTS, shares):
        slots[pl.ds(pl.multiple_of(lax.rem(rank + ranks - k, ranks) * rows, rows), rows), :] = share[...].astype(f32)
    total = slots[0:rows, :]
    for k in range(1, ranks):
        total += slots[k * rows : (k + 1) * rows, :]
    return total


def update_kernel(
    hidden_all,
    attn_grad,
    attn_weight,
    attn_rows,
    stats,
    feed_grad,
    up_weight,
    down_weight,
    wide_new,
    narrow_old,
    squares,
    share0,
    share1,
    share2,
    share3,
    vec,
    vec_moment,
    *refs,
):
    outs, made, (slots, sems) = refs[0:11], refs[11:22], refs[22:]
    attn_new, attn_new_low, up_new, up_new_low, down_new, down_new_low = made[0:6]
    attn_cols, narrow_new, vec_grad, vec_moment_new, vec_new = made[6:11]
    width = narrow_old.shape[1]
    own_width = attn_rows.shape[1]
    copies = []

    def leave(which, *place):
        source = made[which].at[place] if place else made[which]
        target = outs[which].at[place] if place else outs[which]
        copy = pltpu.make_async_copy(source, target, sems.at[len(copies)])
        copy.start()
        copies.append(copy)

    total = add_shares((share0, share1, share2, share3), slots)
    scalars = total[16:17, :] + total[17:18, :]
    entries = float(width * hidden_all)
    rows = decay * narrow_old[0:1, :] + (1.0 - decay) * total[12:13, :] / hidden_all
    narrow_new[0:1, :] = rows
    cols = decay * narrow_old[1:2, :] + (1.0 - decay) * total[14:15, :] / hidden_all
    narrow_new[1:2, :] = cols
    mean_up = jnp.mean(rows, axis=1, keepdims=True)
    mean_down = lane_scalar(scalars, 4) / hidden_all

    def step_size(scaled, weight_square, count):
        clip = jnp.maximum(1.0, jnp.sqrt(scaled / count) / clip_limit)
        return learn_rate * jnp.sqrt(weight_square / count) / clip

    up_size = step_size(
        jnp.sum(total[13:14, :] / rows, axis=1, keepdims=True) * mean_up, lane_scalar(scalars, 5), entries
    )
    down_size = step_size(
        jnp.sum(total[15:16, :] / cols, axis=1, keepdims=True) * mean_down, lane_scalar(scalars, 6), entries
    )

    def block(which, here, grad, weight, row, col, mean, size):
        scale = row * col * (1.0 / mean)
        value = weight - size * (grad * lax.rsqrt(scale))
        made[which][here] = value
        made[which + 1][here] = value.astype(bf16)
        leave(which, *here)
        leave(which + 1, *here)

    pieces = 4
    row = as_column(rows)
    step = up_weight.shape[0] // pieces
    for n in range(pieces):
        here = slice(n * step, (n + 1) * step)
        block(2, (here, slice(None)), feed_grad[here, :], up_weight[here, :], row[here], wide_new[0:1, :], mean_up, up_size)
    row = as_column(wide_new[1:2, :])
    step = down_weight.shape[0] // pieces
    for n in range(pieces):
        here = slice(n * step, (n + 1) * step)
        below = slice(up_weight.shape[0] + n * step, up_weight.shape[0] + (n + 1) * step)
        block(4, (here, slice(None)), feed_grad[below, :], down_weight[here, :], row[here], cols, mean_down, down_size)
    leave(7)
    entries = float(width * width)
    for k in range(4):
        col = decay * stats[k, 1:2, :] + (1.0 - decay) * total[k : k + 1, :] / width
        attn_cols[k : k + 1, :] = col
        mean = lane_scalar(scalars, k) / width
        size = step_size(
            jnp.sum(total[4 + k : 5 + k, :] / col, axis=1, keepdims=True) * mean,
            jnp.sum(squares[k : k + 1, :], axis=1, keepdims=True),
            entries,
        )
        block(
            0, (k,), attn_grad[k * own_width : (k + 1) * own_width, :], attn_weight[k], as_column(attn_rows[k : k + 1, :]),
            col, mean, size,
        )
    leave(6)
    grads = total[8:12, :]
    vec_grad[...] = grads
    leave(8)
    moment = decay * vec_moment[...] + (1.0 - decay) * (grads * grads + tiny_square)
    vec_moment_new[...] = moment
    leave(9)
    scaled = grads * lax.rsqrt(moment)
    clip = jnp.maximum(1.0, jnp.sqrt(jnp.mean(scaled * scaled, axis=1, keepdims=True)) / clip_limit)
    held = vec[...]
    spread = jnp.sqrt(jnp.mean(held * held, axis=1, keepdims=True))
    vec_new[...] = held - learn_rate * spread * scaled / clip
    leave(10)
    for copy in copies:
        copy.wait()


def update(
    attn_grad, attn_weight, attn_rows, stats, feed_grad, up_weight, down_weight, wide_new, narrow_old, squares, shares,
    vec, vec_moment, hidden_all,
):
    _, own_width, width = attn_weight.shape
    hidden = up_weight.shape[1]
    outs = [((4, own_width, width), t) for t in (f32, bf16)]
    outs += [((width, hidden), t) for t in (f32, bf16)] + [((hidden, width), t) for t in (f32, bf16)]
    outs += [((4, width), f32), ((2, width), f32)] + [((4, width), f32)] * 3
    return pl.pallas_call(
        functools.partial(update_kernel, hidden_all),
        in_specs=[pl.BlockSpec(memory_space=pltpu.VMEM)] * 16,
        out_specs=[pl.BlockSpec(memory_space=pl.ANY)] * 11,
        out_shape=[pltpu.HBM(*out) for out in outs],
        scratch_shapes=[pltpu.VMEM(*out) for out in outs]
        + [pltpu.VMEM((SHARE_ROWS * len(shares), width), f32), pltpu.SemaphoreType.DMA((29,))],
        compiler_params=params(24),
        name="update",
    )(
        *all_vmem((attn_grad, attn_weight, attn_rows)), stats,
        *all_vmem((feed_grad, up_weight, down_weight, wide_new)), narrow_old, in_vmem(squares), in_vmem(shares[0]),
        *shares[1:], vec, vec_moment,
    )


def to_next(block, shift, ranks):
    return lax.ppermute(block, "mp", [(i, (i + shift) % ranks) for i in range(ranks)])


def exchange(parts, shifts=SHIFTS):
    return [parts[0]] + [to_next(part, shift, len(parts)) for part, shift in zip(parts[1:], shifts[1:])]


def spread_out(block, ranks):
    return exchange([block] * ranks)


def on_device(
    tokens,
    cotangent,
    seq_starts,
    attn_weight,
    up_weight,
    down_weight,
    vec_params,
    attn_stats,
    ffn_narrow_stats,
    ffn_wide_stats,
    vec_moment,
):
    ranks = lax.axis_size("mp")
    local, width = tokens.shape
    own_width = width // ranks
    hidden_all = up_weight.shape[1] * ranks

    blocks = spread_out(tokens, ranks)
    attn_low, up_low, down_low, mask, mask_t, squares = prepare(
        seq_starts, attn_weight, up_weight, down_weight, local * ranks
    )
    (
        x_all,
        query_feat,
        key_feat,
        value_low,
        mixed_low,
        inverse,
        own_sum,
        own_first,
        first_low,
        pre_act,
        hidden_low,
        *parts,
    ) = forward(blocks, attn_low, up_low, down_low, mask, vec_params)
    parts = exchange(parts, SUM_SHIFTS)
    weights_t, query_slope, key_slope, slope = slopes(query_feat, key_feat, mask_t, pre_act)
    own_first, slope = lax.optimization_barrier((own_first, slope))
    feats = (query_feat, key_feat, value_low, query_slope, key_slope, weights_t, mask, mask_t)
    mixing = (attn_low, mixed_low, inverse, *feats)
    feeding = (up_low, down_low, first_low, slope, hidden_low)
    block_out, d_second, sums, *d_branch = middle(
        parts, own_first, cotangent, vec_params, (*mixing, *feeding, own_sum, x_all)
    )
    turned_from, d_second = lax.optimization_barrier((x_all, d_second))
    x_slice, mixed_slice = own_columns(turned_from, mixed_low, own_width)
    slope, x_slice = lax.optimization_barrier((slope, x_slice))
    d_branch, d_pre, *parts = feed_back(
        exchange(d_branch), slope, up_low, down_low, (*mixing, first_low, hidden_low, own_sum, d_second, sums, x_slice, mixed_slice)
    )
    staged = lax.axis_size("dp") == STAGED

    parts = exchange(parts, SUM_SHIFTS)
    *feed_keep, up_send, down_send = feed_grads(first_low, d_pre, hidden_low, d_branch)
    if staged:
        up = fold_first(feed_keep[0], across(up_send, 1))
        down = fold_first(feed_keep[1], across(down_send, 1))
        parts[0], up, down = lax.optimization_barrier((parts[0], up, down))
        got_up, got_down = [[across(a, 2), across(b, 4)] for a, b in (up, down)]
    d_resid, sums, *d_attn = first_back(
        parts, d_second, own_sum, sums, vec_params, (*mixing, x_slice, mixed_slice)
    )
    blocks = exchange(d_attn)
    if staged:
        d_resid, up, down = lax.optimization_barrier((d_resid, up, down))
        feed_a, feed_b = fold_feed((*up, *down), (*got_up, *got_down))
        blocks[0], feed_a, feed_b = lax.optimization_barrier((blocks[0], feed_a, feed_b))
        got_a, got_b = across(feed_a, 4), across(feed_b, 2)
    first = mix_first(blocks, attn_low, mixed_low, inverse, feats)
    *d_mix, vec_part, attn_keep, attn_send = mix_second(first, attn_low, feats, x_slice, mixed_slice, sums)
    if staged:
        feed_even = fold_feed_last(feed_a, got_a, feed_b, got_b)
        attn_send, feed_even = lax.optimization_barrier((attn_send, feed_even))
        received = across(attn_send, 1)
        feed_odd = across(feed_even, 1)
        vec_part, attn_a, attn_b = fold_first(attn_keep, received, vec_part)
        got_a, got_b = across(attn_a, 2), across(attn_b, 4)
    else:
        feed_even, feed_odd, attn_even, attn_odd, vec_part = lax.psum(
            (jnp.concatenate(feed_keep), jnp.concatenate([up_send, down_send]).astype(f32), attn_keep, attn_send[: 2 * own_width].astype(f32), vec_part), "dp"
        )
    up_grad, down_grad, wide_out, feed_near, wide_near, feed_shares = feed_stats(
        feed_even, feed_odd, ffn_wide_stats, squares
    )
    tokens_grad, own_attn, own_up, own_down = tokens_back(
        *d_mix, attn_low, d_resid, attn_weight, up_weight, down_weight, own_width
    )
    if staged:
        attn_a, feed_shares = lax.optimization_barrier((attn_a, feed_shares))
        vec_part, attn_a, attn_b = fold_second(attn_a, got_a, attn_b, got_b, vec_part)
        got_a, got_b = across(attn_a, 4), across(attn_b, 2)
        attn_a, tokens_grad = lax.optimization_barrier((attn_a, tokens_grad))
        vec_part, attn_even = fold_last(attn_a, got_a, attn_b, got_b, vec_part)
        attn_odd = across(attn_even, 1)
    attn_near, rows_near, shares = attn_stats_call(attn_even, attn_odd, vec_part, attn_stats, feed_shares, own_width)
    shares = spread_out(shares, ranks)
    attn_grad, attn_rows = attn_out(attn_near, rows_near)
    attn_near, attn_grad = lax.optimization_barrier((attn_near, attn_grad))
    (
        attn_new,
        attn_new_low,
        up_new,
        up_new_low,
        down_new,
        down_new_low,
        attn_cols,
        narrow_new,
        vec_grad,
        vec_moment_new,
        vec_new,
    ) = update(
        attn_near, own_attn, rows_near, attn_stats, feed_near, own_up, own_down, wide_near, ffn_narrow_stats,
        squares, shares, vec_params, vec_moment, hidden_all,
    )
    return (
        block_out,
        tokens_grad,
        attn_grad,
        attn_rows,
        attn_cols,
        attn_new,
        attn_new_low,
        up_grad,
        down_grad,
        narrow_new,
        wide_out,
        up_new,
        down_new,
        up_new_low,
        down_new_low,
        vec_grad,
        vec_moment_new,
        vec_new,
    )


def solution(mesh):
    in_specs = (
        P(("dp", "mp"), None),
        P(("dp", "mp"), None),
        P("dp", None),
        P(),
        P(None, "mp"),
        P("mp", None),
        P(),
        P(),
        P(),
        P(None, "mp"),
        P(),
    )
    out_specs = (
        P(("dp", "mp"), None),
        P(("dp", "mp"), None),
        P(None, "mp", None),
        P(None, "mp"),
        P(),
        P(None, "mp", None),
        P(None, "mp", None),
        P(None, "mp"),
        P("mp", None),
        P(),
        P(None, "mp"),
        P(None, "mp"),
        P("mp", None),
        P(None, "mp"),
        P("mp", None),
        P(),
        P(),
        P(),
    )
    return jax.shard_map(
        on_device, mesh=mesh, in_specs=in_specs, out_specs=out_specs, check_vma=False
    )
```

```python
import functools
import math

import jax
import jax.numpy as jnp
from jax import lax
from jax.experimental import pallas as pl
from jax.experimental.pallas import tpu as pltpu
from jax.sharding import PartitionSpec as P

HEADS = 12
STEP = 10

norm_eps = 1e-05
tiny_square = 1e-30
learn_rate = 0.3
clip_limit = 1.0
decay = 1.0 - float(STEP) ** (-0.8)

f32 = jnp.float32
bf16 = jnp.bfloat16

NN = (((1,), (0,)), ((), ()))
NT = (((1,), (1,)), ((), ()))
TN = (((0,), (0,)), ((), ()))


def mm(a, b, dims=NN):
    return lax.dot_general(a, b, dims, preferred_element_type=f32)


def params(mib):
    return pltpu.CompilerParams(vmem_limit_bytes=mib * 1024 * 1024)


def sds(shape, dtype):
    return jax.ShapeDtypeStruct(shape, dtype)


def in_hbm(array):
    return pltpu.with_memory_space_constraint(array, pltpu.HBM)


def in_vmem(array):
    return pltpu.with_memory_space_constraint(array, pltpu.VMEM)


def all_vmem(arrays):
    return [in_vmem(array) for array in arrays]


def near(shape, dtype):
    return pltpu.VMEM(shape, dtype)


NO_COST = pl.CostEstimate(flops=0, bytes_accessed=0, transcendentals=0)


def holding(kernel, count, held):
    def body(*refs):
        for ref in refs[count : count + held]:
            pltpu.touch(ref)
        kernel(*refs[:count], *refs[count + held :])

    return body


STAGED = 8
VEC_ROWS = 16
TOKEN_STEPS = (0, -2, -1, -3)
BRANCH_STEPS = (0, 1, 2, 3)
BACK_STEPS = (0, 2, 1, 3)
FIRST_STEPS = (0, 1, 2, 3)
MIX_STEPS = (0, 2, 1, 3)
SHARE_STEPS = (0, -1, -2, -3)


def target(rank, step, ranks):
    return rank ^ -step if step <= 0 else (rank + step) % ranks


def source(rank, step, ranks):
    return rank ^ -step if step <= 0 else (rank + ranks - step) % ranks


def rank_rows(rank, rows):
    return pl.ds(pl.multiple_of(rank * rows, rows), rows)


def half_rows(count, mine):
    rows = count // 2
    side = lax.rem(lax.axis_index("dp"), 2) if lax.axis_size("dp") == STAGED else 0
    return pl.ds(pl.multiple_of((side if mine else 1 - side) * rows, rows), rows)


def write_halves(total, keep, send):
    rows = total.shape[0] // 2
    keep[...] = total[half_rows(total.shape[0], True), :]
    send[0:rows, :] = total[half_rows(total.shape[0], False), :].astype(send.dtype)


def read_halves(mine, other, total):
    total[half_rows(total.shape[0], True), :] = mine[...].astype(total.dtype)
    total[half_rows(total.shape[0], False), :] = other[...].astype(total.dtype)


def two_parts(values):
    high = values.astype(bf16).astype(f32)
    low = (values - high).astype(bf16).astype(f32)
    both = jnp.concatenate([high, low], axis=0)
    return high + low, jnp.concatenate([both, jnp.zeros_like(both)], axis=0).astype(bf16)


def joined(block):
    block = block.astype(f32)
    return block[0:4, :] + block[4:8, :]


def add_vec(vec, block, vec_out, send=None):
    held, packed = two_parts(vec[0:4, :] + joined(block))
    vec_out[0:4, :] = held
    vec_out[4:8, :] = jnp.zeros_like(held)
    if send is not None:
        send[...] = packed


def fold_first_kernel(keep, received, *refs):
    send_a, send_b = refs[-2:]
    rows = keep.shape[0] // 2
    send_a[0:rows, :] = (keep[0:rows, :] + received[0:rows, :].astype(f32)).astype(bf16)
    send_b[...] = (keep[rows : 2 * rows, :] + received[rows : 2 * rows, :].astype(f32)).astype(bf16)
    if len(refs) > 2:
        add_vec(refs[0], received[2 * rows :, :], refs[1], send_a.at[rows:, :])


def fold_second_kernel(own_a, got_a, own_b, got_b, *refs):
    send_a, send_b = refs[-2:]
    rows = own_b.shape[0]
    send_a[0:rows, :] = (own_a[0:rows, :].astype(f32) + got_a[0:rows, :].astype(f32)).astype(bf16)
    send_b[...] = (own_b[...].astype(f32) + got_b[...].astype(f32)).astype(bf16)
    if len(refs) > 2:
        add_vec(refs[0], got_a[rows:, :], refs[1], send_a.at[rows:, :])


def fold_last_kernel(own_a, got_a, own_b, got_b, *refs):
    total = refs[-1]
    rows = own_b.shape[0]
    total[0:rows, :] = (own_a[0:rows, :].astype(f32) + got_a[0:rows, :].astype(f32)).astype(bf16)
    total[rows:, :] = (own_b[...].astype(f32) + got_b[...].astype(f32)).astype(bf16)
    if len(refs) > 1:
        add_vec(refs[0], got_a[rows:, :], refs[1])


def fold_call(kernel, name, inputs, vec, outs):
    width = inputs[0].shape[1]
    extra_in, extra_out = ([in_vmem(vec)], [near((8, width), f32)]) if vec is not None else ([], [])
    return pl.pallas_call(
        kernel,
        out_shape=extra_out + [near((rows, width), bf16) for rows in outs],
        compiler_params=params(8),
        cost_estimate=NO_COST,
        name=name,
    )(in_vmem(inputs[0]), *inputs[1:], *extra_in)


def fold_first(keep, received, vec=None):
    rows = keep.shape[0] // 2
    return fold_call(
        fold_first_kernel, "fold_first", (keep, received), vec, (rows if vec is None else rows + VEC_ROWS, rows)
    )


def fold_second(own_a, got_a, own_b, got_b, vec=None):
    return fold_call(
        fold_second_kernel, "fold_second", (own_a, got_a, own_b, got_b), vec, (own_a.shape[0], own_b.shape[0])
    )


def fold_last(own_a, got_a, own_b, got_b, vec=None):
    return fold_call(fold_last_kernel, "fold_last", (own_a, got_a, own_b, got_b), vec, (2 * own_b.shape[0],))


def fold_feed_kernel(*refs):
    own, got, (send_a, send_b) = refs[0:4], refs[4:8], refs[8:]
    rows = own[0].shape[0]
    for n, (block, other) in enumerate(zip(own, got)):
        send = (send_a, send_b)[n % 2]
        place = n // 2 * rows
        send[place : place + rows, :] = (block[...].astype(f32) + other[...].astype(f32)).astype(bf16)


def fold_feed(own, got):
    rows, width = own[0].shape
    return pl.pallas_call(
        fold_feed_kernel,
        out_shape=[near((2 * rows, width), bf16)] * 2,
        compiler_params=params(8),
        cost_estimate=NO_COST,
        name="fold_feed",
    )(*all_vmem(own), *got)


def fold_feed_last_kernel(own_a, got_a, own_b, got_b, total):
    rows = own_a.shape[0] // 2
    for n, (block, other) in enumerate(((own_a, got_a), (own_b, got_b))):
        for part in range(2):
            here = slice(part * rows, (part + 1) * rows)
            place = (2 * part + n) * rows
            total[place : place + rows, :] = (block[here, :].astype(f32) + other[here, :].astype(f32)).astype(bf16)


def fold_feed_last(own_a, got_a, own_b, got_b):
    rows, width = own_a.shape
    return pl.pallas_call(
        fold_feed_last_kernel,
        out_shape=near((2 * rows, width), bf16),
        compiler_params=params(8),
        cost_estimate=NO_COST,
        name="fold_feed_last",
    )(in_vmem(own_a), got_a, in_vmem(own_b), got_b)


def across(block, bit):
    return lax.ppermute(block, "dp", [(i, i ^ bit) for i in range(STAGED)])


def prepare_kernel(seqs, tokens_pack, starts, attn, up, down, attn_low, up_low, down_low, mask, mask_t, squares):
    step = pl.program_id(0)

    @pl.when(step == 0)
    def _():
        squares[...] = jnp.zeros_like(squares)

    for k in range(4):
        block = attn[k]
        attn_low[k] = block.astype(bf16)
        squares[k : k + 1, :] += jnp.sum(block * block, axis=0, keepdims=True)
    for k, (source, target) in enumerate(((up, up_low), (down, down_low))):
        block = source[...]
        target[...] = block.astype(bf16)
        squares[4 + k : 5 + k, :] += jnp.sum(block * block, axis=0, keepdims=True)

    def layout(index):
        seq = jnp.zeros_like(index)
        begin = jnp.zeros_like(index)
        length = jnp.ones_like(index)
        for s in range(seqs):
            start = starts[0, s]
            finish = starts[0, s + 1] if s + 1 < seqs else tokens_pack
            inside = index >= start
            seq = jnp.where(inside, s, seq)
            begin = jnp.where(inside, start, begin)
            length = jnp.where(inside, finish - start, length)
        angle = 0.5 * math.pi * (index - begin).astype(f32) / length.astype(f32)
        return seq, jnp.cos(angle), jnp.sin(angle)

    rows = mask.shape[0]
    row = lax.broadcasted_iota(jnp.int32, (rows, 128), 0) + step * rows
    col = lax.broadcasted_iota(jnp.int32, (8, tokens_pack), 1)
    row_seq, row_cos, row_sin = (a[:, 0:1] for a in layout(row))
    col_seq, col_cos, col_sin = (a[0:1, :] for a in layout(col))
    same = row_seq == col_seq
    value = row_cos * col_cos + row_sin * col_sin
    row, col = row[:, 0:1], col[0:1, :]
    mask[...] = jnp.where(same & (col <= row), value, 0.0)
    mask_t[...] = jnp.where(same & (row <= col), value, 0.0)


def prepare(seq_starts, attn_weight, up_weight, down_weight, tokens_pack):
    steps = 8
    seqs = seq_starts.shape[1]
    heads4, width, _ = attn_weight.shape
    hidden = up_weight.shape[1]
    a_rows, u_rows, d_rows, m_rows = width // steps, width // steps, hidden // steps, tokens_pack // steps
    return pl.pallas_call(
        functools.partial(prepare_kernel, seqs, tokens_pack),
        grid=(steps,),
        in_specs=[
            pl.BlockSpec(memory_space=pltpu.SMEM),
            pl.BlockSpec((4, a_rows, width), lambda i: (0, i, 0)),
            pl.BlockSpec((u_rows, hidden), lambda i: (i, 0)),
            pl.BlockSpec((d_rows, width), lambda i: (i, 0)),
        ],
        out_specs=[
            pl.BlockSpec((4, a_rows, width), lambda i: (0, i, 0)),
            pl.BlockSpec((u_rows, hidden), lambda i: (i, 0)),
            pl.BlockSpec((d_rows, width), lambda i: (i, 0)),
            pl.BlockSpec((m_rows, tokens_pack), lambda i: (i, 0)),
            pl.BlockSpec((m_rows, tokens_pack), lambda i: (i, 0)),
            pl.BlockSpec((8, width), lambda i: (0, 0)),
        ],
        out_shape=[
            near((4, width, width), bf16),
            near((width, hidden), bf16),
            near((hidden, width), bf16),
            near((tokens_pack, tokens_pack), f32),
            near((tokens_pack, tokens_pack), f32),
            near((8, width), f32),
        ],
        compiler_params=params(24),
        cost_estimate=pl.CostEstimate(flops=10_000_000, bytes_accessed=22_000_000, transcendentals=0),
        name="prepare",
    )(seq_starts, in_hbm(attn_weight), in_hbm(up_weight), in_hbm(down_weight))


def half_lanes(width):
    return lax.broadcasted_iota(jnp.int32, (1, width), 1) < width // 2


def norm_parts(values):
    centered = values - jnp.mean(values, axis=-1, keepdims=True)
    spread = lax.rsqrt(jnp.mean(centered * centered, axis=-1, keepdims=True) + norm_eps)
    return centered * spread, spread


def norm_back(grad, unit, spread, gain):
    scaled = grad * gain
    return spread * (
        scaled
        - jnp.mean(scaled, axis=-1, keepdims=True)
        - unit * jnp.mean(scaled * unit, axis=-1, keepdims=True)
    )


def causal_blocks(tokens, size):
    return [(i, min(size, tokens - i)) for i in range(0, tokens, size)]


def forward_kernel(
    local,
    x0,
    x1,
    x2,
    x3,
    attn_low,
    up_low,
    down_low,
    mask,
    vec,
    x_all,
    query_feat,
    key_feat,
    value_low,
    mixed_low,
    inverse,
    own_sum,
    own_first,
    first_low,
    pre_act,
    hidden_low,
    part0,
    part1,
    part2,
    part3,
    branch,
):
    rank = lax.axis_index("mp")
    tokens, width = x_all.shape
    ranks = tokens // local

    for step, block in zip(TOKEN_STEPS, (x0, x1, x2, x3)):
        x_all[rank_rows(source(rank, step, ranks), local), :] = block[...]

    piece = 256
    for c in range(0, width, piece):
        cols = slice(c, c + piece)
        for which, feat in ((0, query_feat), (1, key_feat)):
            raw = mm(x_all[...], attn_low[which, :, cols])
            feat[:, cols] = jax.nn.softplus(raw).astype(bf16)
        value_low[:, cols] = mm(x_all[...], attn_low[2, :, cols]).astype(bf16)

    pair = 2 * (width // HEADS)
    first_half = half_lanes(pair)
    for c in range(0, width, pair):
        cols = slice(c, c + pair)
        keys = key_feat[:, cols]
        values = value_low[:, cols]
        zero = jnp.zeros_like(keys)
        one = jnp.ones_like(values)
        sides = (first_half, ~first_half)
        own_keys = [jnp.where(own, keys, zero) for own in sides]
        own_values = [
            jnp.concatenate([jnp.where(own, values, zero), jnp.where(own, one, zero)], axis=1) for own in sides
        ]
        for i, rows in causal_blocks(tokens, 256):
            here = slice(i, i + rows)
            upto = i + rows
            queries = query_feat[here, cols]
            allowed = mask[here, :upto]
            scores = mm(queries, jnp.concatenate([block[:upto] for block in own_keys], axis=0), NT)
            weights = (scores * jnp.concatenate([allowed, allowed], axis=1)).astype(bf16)
            both = mm(weights, jnp.concatenate([block[:upto] for block in own_values], axis=0))
            inv = 1.0 / both[:, pair:]
            inverse[here, cols] = inv
            mixed_low[here, cols] = (both[:, :pair] * inv).astype(bf16)

    for i, rows in causal_blocks(tokens, 256):
        here = slice(i, i + rows)
        summed = x_all[here, :].astype(f32) + mm(mixed_low[here, :], attn_low[3])
        branch[here, :] = summed
        unit, _ = norm_parts(summed)
        first_low[here, :] = (unit * vec[0:1, :] + vec[1:2, :]).astype(bf16)
    own_sum[...] = branch[rank_rows(rank, local), :]
    unit, _ = norm_parts(own_sum[...])
    own_first[...] = unit * vec[0:1, :] + vec[1:2, :]

    hidden_count = up_low.shape[1]
    for c in range(0, hidden_count, piece):
        cols = slice(c, c + piece)
        pre = mm(first_low[...], up_low[:, cols])
        cdf = 0.5 * (1.0 + lax.erf(pre * math.sqrt(0.5)))
        hidden_low[:, cols] = (pre * cdf).astype(bf16)
        pre_act[:, cols] = pre

    branch[...] = mm(hidden_low[...], down_low[...])
    for step, part in zip(BRANCH_STEPS, (part0, part1, part2, part3)):
        part[...] = branch[rank_rows(target(rank, step, ranks), local), :].astype(part.dtype)


def forward(blocks, attn_low, up_low, down_low, mask, vec):
    local, width = blocks[0].shape
    tokens = mask.shape[0]
    hidden = up_low.shape[1]
    return pl.pallas_call(
        functools.partial(forward_kernel, local),
        out_shape=[near((tokens, width), bf16)] * 5
        + [near((tokens, width), f32), near((local, width), f32), near((local, width), f32)]
        + [near((tokens, width), bf16), near((tokens, hidden), f32), near((tokens, hidden), bf16)]
        + [near((local, width), f32)]
        + [near((local, width), bf16)] * 3,
        scratch_shapes=[pltpu.VMEM((tokens, width), f32)],
        compiler_params=params(16),
        cost_estimate=pl.CostEstimate(flops=8_000_000_000, bytes_accessed=20_000_000, transcendentals=2_000_000),
        name="forward",
    )(*blocks, *all_vmem((attn_low, up_low, down_low, mask)), vec)


def slopes_kernel(query_feat, key_feat, mask_t, pre_act, weights_t, query_slope, key_slope, slope):
    tokens, width = query_feat.shape
    piece = 256
    for c in range(0, width, piece):
        cols = slice(c, c + piece)
        for feat, grad in ((query_feat, query_slope), (key_feat, key_slope)):
            value = feat[:, cols].astype(f32)
            small = value * (1.0 - value * (0.5 - value * (1.0 / 6.0)))
            grad[:, cols] = jnp.where(value < 0.02, small, 1.0 - jnp.exp(-value)).astype(bf16)
    for c in range(0, pre_act.shape[1], piece):
        cols = slice(c, c + piece)
        pre = pre_act[:, cols]
        cdf = 0.5 * (1.0 + lax.erf(pre * math.sqrt(0.5)))
        slope[:, cols] = cdf + pre * (jnp.exp(-0.5 * pre * pre) * (1.0 / math.sqrt(2.0 * math.pi)))
    pair = 2 * (width // HEADS)
    first_half = half_lanes(pair)
    for head in range(HEADS):
        cols = slice(head // 2 * pair, (head // 2 + 1) * pair)
        own = first_half if head % 2 == 0 else ~first_half
        for i, rows in causal_blocks(tokens, 256):
            here = slice(i, i + rows)
            keys = key_feat[here, cols]
            scores = mm(jnp.where(own, keys, jnp.zeros_like(keys)), query_feat[i:, cols], NT)
            weights_t[head * tokens + i : head * tokens + i + rows, i:] = (scores * mask_t[here, i:]).astype(bf16)


def slopes(query_feat, key_feat, mask_t, pre_act):
    tokens, width = query_feat.shape
    return pl.pallas_call(
        slopes_kernel,
        out_shape=[near((HEADS * tokens, tokens), bf16)]
        + [near((tokens, width), bf16)] * 2
        + [near(pre_act.shape, f32)],
        compiler_params=params(16),
        cost_estimate=NO_COST,
        name="slopes",
    )(*all_vmem((query_feat, key_feat, mask_t, pre_act)))


def middle_kernel(part0, part1, part2, part3, own_first, cotangent, vec, block_out, d_second, sums, *d_branch):
    branch = part0[...] + part1[...].astype(f32) + part2[...].astype(f32) + part3[...].astype(f32)
    unit, spread = norm_parts(own_first[...] + branch)
    gain = vec[2:3, :]
    block_out[...] = unit * gain + vec[3:4, :]
    grad = cotangent[...].astype(f32)
    inner = norm_back(grad, unit, spread, gain)
    d_second[...] = inner
    for copy in d_branch:
        copy[...] = inner.astype(bf16)
    sums[...] = jnp.zeros_like(sums)
    sums[2:3, :] = jnp.sum(grad * unit, axis=0, keepdims=True)
    sums[3:4, :] = jnp.sum(grad, axis=0, keepdims=True)


def middle(parts, own_first, cotangent, vec, held):
    local, width = own_first.shape
    return pl.pallas_call(
        holding(middle_kernel, 7, len(held)),
        out_shape=[near((local, width), f32), near((local, width), f32), near((8, width), f32)]
        + [near((local, width), bf16)] * 4,
        compiler_params=params(8),
        name="middle",
    )(in_vmem(parts[0]), *parts[1:], in_vmem(own_first), cotangent, vec, *all_vmem(held))


def feed_back_kernel(
    local, d0, d1, d2, d3, slope, up_low, down_low, d_branch, d_pre, part0, part1, part2, part3, total
):
    rank = lax.axis_index("mp")
    tokens, width = d_branch.shape
    ranks = tokens // local

    for step, block in zip(BACK_STEPS, (d0, d1, d2, d3)):
        d_branch[rank_rows(source(rank, step, ranks), local), :] = block[...]
    piece = 256
    for c in range(0, d_pre.shape[1], piece):
        cols = slice(c, c + piece)
        d_pre[:, cols] = (mm(d_branch[...], down_low[cols, :], NT) * slope[:, cols]).astype(bf16)
    total[...] = mm(d_pre[...], up_low[...], NT)
    for step, part in zip(FIRST_STEPS, (part0, part1, part2, part3)):
        part[...] = total[rank_rows(target(rank, step, ranks), local), :].astype(part.dtype)


def feed_back(blocks, slope, up_low, down_low, held):
    local, width = blocks[0].shape
    tokens, hidden = slope.shape
    return pl.pallas_call(
        holding(functools.partial(feed_back_kernel, local), 7, len(held)),
        out_shape=[near((tokens, width), bf16), near((tokens, hidden), bf16), near((local, width), f32)]
        + [near((local, width), bf16)] * 3,
        scratch_shapes=[pltpu.VMEM((tokens, width), f32)],
        compiler_params=params(16),
        cost_estimate=pl.CostEstimate(flops=1_200_000_000, bytes_accessed=9_000_000, transcendentals=0),
        name="feed_back",
    )(in_vmem(blocks[0]), *blocks[1:], *all_vmem((slope, up_low, down_low, *held)))


def feed_grads_kernel(first_low, d_pre, hidden_low, d_branch, keep_up, keep_down, send_up, send_down):
    for left, right, keep, send in (
        (first_low, d_pre, keep_up, send_up),
        (hidden_low, d_branch, keep_down, send_down),
    ):
        keep[...] = mm(left[:, half_rows(left.shape[1], True)], right[...], TN)
        send[...] = mm(left[:, half_rows(left.shape[1], False)], right[...], TN).astype(bf16)


def feed_grads(first_low, d_pre, hidden_low, d_branch):
    width, hidden = first_low.shape[1], d_pre.shape[1]
    return pl.pallas_call(
        feed_grads_kernel,
        out_shape=[near((width // 2, hidden), f32), near((hidden // 2, width), f32)]
        + [near((width // 2, hidden), bf16), near((hidden // 2, width), bf16)],
        compiler_params=params(16),
        cost_estimate=NO_COST,
        name="feed_grads",
    )(*all_vmem((first_low, d_pre, hidden_low, d_branch)))


def first_back_kernel(part0, part1, part2, part3, d_second, own_sum, sums_in, vec, d_resid, sums, *d_attn):
    grad = d_second[...] + part0[...] + part1[...].astype(f32) + part2[...].astype(f32) + part3[...].astype(f32)
    unit, spread = norm_parts(own_sum[...])
    inner = norm_back(grad, unit, spread, vec[0:1, :])
    d_resid[...] = inner
    for copy in d_attn:
        copy[...] = inner.astype(bf16)
    sums[...] = sums_in[...]
    sums[0:1, :] = jnp.sum(grad * unit, axis=0, keepdims=True)
    sums[1:2, :] = jnp.sum(grad, axis=0, keepdims=True)


def first_back(parts, d_second, own_sum, sums, vec, held):
    local, width = own_sum.shape
    return pl.pallas_call(
        holding(first_back_kernel, 8, len(held)),
        out_shape=[near((local, width), f32), near((8, width), f32)] + [near((local, width), bf16)] * 4,
        compiler_params=params(8),
        name="first_back",
    )(in_vmem(parts[0]), *parts[1:], *all_vmem((d_second, own_sum, sums)), vec, *all_vmem(held))


def own_columns_kernel(x_all, mixed_low, block_near, x_slice, mixed_slice, block_out, turned):
    block_out[...] = block_near[...]
    rows = x_slice.shape[0]
    mine = pl.ds(pl.multiple_of(lax.axis_index("mp") * rows, rows), rows)
    for source, target in ((x_all, x_slice), (mixed_low, mixed_slice)):
        turned[...] = jnp.transpose(source[...])
        target[...] = turned[mine, :]


def own_columns(x_all, mixed_low, block_near, own_width):
    tokens, width = x_all.shape
    return pl.pallas_call(
        own_columns_kernel,
        out_shape=[near((own_width, tokens), bf16)] * 2 + [sds(block_near.shape, f32)],
        scratch_shapes=[pltpu.VMEM((width, tokens), bf16)],
        compiler_params=params(8),
        cost_estimate=NO_COST,
        name="own_columns",
    )(*all_vmem((x_all, mixed_low, block_near)))


def mix_heads(
    start, d_num, d_den, query_feat, key_feat, value_low, query_slope, key_slope, weights_t, mask, mask_t, d_query, d_key,
    d_value,
):
    tokens, width = query_feat.shape
    pair = 2 * (width // HEADS)
    first_half = half_lanes(pair)
    spans = causal_blocks(tokens, 256)
    for c in range(start, start + width // 2, pair):
        cols = slice(c, c + pair)
        queries = query_feat[:, cols]
        keys = key_feat[:, cols]
        values = value_low[:, cols]
        nums = d_num[:, cols]
        left = jnp.concatenate([nums, d_den[:, cols]], axis=1)
        zero = jnp.zeros_like(keys)
        minus = jnp.full_like(values, -1)
        sides = (first_half, ~first_half)
        own_query = [jnp.where(own, queries, zero) for own in sides]
        own_key = [jnp.where(own, keys, zero) for own in sides]
        own_num = [jnp.where(own, nums, zero) for own in sides]
        right = [
            jnp.concatenate([jnp.where(own, values, zero), jnp.where(own, minus, zero)], axis=1) for own in sides
        ]
        base = 2 * (c // pair) * tokens
        out = slice(c - start, c - start + pair)
        for i, rows in spans:
            here = slice(i, i + rows)
            upto = i + rows
            allowed = mask[here, :upto]
            d_scores = mm(left[here], jnp.concatenate([block[:upto] for block in right], axis=0), NT)
            d_scores = (d_scores * jnp.concatenate([allowed, allowed], axis=1)).astype(bf16)
            grad = mm(d_scores, jnp.concatenate([block[:upto] for block in own_key], axis=0))
            d_query[here, out] = (grad * query_slope[here, cols].astype(f32)).astype(bf16)
            weights = jnp.concatenate(
                [weights_t[base + half * tokens + i : base + half * tokens + i + rows, i:] for half in range(2)], axis=1
            )
            grad = mm(weights, jnp.concatenate([block[i:] for block in own_num], axis=0))
            d_value[here, out] = grad.astype(bf16)
            allowed = mask_t[here, i:]
            d_scores_t = mm(jnp.concatenate([block[here] for block in right], axis=0), left[i:], NT)
            d_scores_t = [(d_scores_t[half * rows : (half + 1) * rows] * allowed).astype(bf16) for half in range(2)]
            grad = mm(
                jnp.concatenate(d_scores_t, axis=1), jnp.concatenate([block[i:] for block in own_query], axis=0)
            )
            d_key[here, out] = (grad * key_slope[here, cols].astype(f32)).astype(bf16)


def mix_first_kernel(
    local,
    a0,
    a1,
    a2,
    a3,
    attn_low,
    mixed_low,
    inverse,
    query_feat,
    key_feat,
    value_low,
    query_slope,
    key_slope,
    weights_t,
    mask,
    mask_t,
    d_attn,
    d_num,
    d_den,
    d_query,
    d_key,
    d_value,
):
    rank = lax.axis_index("mp")
    tokens, width = d_attn.shape
    ranks = tokens // local
    for step, block in zip(MIX_STEPS, (a0, a1, a2, a3)):
        d_attn[rank_rows(source(rank, step, ranks), local), :] = block[...]
    piece = 768
    for c in range(0, width, piece):
        cols = slice(c, c + piece)
        d_mixed = mm(d_attn[...], attn_low[3, cols, :], NT) * inverse[:, cols]
        d_num[:, cols] = d_mixed.astype(bf16)
        d_den[:, cols] = (d_mixed * mixed_low[:, cols].astype(f32)).astype(bf16)
    mix_heads(
        0, d_num, d_den, query_feat, key_feat, value_low, query_slope, key_slope, weights_t, mask, mask_t, d_query,
        d_key, d_value,
    )


def mix_first(blocks, attn_low, mixed_low, inverse, feats):
    local, width = blocks[0].shape
    tokens = mixed_low.shape[0]
    return pl.pallas_call(
        functools.partial(mix_first_kernel, local),
        out_shape=[near((tokens, width), bf16)] * 3 + [near((tokens, width // 2), bf16)] * 3,
        compiler_params=params(16),
        cost_estimate=pl.CostEstimate(flops=6_000_000_000, bytes_accessed=18_000_000, transcendentals=0),
        name="mix_first",
    )(in_vmem(blocks[0]), *blocks[1:], *all_vmem((attn_low, mixed_low, inverse, *feats)))


def mix_second_kernel(
    d_attn,
    d_num,
    d_den,
    first_query,
    first_key,
    first_value,
    attn_low,
    query_feat,
    key_feat,
    value_low,
    query_slope,
    key_slope,
    weights_t,
    mask,
    mask_t,
    x_slice,
    mixed_slice,
    sums,
    d_query,
    d_key,
    d_value,
    vec,
    keep,
    send,
    attn_grad,
):
    width = d_attn.shape[1]
    own_width = x_slice.shape[0]
    half = width // 2
    for source, target in ((first_query, d_query), (first_key, d_key), (first_value, d_value)):
        target[:, 0:half] = source[...]
    mix_heads(
        half, d_num, d_den, query_feat, key_feat, value_low, query_slope, key_slope, weights_t, mask, mask_t,
        d_query.at[:, half:width], d_key.at[:, half:width], d_value.at[:, half:width],
    )
    for k, grad in enumerate((d_query, d_key, d_value)):
        attn_grad[k * own_width : (k + 1) * own_width, :] = mm(x_slice[...], grad[...])
    attn_grad[3 * own_width : 4 * own_width, :] = mm(mixed_slice[...], d_attn[...])
    write_halves(attn_grad, keep, send)
    held, packed = two_parts(sums[0:4, :])
    send[2 * own_width :, :] = packed
    vec[0:4, :] = held
    vec[4:8, :] = jnp.zeros_like(held)


def mix_second(first, attn_low, feats, x_slice, mixed_slice, sums):
    tokens, width = first[0].shape
    own_width = x_slice.shape[0]
    return pl.pallas_call(
        mix_second_kernel,
        out_shape=[near((tokens, width), bf16)] * 3
        + [
            near((8, width), f32),
            near((2 * own_width, width), f32),
            near((2 * own_width + VEC_ROWS, width), bf16),
        ],
        scratch_shapes=[pltpu.VMEM((4 * own_width, width), f32)],
        compiler_params=params(16),
        cost_estimate=pl.CostEstimate(flops=6_000_000_000, bytes_accessed=18_000_000, transcendentals=0),
        name="mix_second",
    )(*all_vmem((*first, attn_low, *feats, x_slice, mixed_slice, sums)))


def tokens_back_kernel(
    d_query, d_key, d_value, attn_low, d_resid, attn_weight, up_weight, down_weight, tokens_grad, own_attn, own_up, own_down,
    sems,
):
    local, own_width = d_resid.shape[0], own_attn.shape[1]
    rank = lax.axis_index("mp")
    columns = pl.ds(pl.multiple_of(rank * own_width, own_width), own_width)
    copies = [
        pltpu.make_async_copy(attn_weight.at[:, columns, :], own_attn, sems.at[0]),
        pltpu.make_async_copy(up_weight, own_up, sems.at[1]),
        pltpu.make_async_copy(down_weight, own_down, sems.at[2]),
    ]
    for copy in copies:
        copy.start()
    mine = pl.ds(pl.multiple_of(rank * local, local), local)
    tokens_grad[...] = (
        d_resid[...]
        + mm(d_query[mine, :], attn_low[0], NT)
        + mm(d_key[mine, :], attn_low[1], NT)
        + mm(d_value[mine, :], attn_low[2], NT)
    )
    for copy in copies:
        copy.wait()


def tokens_back(d_query, d_key, d_value, attn_low, d_resid, attn_weight, up_weight, down_weight, own_width):
    return pl.pallas_call(
        tokens_back_kernel,
        in_specs=[pl.BlockSpec(memory_space=pltpu.VMEM)] * 5 + [pl.BlockSpec(memory_space=pl.ANY)] * 3,
        out_shape=[
            sds(d_resid.shape, f32),
            near((4, own_width, d_resid.shape[1]), f32),
            near(up_weight.shape, f32),
            near(down_weight.shape, f32),
        ],
        scratch_shapes=[pltpu.SemaphoreType.DMA((3,))],
        compiler_params=params(16),
        cost_estimate=NO_COST,
        name="tokens_back",
    )(
        *all_vmem((d_query, d_key, d_value, attn_low, d_resid)), in_hbm(attn_weight), in_hbm(up_weight),
        in_hbm(down_weight),
    )


def as_row(column):
    return jnp.transpose(jnp.broadcast_to(column, (column.shape[0], 128)))[0:1, :]


def as_column(row):
    return jnp.transpose(jnp.broadcast_to(row, (128, row.shape[1])))[:, 0:1]


SHARE_ROWS = 32


def lane_scalars(values, width):
    lane = lax.broadcasted_iota(jnp.int32, (1, width), 1)
    row = jnp.zeros((1, width), f32)
    for k, value in enumerate(values):
        row = jnp.where(lane == k, value, row)
    return row


def lane_scalar(row, k):
    lane = lax.broadcasted_iota(jnp.int32, row.shape, 1)
    return jnp.sum(jnp.where(lane == k, row, 0.0), axis=1, keepdims=True)


def attn_stats_kernel(even, odd, vec, stats, feed_shares, total, rows_new, shares, columns, rows16):
    own_width, width = total.shape[0] // 4, total.shape[1]
    mine = pl.ds(pl.multiple_of(lax.axis_index("mp") * own_width, own_width), own_width)
    read_halves(even, odd, total)
    scalars = []
    for k in range(4):
        grad = total[k * own_width : (k + 1) * own_width, :]
        square = grad * grad
        columns[...] = as_column(stats[k, 0:1, :])
        rows = decay * columns[mine, :] + (1.0 - decay) * jnp.mean(square + tiny_square, axis=1, keepdims=True)
        rows_new[k : k + 1, :] = as_row(rows)
        rows16[k : k + 1, :] = jnp.sum(square + tiny_square, axis=0, keepdims=True)
        rows16[4 + k : 5 + k, :] = jnp.sum(square * (1.0 / rows), axis=0, keepdims=True)
        scalars.append(jnp.sum(rows, axis=0, keepdims=True))
    rows16[8:12, :] = vec[0:4, :]
    rows16[12:16, :] = feed_shares[0:4, :]
    shares[0:16, :] = rows16[...].astype(bf16)
    row = lane_scalars(scalars, width) + feed_shares[4:5, :]
    high = row.astype(bf16).astype(f32)
    low = (row - high).astype(bf16).astype(f32)
    shares[16:, :] = jnp.concatenate([high, low, jnp.zeros((SHARE_ROWS - 18, width), f32)], axis=0).astype(bf16)


def attn_stats_call(even, odd, vec, stats, feed_shares, own_width):
    width = even.shape[1]
    return pl.pallas_call(
        attn_stats_kernel,
        out_shape=[near((4 * own_width, width), f32), near((4, own_width), f32), near((SHARE_ROWS, width), bf16)],
        scratch_shapes=[pltpu.VMEM((width, 1), f32), pltpu.VMEM((16, width), f32)],
        compiler_params=params(16),
        name="attn_stats",
    )(in_vmem(even), odd, in_vmem(vec), stats, in_vmem(feed_shares))


def attn_out_kernel(total, rows, grad_out, rows_out):
    own_width = grad_out.shape[1]
    for k in range(4):
        grad_out[k] = total[k * own_width : (k + 1) * own_width, :]
    rows_out[...] = rows[...]


def attn_out(total, rows):
    own_width, width = rows.shape[1], total.shape[1]
    return pl.pallas_call(
        attn_out_kernel,
        out_shape=[sds((4, own_width, width), f32), sds((4, own_width), f32)],
        compiler_params=params(8),
        cost_estimate=NO_COST,
        name="attn_out",
    )(*all_vmem((total, rows)))


def feed_stats_kernel(mine, other, wide_old, squares, up_grad_out, down_grad_out, wide_out, grads, wide_new, shares):
    width, hidden = up_grad_out.shape
    for part, rows in enumerate((width, hidden)):
        half = slice(part * width // 2, (part * width + rows) // 2)
        read_halves(mine.at[half], other.at[half], grads.at[part * width : part * width + rows])
    grad = grads[0:width, :]
    up_grad_out[...] = grad
    square = grad * grad
    columns = decay * wide_old[0:1, :] + (1.0 - decay) * jnp.mean(square + tiny_square, axis=0, keepdims=True)
    wide_new[0:1, :] = columns
    shares[0:1, :] = as_row(jnp.sum(square + tiny_square, axis=1, keepdims=True))
    shares[1:2, :] = as_row(jnp.sum(square * (1.0 / columns), axis=1, keepdims=True))
    grad = grads[width:, :]
    down_grad_out[...] = grad
    square = grad * grad
    rows = decay * as_column(wide_old[1:2, :]) + (1.0 - decay) * jnp.mean(
        square + tiny_square, axis=1, keepdims=True
    )
    wide_new[1:2, :] = as_row(rows)
    wide_out[...] = wide_new[...]
    shares[2:3, :] = jnp.sum(square + tiny_square, axis=0, keepdims=True)
    shares[3:4, :] = jnp.sum(square * (1.0 / rows), axis=0, keepdims=True)
    scalars = [jnp.sum(rows, axis=0, keepdims=True)]
    for k in range(2):
        scalars.append(jnp.sum(squares[4 + k : 5 + k, :], axis=1, keepdims=True))
    shares[4:5, :] = lane_scalars([0.0] * 4 + scalars, width)
    shares[5:8, :] = jnp.zeros((3, width), f32)


def feed_stats(even, odd, wide_old, squares):
    width, hidden = squares.shape[1], wide_old.shape[1]
    return pl.pallas_call(
        feed_stats_kernel,
        out_shape=[
            sds((width, hidden), f32),
            sds((hidden, width), f32),
            sds((2, hidden), f32),
            near((width + hidden, width), f32),
            near((2, hidden), f32),
            near((8, width), f32),
        ],
        compiler_params=params(16),
        cost_estimate=NO_COST,
        name="feed_stats",
    )(in_vmem(even), odd, wide_old, in_vmem(squares))


def update_kernel(
    hidden_all,
    attn_grad,
    attn_weight,
    attn_rows,
    stats,
    feed_grad,
    up_weight,
    down_weight,
    wide_new,
    narrow_old,
    squares,
    share,
    share1,
    share2,
    share3,
    vec,
    vec_moment,
    *refs,
):
    outs, made, sems = refs[0:11], refs[11:22], refs[22]
    attn_new, attn_new_low, up_new, up_new_low, down_new, down_new_low = made[0:6]
    attn_cols, narrow_new, vec_grad, vec_moment_new, vec_new = made[6:11]
    width = narrow_old.shape[1]
    own_width = attn_rows.shape[1]
    copies = []

    def leave(which, *place):
        source = made[which].at[place] if place else made[which]
        target = outs[which].at[place] if place else outs[which]
        copy = pltpu.make_async_copy(source, target, sems.at[len(copies)])
        copy.start()
        copies.append(copy)

    total = (share[...].astype(f32) + share1[...].astype(f32)) + (share2[...].astype(f32) + share3[...].astype(f32))
    scalars = total[16:17, :] + total[17:18, :]
    entries = float(width * hidden_all)
    rows = decay * narrow_old[0:1, :] + (1.0 - decay) * total[12:13, :] / hidden_all
    narrow_new[0:1, :] = rows
    cols = decay * narrow_old[1:2, :] + (1.0 - decay) * total[14:15, :] / hidden_all
    narrow_new[1:2, :] = cols
    mean_up = jnp.mean(rows, axis=1, keepdims=True)
    mean_down = lane_scalar(scalars, 4) / hidden_all

    def step_size(scaled, weight_square, count):
        clip = jnp.maximum(1.0, jnp.sqrt(scaled / count) / clip_limit)
        return learn_rate * jnp.sqrt(weight_square / count) / clip

    up_size = step_size(
        jnp.sum(total[13:14, :] / rows, axis=1, keepdims=True) * mean_up, lane_scalar(scalars, 5), entries
    )
    down_size = step_size(
        jnp.sum(total[15:16, :] / cols, axis=1, keepdims=True) * mean_down, lane_scalar(scalars, 6), entries
    )

    def block(which, here, grad, weight, row, col, mean, size):
        scale = row * col * (1.0 / mean)
        value = weight - size * (grad * lax.rsqrt(scale))
        made[which][here] = value
        made[which + 1][here] = value.astype(bf16)
        leave(which, *here)
        leave(which + 1, *here)

    pieces = 4
    row = as_column(rows)
    step = up_weight.shape[0] // pieces
    for n in range(pieces):
        here = slice(n * step, (n + 1) * step)
        block(2, (here, slice(None)), feed_grad[here, :], up_weight[here, :], row[here], wide_new[0:1, :], mean_up, up_size)
    row = as_column(wide_new[1:2, :])
    step = down_weight.shape[0] // pieces
    for n in range(pieces):
        here = slice(n * step, (n + 1) * step)
        below = slice(up_weight.shape[0] + n * step, up_weight.shape[0] + (n + 1) * step)
        block(4, (here, slice(None)), feed_grad[below, :], down_weight[here, :], row[here], cols, mean_down, down_size)
    leave(7)
    entries = float(width * width)
    for k in range(4):
        col = decay * stats[k, 1:2, :] + (1.0 - decay) * total[k : k + 1, :] / width
        attn_cols[k : k + 1, :] = col
        mean = lane_scalar(scalars, k) / width
        size = step_size(
            jnp.sum(total[4 + k : 5 + k, :] / col, axis=1, keepdims=True) * mean,
            jnp.sum(squares[k : k + 1, :], axis=1, keepdims=True),
            entries,
        )
        block(
            0, (k,), attn_grad[k * own_width : (k + 1) * own_width, :], attn_weight[k], as_column(attn_rows[k : k + 1, :]),
            col, mean, size,
        )
    leave(6)
    grads = total[8:12, :]
    vec_grad[...] = grads
    leave(8)
    moment = decay * vec_moment[...] + (1.0 - decay) * (grads * grads + tiny_square)
    vec_moment_new[...] = moment
    leave(9)
    scaled = grads * lax.rsqrt(moment)
    clip = jnp.maximum(1.0, jnp.sqrt(jnp.mean(scaled * scaled, axis=1, keepdims=True)) / clip_limit)
    held = vec[...]
    spread = jnp.sqrt(jnp.mean(held * held, axis=1, keepdims=True))
    vec_new[...] = held - learn_rate * spread * scaled / clip
    leave(10)
    for copy in copies:
        copy.wait()


def update(
    attn_grad, attn_weight, attn_rows, stats, feed_grad, up_weight, down_weight, wide_new, narrow_old, squares, shares,
    vec, vec_moment, hidden_all,
):
    _, own_width, width = attn_weight.shape
    hidden = up_weight.shape[1]
    outs = [((4, own_width, width), t) for t in (f32, bf16)]
    outs += [((width, hidden), t) for t in (f32, bf16)] + [((hidden, width), t) for t in (f32, bf16)]
    outs += [((4, width), f32), ((2, width), f32)] + [((4, width), f32)] * 3
    return pl.pallas_call(
        functools.partial(update_kernel, hidden_all),
        in_specs=[pl.BlockSpec(memory_space=pltpu.VMEM)] * 16,
        out_specs=[pl.BlockSpec(memory_space=pl.ANY)] * 11,
        out_shape=[pltpu.HBM(*out) for out in outs],
        scratch_shapes=[pltpu.VMEM(*out) for out in outs]
        + [pltpu.SemaphoreType.DMA((29,))],
        compiler_params=params(24),
        name="update",
    )(
        *all_vmem((attn_grad, attn_weight, attn_rows)), stats,
        *all_vmem((feed_grad, up_weight, down_weight, wide_new)), narrow_old, in_vmem(squares), in_vmem(shares[0]),
        *shares[1:], vec, vec_moment,
    )


def exchange(parts, steps):
    ranks = len(parts)
    moved = [
        lax.ppermute(part, "mp", [(i, target(i, step, ranks)) for i in range(ranks)])
        for part, step in zip(parts[1:], steps[1:])
    ]
    return [parts[0]] + moved


def on_device(
    tokens,
    cotangent,
    seq_starts,
    attn_weight,
    up_weight,
    down_weight,
    vec_params,
    attn_stats,
    ffn_narrow_stats,
    ffn_wide_stats,
    vec_moment,
):
    ranks = lax.axis_size("mp")
    local, width = tokens.shape
    own_width = width // ranks
    hidden_all = up_weight.shape[1] * ranks

    blocks = exchange([tokens] * ranks, TOKEN_STEPS)
    attn_low, up_low, down_low, mask, mask_t, squares = prepare(
        seq_starts, attn_weight, up_weight, down_weight, local * ranks
    )
    (
        x_all,
        query_feat,
        key_feat,
        value_low,
        mixed_low,
        inverse,
        own_sum,
        own_first,
        first_low,
        pre_act,
        hidden_low,
        *parts,
    ) = forward(blocks, attn_low, up_low, down_low, mask, vec_params)
    parts = exchange(parts, BRANCH_STEPS)
    weights_t, query_slope, key_slope, slope = slopes(query_feat, key_feat, mask_t, pre_act)
    own_first, slope = lax.optimization_barrier((own_first, slope))
    feats = (query_feat, key_feat, value_low, query_slope, key_slope, weights_t, mask, mask_t)
    mixing = (attn_low, mixed_low, inverse, *feats)
    feeding = (up_low, down_low, first_low, slope, hidden_low)
    block_near, d_second, sums, *d_branch = middle(
        parts, own_first, cotangent, vec_params, (*mixing, *feeding, own_sum, x_all)
    )
    turned_from, d_second = lax.optimization_barrier((x_all, d_second))
    x_slice, mixed_slice, block_out = own_columns(turned_from, mixed_low, block_near, own_width)
    slope, x_slice = lax.optimization_barrier((slope, x_slice))
    d_branch, d_pre, *parts = feed_back(
        exchange(d_branch, BACK_STEPS), slope, up_low, down_low, (*mixing, first_low, hidden_low, own_sum, d_second, sums, x_slice, mixed_slice)
    )
    staged = lax.axis_size("dp") == STAGED

    parts = exchange(parts, FIRST_STEPS)
    *feed_keep, up_send, down_send = feed_grads(first_low, d_pre, hidden_low, d_branch)
    if staged:
        up = fold_first(feed_keep[0], across(up_send, 1))
        down = fold_first(feed_keep[1], across(down_send, 1))
        parts[0], up, down = lax.optimization_barrier((parts[0], up, down))
        got_up, got_down = [[across(a, 2), across(b, 4)] for a, b in (up, down)]
    d_resid, sums, *d_attn = first_back(
        parts, d_second, own_sum, sums, vec_params, (*mixing, x_slice, mixed_slice)
    )
    blocks = exchange(d_attn, MIX_STEPS)
    if staged:
        d_resid, up, down = lax.optimization_barrier((d_resid, up, down))
        feed_a, feed_b = fold_feed((*up, *down), (*got_up, *got_down))
        blocks[0], feed_a, feed_b = lax.optimization_barrier((blocks[0], feed_a, feed_b))
        got_a, got_b = across(feed_a, 4), across(feed_b, 2)
    first = mix_first(blocks, attn_low, mixed_low, inverse, feats)
    *d_mix, vec_part, attn_keep, attn_send = mix_second(first, attn_low, feats, x_slice, mixed_slice, sums)
    if staged:
        feed_even = fold_feed_last(feed_a, got_a, feed_b, got_b)
        attn_send, feed_even = lax.optimization_barrier((attn_send, feed_even))
        received = across(attn_send, 1)
        feed_odd = across(feed_even, 1)
        vec_part, attn_a, attn_b = fold_first(attn_keep, received, vec_part)
        got_a, got_b = across(attn_a, 2), across(attn_b, 4)
    else:
        feed_even, feed_odd, attn_even, attn_odd, vec_part = lax.psum(
            (jnp.concatenate(feed_keep), jnp.concatenate([up_send, down_send]).astype(f32), attn_keep, attn_send[: 2 * own_width].astype(f32), vec_part), "dp"
        )
    up_grad, down_grad, wide_out, feed_near, wide_near, feed_shares = feed_stats(
        feed_even, feed_odd, ffn_wide_stats, squares
    )
    tokens_grad, own_attn, own_up, own_down = tokens_back(
        *d_mix, attn_low, d_resid, attn_weight, up_weight, down_weight, own_width
    )
    if staged:
        attn_a, feed_shares = lax.optimization_barrier((attn_a, feed_shares))
        vec_part, attn_a, attn_b = fold_second(attn_a, got_a, attn_b, got_b, vec_part)
        got_a, got_b = across(attn_a, 4), across(attn_b, 2)
        attn_a, tokens_grad = lax.optimization_barrier((attn_a, tokens_grad))
        vec_part, attn_even = fold_last(attn_a, got_a, attn_b, got_b, vec_part)
        attn_odd = across(attn_even, 1)
    attn_near, rows_near, shares = attn_stats_call(attn_even, attn_odd, vec_part, attn_stats, feed_shares, own_width)
    shares = exchange([shares] * ranks, SHARE_STEPS)
    attn_grad, attn_rows = attn_out(attn_near, rows_near)
    attn_near, attn_grad = lax.optimization_barrier((attn_near, attn_grad))
    (
        attn_new,
        attn_new_low,
        up_new,
        up_new_low,
        down_new,
        down_new_low,
        attn_cols,
        narrow_new,
        vec_grad,
        vec_moment_new,
        vec_new,
    ) = update(
        attn_near, own_attn, rows_near, attn_stats, feed_near, own_up, own_down, wide_near, ffn_narrow_stats,
        squares, shares, vec_params, vec_moment, hidden_all,
    )
    return (
        block_out,
        tokens_grad,
        attn_grad,
        attn_rows,
        attn_cols,
        attn_new,
        attn_new_low,
        up_grad,
        down_grad,
        narrow_new,
        wide_out,
        up_new,
        down_new,
        up_new_low,
        down_new_low,
        vec_grad,
        vec_moment_new,
        vec_new,
    )


def solution(mesh):
    in_specs = (
        P(("dp", "mp"), None),
        P(("dp", "mp"), None),
        P("dp", None),
        P(),
        P(None, "mp"),
        P("mp", None),
        P(),
        P(),
        P(),
        P(None, "mp"),
        P(),
    )
    out_specs = (
        P(("dp", "mp"), None),
        P(("dp", "mp"), None),
        P(None, "mp", None),
        P(None, "mp"),
        P(),
        P(None, "mp", None),
        P(None, "mp", None),
        P(None, "mp"),
        P("mp", None),
        P(),
        P(None, "mp"),
        P(None, "mp"),
        P("mp", None),
        P(None, "mp"),
        P("mp", None),
        P(),
        P(),
        P(),
    )
    return jax.shard_map(
        on_device, mesh=mesh, in_specs=in_specs, out_specs=out_specs, check_vma=False
    )
```

```python
import functools
import math

import jax
import jax.numpy as jnp
from jax import lax
from jax.experimental import pallas as pl
from jax.experimental.pallas import tpu as pltpu
from jax.sharding import PartitionSpec as P

HEADS = 12
STEP = 10

norm_eps = 1e-05
tiny_square = 1e-30
learn_rate = 0.3
clip_limit = 1.0
decay = 1.0 - float(STEP) ** (-0.8)

f32 = jnp.float32
bf16 = jnp.bfloat16

NN = (((1,), (0,)), ((), ()))
NT = (((1,), (1,)), ((), ()))
TN = (((0,), (0,)), ((), ()))


def mm(a, b, dims=NN):
    return lax.dot_general(a, b, dims, preferred_element_type=f32)


def params(mib):
    return pltpu.CompilerParams(vmem_limit_bytes=mib * 1024 * 1024)


def sds(shape, dtype):
    return jax.ShapeDtypeStruct(shape, dtype)


def in_hbm(array):
    return pltpu.with_memory_space_constraint(array, pltpu.HBM)


def in_vmem(array):
    return pltpu.with_memory_space_constraint(array, pltpu.VMEM)


def all_vmem(arrays):
    return [in_vmem(array) for array in arrays]


def near(shape, dtype):
    return pltpu.VMEM(shape, dtype)


NO_COST = pl.CostEstimate(flops=0, bytes_accessed=0, transcendentals=0)


def holding(kernel, count, held):
    def body(*refs):
        for ref in refs[count : count + held]:
            pltpu.touch(ref)
        kernel(*refs[:count], *refs[count + held :])

    return body


STAGED = 8
VEC_ROWS = 16
TOKEN_STEPS = (0, -2, -1, -3)
BRANCH_STEPS = (0, 1, 2, 3)
BACK_STEPS = (0, 2, 1, 3)
FIRST_STEPS = (0, 1, 2, 3)
MIX_STEPS = (0, 2, 1, 3)
SHARE_STEPS = (0, -1, -2, -3)


def target(rank, step, ranks):
    return rank ^ -step if step <= 0 else (rank + step) % ranks


def source(rank, step, ranks):
    return rank ^ -step if step <= 0 else (rank + ranks - step) % ranks


def rank_rows(rank, rows):
    return pl.ds(pl.multiple_of(rank * rows, rows), rows)


def half_rows(count, mine):
    rows = count // 2
    side = lax.rem(lax.axis_index("dp"), 2) if lax.axis_size("dp") == STAGED else 0
    return pl.ds(pl.multiple_of((side if mine else 1 - side) * rows, rows), rows)


def write_halves(total, keep, send):
    rows = total.shape[0] // 2
    keep[...] = total[half_rows(total.shape[0], True), :]
    send[0:rows, :] = total[half_rows(total.shape[0], False), :].astype(send.dtype)


def read_halves(mine, other, total):
    total[half_rows(total.shape[0], True), :] = mine[...].astype(total.dtype)
    total[half_rows(total.shape[0], False), :] = other[...].astype(total.dtype)


def two_parts(values):
    high = values.astype(bf16).astype(f32)
    low = (values - high).astype(bf16).astype(f32)
    both = jnp.concatenate([high, low], axis=0)
    return high + low, jnp.concatenate([both, jnp.zeros_like(both)], axis=0).astype(bf16)


def joined(block):
    block = block.astype(f32)
    return block[0:4, :] + block[4:8, :]


def add_vec(vec, block, vec_out, send=None):
    held, packed = two_parts(vec[0:4, :] + joined(block))
    vec_out[0:4, :] = held
    vec_out[4:8, :] = jnp.zeros_like(held)
    if send is not None:
        send[...] = packed


def fold_first_kernel(keep, received, *refs):
    send_a, send_b = refs[-2:]
    rows = keep.shape[0] // 2
    send_a[0:rows, :] = (keep[0:rows, :] + received[0:rows, :].astype(f32)).astype(bf16)
    send_b[...] = (keep[rows : 2 * rows, :] + received[rows : 2 * rows, :].astype(f32)).astype(bf16)
    if len(refs) > 2:
        add_vec(refs[0], received[2 * rows :, :], refs[1], send_a.at[rows:, :])


def fold_second_kernel(own_a, got_a, own_b, got_b, *refs):
    send_a, send_b = refs[-2:]
    rows = own_b.shape[0]
    send_a[0:rows, :] = (own_a[0:rows, :].astype(f32) + got_a[0:rows, :].astype(f32)).astype(bf16)
    send_b[...] = (own_b[...].astype(f32) + got_b[...].astype(f32)).astype(bf16)
    if len(refs) > 2:
        add_vec(refs[0], got_a[rows:, :], refs[1], send_a.at[rows:, :])


def fold_last_kernel(own_a, got_a, own_b, got_b, *refs):
    total = refs[-1]
    rows = own_b.shape[0]
    total[0:rows, :] = (own_a[0:rows, :].astype(f32) + got_a[0:rows, :].astype(f32)).astype(bf16)
    total[rows:, :] = (own_b[...].astype(f32) + got_b[...].astype(f32)).astype(bf16)
    if len(refs) > 1:
        add_vec(refs[0], got_a[rows:, :], refs[1])


def fold_call(kernel, name, inputs, vec, outs):
    width = inputs[0].shape[1]
    extra_in, extra_out = ([in_vmem(vec)], [near((8, width), f32)]) if vec is not None else ([], [])
    return pl.pallas_call(
        kernel,
        out_shape=extra_out + [near((rows, width), bf16) for rows in outs],
        compiler_params=params(8),
        cost_estimate=NO_COST,
        name=name,
    )(in_vmem(inputs[0]), *inputs[1:], *extra_in)


def fold_first(keep, received, vec=None):
    rows = keep.shape[0] // 2
    return fold_call(
        fold_first_kernel, "fold_first", (keep, received), vec, (rows if vec is None else rows + VEC_ROWS, rows)
    )


def fold_second(own_a, got_a, own_b, got_b, vec=None):
    return fold_call(
        fold_second_kernel, "fold_second", (own_a, got_a, own_b, got_b), vec, (own_a.shape[0], own_b.shape[0])
    )


def fold_last(own_a, got_a, own_b, got_b, vec=None):
    return fold_call(fold_last_kernel, "fold_last", (own_a, got_a, own_b, got_b), vec, (2 * own_b.shape[0],))


def fold_feed_kernel(*refs):
    own, got, (send_a, send_b) = refs[0:4], refs[4:8], refs[8:]
    rows = own[0].shape[0]
    for n, (block, other) in enumerate(zip(own, got)):
        send = (send_a, send_b)[n % 2]
        place = n // 2 * rows
        send[place : place + rows, :] = (block[...].astype(f32) + other[...].astype(f32)).astype(bf16)


def fold_feed(own, got):
    rows, width = own[0].shape
    return pl.pallas_call(
        fold_feed_kernel,
        out_shape=[near((2 * rows, width), bf16)] * 2,
        compiler_params=params(8),
        cost_estimate=NO_COST,
        name="fold_feed",
    )(*all_vmem(own), *got)


def fold_feed_last_kernel(own_a, got_a, own_b, got_b, total):
    rows = own_a.shape[0] // 2
    for n, (block, other) in enumerate(((own_a, got_a), (own_b, got_b))):
        for part in range(2):
            here = slice(part * rows, (part + 1) * rows)
            place = (2 * part + n) * rows
            total[place : place + rows, :] = (block[here, :].astype(f32) + other[here, :].astype(f32)).astype(bf16)


def fold_feed_last(own_a, got_a, own_b, got_b):
    rows, width = own_a.shape
    return pl.pallas_call(
        fold_feed_last_kernel,
        out_shape=near((2 * rows, width), bf16),
        compiler_params=params(8),
        cost_estimate=NO_COST,
        name="fold_feed_last",
    )(in_vmem(own_a), got_a, in_vmem(own_b), got_b)


def across(block, bit):
    return lax.ppermute(block, "dp", [(i, i ^ bit) for i in range(STAGED)])


def prepare_kernel(seqs, tokens_pack, starts, attn, up, down, attn_low, up_low, down_low, mask, mask_t, squares):
    step = pl.program_id(0)

    @pl.when(step == 0)
    def _():
        squares[...] = jnp.zeros_like(squares)

    for k in range(4):
        block = attn[k]
        attn_low[k] = block.astype(bf16)
        squares[k : k + 1, :] += jnp.sum(block * block, axis=0, keepdims=True)
    for k, (source, target) in enumerate(((up, up_low), (down, down_low))):
        block = source[...]
        target[...] = block.astype(bf16)
        squares[4 + k : 5 + k, :] += jnp.sum(block * block, axis=0, keepdims=True)

    def layout(index):
        seq = jnp.zeros_like(index)
        begin = jnp.zeros_like(index)
        length = jnp.ones_like(index)
        for s in range(seqs):
            start = starts[0, s]
            finish = starts[0, s + 1] if s + 1 < seqs else tokens_pack
            inside = index >= start
            seq = jnp.where(inside, s, seq)
            begin = jnp.where(inside, start, begin)
            length = jnp.where(inside, finish - start, length)
        angle = 0.5 * math.pi * (index - begin).astype(f32) / length.astype(f32)
        return seq, jnp.cos(angle), jnp.sin(angle)

    rows = mask.shape[0]
    row = lax.broadcasted_iota(jnp.int32, (rows, 128), 0) + step * rows
    col = lax.broadcasted_iota(jnp.int32, (8, tokens_pack), 1)
    row_seq, row_cos, row_sin = (a[:, 0:1] for a in layout(row))
    col_seq, col_cos, col_sin = (a[0:1, :] for a in layout(col))
    same = row_seq == col_seq
    value = row_cos * col_cos + row_sin * col_sin
    row, col = row[:, 0:1], col[0:1, :]
    mask[...] = jnp.where(same & (col <= row), value, 0.0)
    mask_t[...] = jnp.where(same & (row <= col), value, 0.0)


def prepare(seq_starts, attn_weight, up_weight, down_weight, tokens_pack):
    steps = 8
    seqs = seq_starts.shape[1]
    heads4, width, _ = attn_weight.shape
    hidden = up_weight.shape[1]
    a_rows, u_rows, d_rows, m_rows = width // steps, width // steps, hidden // steps, tokens_pack // steps
    return pl.pallas_call(
        functools.partial(prepare_kernel, seqs, tokens_pack),
        grid=(steps,),
        in_specs=[
            pl.BlockSpec(memory_space=pltpu.SMEM),
            pl.BlockSpec((4, a_rows, width), lambda i: (0, i, 0)),
            pl.BlockSpec((u_rows, hidden), lambda i: (i, 0)),
            pl.BlockSpec((d_rows, width), lambda i: (i, 0)),
        ],
        out_specs=[
            pl.BlockSpec((4, a_rows, width), lambda i: (0, i, 0)),
            pl.BlockSpec((u_rows, hidden), lambda i: (i, 0)),
            pl.BlockSpec((d_rows, width), lambda i: (i, 0)),
            pl.BlockSpec((m_rows, tokens_pack), lambda i: (i, 0)),
            pl.BlockSpec((m_rows, tokens_pack), lambda i: (i, 0)),
            pl.BlockSpec((8, width), lambda i: (0, 0)),
        ],
        out_shape=[
            near((4, width, width), bf16),
            near((width, hidden), bf16),
            near((hidden, width), bf16),
            near((tokens_pack, tokens_pack), f32),
            near((tokens_pack, tokens_pack), f32),
            near((8, width), f32),
        ],
        compiler_params=params(24),
        cost_estimate=pl.CostEstimate(flops=10_000_000, bytes_accessed=22_000_000, transcendentals=0),
        name="prepare",
    )(seq_starts, in_hbm(attn_weight), in_hbm(up_weight), in_hbm(down_weight))


def half_lanes(width):
    return lax.broadcasted_iota(jnp.int32, (1, width), 1) < width // 2


def norm_parts(values):
    centered = values - jnp.mean(values, axis=-1, keepdims=True)
    spread = lax.rsqrt(jnp.mean(centered * centered, axis=-1, keepdims=True) + norm_eps)
    return centered * spread, spread


def norm_back(grad, unit, spread, gain):
    scaled = grad * gain
    return spread * (
        scaled
        - jnp.mean(scaled, axis=-1, keepdims=True)
        - unit * jnp.mean(scaled * unit, axis=-1, keepdims=True)
    )


def causal_blocks(tokens, size):
    return [(i, min(size, tokens - i)) for i in range(0, tokens, size)]


def forward_kernel(
    local,
    x0,
    x1,
    x2,
    x3,
    attn_low,
    up_low,
    down_low,
    mask,
    vec,
    x_all,
    query_feat,
    key_feat,
    value_low,
    mixed_low,
    inverse,
    own_sum,
    own_first,
    first_low,
    pre_act,
    hidden_low,
    part0,
    part1,
    part2,
    part3,
    branch,
):
    rank = lax.axis_index("mp")
    tokens, width = x_all.shape
    ranks = tokens // local

    for step, block in zip(TOKEN_STEPS, (x0, x1, x2, x3)):
        x_all[rank_rows(source(rank, step, ranks), local), :] = block[...]

    piece = 256
    for c in range(0, width, piece):
        cols = slice(c, c + piece)
        for which, feat in ((0, query_feat), (1, key_feat)):
            raw = mm(x_all[...], attn_low[which, :, cols])
            feat[:, cols] = jax.nn.softplus(raw).astype(bf16)
        value_low[:, cols] = mm(x_all[...], attn_low[2, :, cols]).astype(bf16)

    pair = 2 * (width // HEADS)
    first_half = half_lanes(pair)
    for c in range(0, width, pair):
        cols = slice(c, c + pair)
        keys = key_feat[:, cols]
        values = value_low[:, cols]
        zero = jnp.zeros_like(keys)
        one = jnp.ones_like(values)
        sides = (first_half, ~first_half)
        own_keys = [jnp.where(own, keys, zero) for own in sides]
        own_values = [
            jnp.concatenate([jnp.where(own, values, zero), jnp.where(own, one, zero)], axis=1) for own in sides
        ]
        for i, rows in causal_blocks(tokens, 256):
            here = slice(i, i + rows)
            upto = i + rows
            queries = query_feat[here, cols]
            allowed = mask[here, :upto]
            scores = mm(queries, jnp.concatenate([block[:upto] for block in own_keys], axis=0), NT)
            weights = (scores * jnp.concatenate([allowed, allowed], axis=1)).astype(bf16)
            both = mm(weights, jnp.concatenate([block[:upto] for block in own_values], axis=0))
            inv = 1.0 / both[:, pair:]
            inverse[here, cols] = inv
            mixed_low[here, cols] = (both[:, :pair] * inv).astype(bf16)

    for i, rows in causal_blocks(tokens, 256):
        here = slice(i, i + rows)
        summed = x_all[here, :].astype(f32) + mm(mixed_low[here, :], attn_low[3])
        branch[here, :] = summed
        unit, _ = norm_parts(summed)
        first_low[here, :] = (unit * vec[0:1, :] + vec[1:2, :]).astype(bf16)
    own_sum[...] = branch[rank_rows(rank, local), :]
    unit, _ = norm_parts(own_sum[...])
    own_first[...] = unit * vec[0:1, :] + vec[1:2, :]

    hidden_count = up_low.shape[1]
    for c in range(0, hidden_count, piece):
        cols = slice(c, c + piece)
        pre = mm(first_low[...], up_low[:, cols])
        cdf = 0.5 * (1.0 + lax.erf(pre * math.sqrt(0.5)))
        hidden_low[:, cols] = (pre * cdf).astype(bf16)
        pre_act[:, cols] = pre

    branch[...] = mm(hidden_low[...], down_low[...])
    for step, part in zip(BRANCH_STEPS, (part0, part1, part2, part3)):
        part[...] = branch[rank_rows(target(rank, step, ranks), local), :].astype(part.dtype)


def forward(blocks, attn_low, up_low, down_low, mask, vec):
    local, width = blocks[0].shape
    tokens = mask.shape[0]
    hidden = up_low.shape[1]
    return pl.pallas_call(
        functools.partial(forward_kernel, local),
        out_shape=[near((tokens, width), bf16)] * 5
        + [near((tokens, width), f32), near((local, width), f32), near((local, width), f32)]
        + [near((tokens, width), bf16), near((tokens, hidden), f32), near((tokens, hidden), bf16)]
        + [near((local, width), f32)]
        + [near((local, width), bf16)] * 3,
        scratch_shapes=[pltpu.VMEM((tokens, width), f32)],
        compiler_params=params(16),
        cost_estimate=pl.CostEstimate(flops=8_000_000_000, bytes_accessed=20_000_000, transcendentals=2_000_000),
        name="forward",
    )(*blocks, *all_vmem((attn_low, up_low, down_low, mask)), vec)


def slopes_kernel(query_feat, key_feat, mask_t, pre_act, weights_t, query_slope, key_slope, slope):
    tokens, width = query_feat.shape
    piece = 256
    for c in range(0, width, piece):
        cols = slice(c, c + piece)
        for feat, grad in ((query_feat, query_slope), (key_feat, key_slope)):
            value = feat[:, cols].astype(f32)
            small = value * (1.0 - value * (0.5 - value * (1.0 / 6.0)))
            grad[:, cols] = jnp.where(value < 0.02, small, 1.0 - jnp.exp(-value)).astype(bf16)
    for c in range(0, pre_act.shape[1], piece):
        cols = slice(c, c + piece)
        pre = pre_act[:, cols]
        cdf = 0.5 * (1.0 + lax.erf(pre * math.sqrt(0.5)))
        slope[:, cols] = cdf + pre * (jnp.exp(-0.5 * pre * pre) * (1.0 / math.sqrt(2.0 * math.pi)))
    pair = 2 * (width // HEADS)
    first_half = half_lanes(pair)
    for head in range(HEADS):
        cols = slice(head // 2 * pair, (head // 2 + 1) * pair)
        own = first_half if head % 2 == 0 else ~first_half
        for i, rows in causal_blocks(tokens, 256):
            here = slice(i, i + rows)
            keys = key_feat[here, cols]
            scores = mm(jnp.where(own, keys, jnp.zeros_like(keys)), query_feat[i:, cols], NT)
            weights_t[head * tokens + i : head * tokens + i + rows, i:] = (scores * mask_t[here, i:]).astype(bf16)


def slopes(query_feat, key_feat, mask_t, pre_act):
    tokens, width = query_feat.shape
    return pl.pallas_call(
        slopes_kernel,
        out_shape=[near((HEADS * tokens, tokens), bf16)]
        + [near((tokens, width), bf16)] * 2
        + [near(pre_act.shape, f32)],
        compiler_params=params(16),
        cost_estimate=NO_COST,
        name="slopes",
    )(*all_vmem((query_feat, key_feat, mask_t, pre_act)))


def middle_kernel(part0, part1, part2, part3, own_first, cotangent, vec, block_out, d_second, sums, *d_branch):
    branch = part0[...] + part1[...].astype(f32) + part2[...].astype(f32) + part3[...].astype(f32)
    unit, spread = norm_parts(own_first[...] + branch)
    gain = vec[2:3, :]
    block_out[...] = unit * gain + vec[3:4, :]
    grad = cotangent[...].astype(f32)
    inner = norm_back(grad, unit, spread, gain)
    d_second[...] = inner
    for copy in d_branch:
        copy[...] = inner.astype(bf16)
    sums[...] = jnp.zeros_like(sums)
    sums[2:3, :] = jnp.sum(grad * unit, axis=0, keepdims=True)
    sums[3:4, :] = jnp.sum(grad, axis=0, keepdims=True)


def middle(parts, own_first, cotangent, vec, held):
    local, width = own_first.shape
    return pl.pallas_call(
        holding(middle_kernel, 7, len(held)),
        out_shape=[near((local, width), f32), near((local, width), f32), near((8, width), f32)]
        + [near((local, width), bf16)] * 4,
        compiler_params=params(8),
        name="middle",
    )(in_vmem(parts[0]), *parts[1:], in_vmem(own_first), cotangent, vec, *all_vmem(held))


def feed_back_kernel(
    local, d0, d1, d2, d3, slope, up_low, down_low, d_branch, d_pre, part0, part1, part2, part3, total
):
    rank = lax.axis_index("mp")
    tokens, width = d_branch.shape
    ranks = tokens // local

    for step, block in zip(BACK_STEPS, (d0, d1, d2, d3)):
        d_branch[rank_rows(source(rank, step, ranks), local), :] = block[...]
    piece = 256
    for c in range(0, d_pre.shape[1], piece):
        cols = slice(c, c + piece)
        d_pre[:, cols] = (mm(d_branch[...], down_low[cols, :], NT) * slope[:, cols]).astype(bf16)
    total[...] = mm(d_pre[...], up_low[...], NT)
    for step, part in zip(FIRST_STEPS, (part0, part1, part2, part3)):
        part[...] = total[rank_rows(target(rank, step, ranks), local), :].astype(part.dtype)


def feed_back(blocks, slope, up_low, down_low, held):
    local, width = blocks[0].shape
    tokens, hidden = slope.shape
    return pl.pallas_call(
        holding(functools.partial(feed_back_kernel, local), 7, len(held)),
        out_shape=[near((tokens, width), bf16), near((tokens, hidden), bf16), near((local, width), f32)]
        + [near((local, width), bf16)] * 3,
        scratch_shapes=[pltpu.VMEM((tokens, width), f32)],
        compiler_params=params(16),
        cost_estimate=pl.CostEstimate(flops=1_200_000_000, bytes_accessed=9_000_000, transcendentals=0),
        name="feed_back",
    )(in_vmem(blocks[0]), *blocks[1:], *all_vmem((slope, up_low, down_low, *held)))


def feed_grads_kernel(first_low, d_pre, hidden_low, d_branch, keep_up, keep_down, send_up, send_down):
    for left, right, keep, send in (
        (first_low, d_pre, keep_up, send_up),
        (hidden_low, d_branch, keep_down, send_down),
    ):
        keep[...] = mm(left[:, half_rows(left.shape[1], True)], right[...], TN)
        send[...] = mm(left[:, half_rows(left.shape[1], False)], right[...], TN).astype(bf16)


def feed_grads(first_low, d_pre, hidden_low, d_branch):
    width, hidden = first_low.shape[1], d_pre.shape[1]
    return pl.pallas_call(
        feed_grads_kernel,
        out_shape=[near((width // 2, hidden), f32), near((hidden // 2, width), f32)]
        + [near((width // 2, hidden), bf16), near((hidden // 2, width), bf16)],
        compiler_params=params(16),
        cost_estimate=NO_COST,
        name="feed_grads",
    )(*all_vmem((first_low, d_pre, hidden_low, d_branch)))


def first_back_kernel(part0, part1, part2, part3, d_second, own_sum, sums_in, vec, d_resid, sums, *d_attn):
    grad = d_second[...] + part0[...] + part1[...].astype(f32) + part2[...].astype(f32) + part3[...].astype(f32)
    unit, spread = norm_parts(own_sum[...])
    inner = norm_back(grad, unit, spread, vec[0:1, :])
    d_resid[...] = inner
    for copy in d_attn:
        copy[...] = inner.astype(bf16)
    sums[...] = sums_in[...]
    sums[0:1, :] = jnp.sum(grad * unit, axis=0, keepdims=True)
    sums[1:2, :] = jnp.sum(grad, axis=0, keepdims=True)


def first_back(parts, d_second, own_sum, sums, vec, held):
    local, width = own_sum.shape
    return pl.pallas_call(
        holding(first_back_kernel, 8, len(held)),
        out_shape=[near((local, width), f32), near((8, width), f32)] + [near((local, width), bf16)] * 4,
        compiler_params=params(8),
        name="first_back",
    )(in_vmem(parts[0]), *parts[1:], *all_vmem((d_second, own_sum, sums)), vec, *all_vmem(held))


def own_columns_kernel(x_all, mixed_low, block_near, x_slice, mixed_slice, block_out, turned):
    block_out[...] = block_near[...]
    rows = x_slice.shape[0]
    mine = pl.ds(pl.multiple_of(lax.axis_index("mp") * rows, rows), rows)
    for source, target in ((x_all, x_slice), (mixed_low, mixed_slice)):
        turned[...] = jnp.transpose(source[...])
        target[...] = turned[mine, :]


def own_columns(x_all, mixed_low, block_near, own_width):
    tokens, width = x_all.shape
    return pl.pallas_call(
        own_columns_kernel,
        out_shape=[near((own_width, tokens), bf16)] * 2 + [sds(block_near.shape, f32)],
        scratch_shapes=[pltpu.VMEM((width, tokens), bf16)],
        compiler_params=params(8),
        cost_estimate=NO_COST,
        name="own_columns",
    )(*all_vmem((x_all, mixed_low, block_near)))


def mix_heads(
    start, d_num, d_den, query_feat, key_feat, value_low, query_slope, key_slope, weights_t, mask, mask_t, d_query, d_key,
    d_value,
):
    tokens, width = query_feat.shape
    pair = 2 * (width // HEADS)
    first_half = half_lanes(pair)
    spans = causal_blocks(tokens, 256)
    for c in range(start, start + width // 2, pair):
        cols = slice(c, c + pair)
        queries = query_feat[:, cols]
        keys = key_feat[:, cols]
        values = value_low[:, cols]
        nums = d_num[:, cols]
        left = jnp.concatenate([nums, d_den[:, cols]], axis=1)
        zero = jnp.zeros_like(keys)
        minus = jnp.full_like(values, -1)
        sides = (first_half, ~first_half)
        own_query = [jnp.where(own, queries, zero) for own in sides]
        own_key = [jnp.where(own, keys, zero) for own in sides]
        own_num = [jnp.where(own, nums, zero) for own in sides]
        right = [
            jnp.concatenate([jnp.where(own, values, zero), jnp.where(own, minus, zero)], axis=1) for own in sides
        ]
        base = 2 * (c // pair) * tokens
        out = slice(c - start, c - start + pair)
        for i, rows in spans:
            here = slice(i, i + rows)
            upto = i + rows
            allowed = mask[here, :upto]
            d_scores = mm(left[here], jnp.concatenate([block[:upto] for block in right], axis=0), NT)
            d_scores = (d_scores * jnp.concatenate([allowed, allowed], axis=1)).astype(bf16)
            grad = mm(d_scores, jnp.concatenate([block[:upto] for block in own_key], axis=0))
            d_query[here, out] = (grad * query_slope[here, cols].astype(f32)).astype(bf16)
            weights = jnp.concatenate(
                [weights_t[base + half * tokens + i : base + half * tokens + i + rows, i:] for half in range(2)], axis=1
            )
            grad = mm(weights, jnp.concatenate([block[i:] for block in own_num], axis=0))
            d_value[here, out] = grad.astype(bf16)
            allowed = mask_t[here, i:]
            d_scores_t = mm(jnp.concatenate([block[here] for block in right], axis=0), left[i:], NT)
            d_scores_t = [(d_scores_t[half * rows : (half + 1) * rows] * allowed).astype(bf16) for half in range(2)]
            grad = mm(
                jnp.concatenate(d_scores_t, axis=1), jnp.concatenate([block[i:] for block in own_query], axis=0)
            )
            d_key[here, out] = (grad * key_slope[here, cols].astype(f32)).astype(bf16)


def mix_first_kernel(
    local,
    a0,
    a1,
    a2,
    a3,
    attn_low,
    mixed_low,
    inverse,
    query_feat,
    key_feat,
    value_low,
    query_slope,
    key_slope,
    weights_t,
    mask,
    mask_t,
    d_attn,
    d_num,
    d_den,
    d_query,
    d_key,
    d_value,
):
    rank = lax.axis_index("mp")
    tokens, width = d_attn.shape
    ranks = tokens // local
    for step, block in zip(MIX_STEPS, (a0, a1, a2, a3)):
        d_attn[rank_rows(source(rank, step, ranks), local), :] = block[...]
    piece = 768
    for c in range(0, width, piece):
        cols = slice(c, c + piece)
        d_mixed = mm(d_attn[...], attn_low[3, cols, :], NT) * inverse[:, cols]
        d_num[:, cols] = d_mixed.astype(bf16)
        d_den[:, cols] = (d_mixed * mixed_low[:, cols].astype(f32)).astype(bf16)
    mix_heads(
        0, d_num, d_den, query_feat, key_feat, value_low, query_slope, key_slope, weights_t, mask, mask_t, d_query,
        d_key, d_value,
    )


def mix_first(blocks, attn_low, mixed_low, inverse, feats):
    local, width = blocks[0].shape
    tokens = mixed_low.shape[0]
    return pl.pallas_call(
        functools.partial(mix_first_kernel, local),
        out_shape=[near((tokens, width), bf16)] * 3 + [near((tokens, width // 2), bf16)] * 3,
        compiler_params=params(16),
        cost_estimate=pl.CostEstimate(flops=6_000_000_000, bytes_accessed=18_000_000, transcendentals=0),
        name="mix_first",
    )(in_vmem(blocks[0]), *blocks[1:], *all_vmem((attn_low, mixed_low, inverse, *feats)))


def mix_second_kernel(
    d_attn,
    d_num,
    d_den,
    first_query,
    first_key,
    first_value,
    attn_low,
    query_feat,
    key_feat,
    value_low,
    query_slope,
    key_slope,
    weights_t,
    mask,
    mask_t,
    x_slice,
    mixed_slice,
    sums,
    d_query,
    d_key,
    d_value,
    vec,
    keep,
    send,
    attn_grad,
):
    width = d_attn.shape[1]
    own_width = x_slice.shape[0]
    half = width // 2
    for source, target in ((first_query, d_query), (first_key, d_key), (first_value, d_value)):
        target[:, 0:half] = source[...]
    mix_heads(
        half, d_num, d_den, query_feat, key_feat, value_low, query_slope, key_slope, weights_t, mask, mask_t,
        d_query.at[:, half:width], d_key.at[:, half:width], d_value.at[:, half:width],
    )
    for k, grad in enumerate((d_query, d_key, d_value)):
        attn_grad[k * own_width : (k + 1) * own_width, :] = mm(x_slice[...], grad[...])
    attn_grad[3 * own_width : 4 * own_width, :] = mm(mixed_slice[...], d_attn[...])
    write_halves(attn_grad, keep, send)
    held, packed = two_parts(sums[0:4, :])
    send[2 * own_width :, :] = packed
    vec[0:4, :] = held
    vec[4:8, :] = jnp.zeros_like(held)


def mix_second(first, attn_low, feats, x_slice, mixed_slice, sums):
    tokens, width = first[0].shape
    own_width = x_slice.shape[0]
    return pl.pallas_call(
        mix_second_kernel,
        out_shape=[near((tokens, width), bf16)] * 3
        + [
            near((8, width), f32),
            near((2 * own_width, width), f32),
            near((2 * own_width + VEC_ROWS, width), bf16),
        ],
        scratch_shapes=[pltpu.VMEM((4 * own_width, width), f32)],
        compiler_params=params(16),
        cost_estimate=pl.CostEstimate(flops=6_000_000_000, bytes_accessed=18_000_000, transcendentals=0),
        name="mix_second",
    )(*all_vmem((*first, attn_low, *feats, x_slice, mixed_slice, sums)))


def tokens_back_kernel(
    d_query, d_key, d_value, attn_low, d_resid, attn_weight, up_weight, down_weight, tokens_grad, own_attn, own_up, own_down,
    sems,
):
    local, own_width = d_resid.shape[0], own_attn.shape[1]
    rank = lax.axis_index("mp")
    columns = pl.ds(pl.multiple_of(rank * own_width, own_width), own_width)
    copies = [
        pltpu.make_async_copy(attn_weight.at[:, columns, :], own_attn, sems.at[0]),
        pltpu.make_async_copy(up_weight, own_up, sems.at[1]),
        pltpu.make_async_copy(down_weight, own_down, sems.at[2]),
    ]
    for copy in copies:
        copy.start()
    mine = pl.ds(pl.multiple_of(rank * local, local), local)
    tokens_grad[...] = (
        d_resid[...]
        + mm(d_query[mine, :], attn_low[0], NT)
        + mm(d_key[mine, :], attn_low[1], NT)
        + mm(d_value[mine, :], attn_low[2], NT)
    )
    for copy in copies:
        copy.wait()


def tokens_back(d_query, d_key, d_value, attn_low, d_resid, attn_weight, up_weight, down_weight, own_width):
    return pl.pallas_call(
        tokens_back_kernel,
        in_specs=[pl.BlockSpec(memory_space=pltpu.VMEM)] * 5 + [pl.BlockSpec(memory_space=pl.ANY)] * 3,
        out_shape=[
            sds(d_resid.shape, f32),
            near((4, own_width, d_resid.shape[1]), f32),
            near(up_weight.shape, f32),
            near(down_weight.shape, f32),
        ],
        scratch_shapes=[pltpu.SemaphoreType.DMA((3,))],
        compiler_params=params(16),
        cost_estimate=NO_COST,
        name="tokens_back",
    )(
        *all_vmem((d_query, d_key, d_value, attn_low, d_resid)), in_hbm(attn_weight), in_hbm(up_weight),
        in_hbm(down_weight),
    )


def as_row(column):
    return jnp.transpose(jnp.broadcast_to(column, (column.shape[0], 128)))[0:1, :]


def as_column(row):
    return jnp.transpose(jnp.broadcast_to(row, (128, row.shape[1])))[:, 0:1]


SHARE_ROWS = 32


def lane_scalars(values, width):
    lane = lax.broadcasted_iota(jnp.int32, (1, width), 1)
    row = jnp.zeros((1, width), f32)
    for k, value in enumerate(values):
        row = jnp.where(lane == k, value, row)
    return row


def lane_scalar(row, k):
    lane = lax.broadcasted_iota(jnp.int32, row.shape, 1)
    return jnp.sum(jnp.where(lane == k, row, 0.0), axis=1, keepdims=True)


def attn_stats_kernel(even, odd, vec, stats, feed_shares, total, rows_new, shares, columns, rows16):
    own_width, width = total.shape[0] // 4, total.shape[1]
    mine = pl.ds(pl.multiple_of(lax.axis_index("mp") * own_width, own_width), own_width)
    read_halves(even, odd, total)
    scalars = []
    for k in range(4):
        grad = total[k * own_width : (k + 1) * own_width, :]
        square = grad * grad
        columns[...] = as_column(stats[k, 0:1, :])
        rows = decay * columns[mine, :] + (1.0 - decay) * jnp.mean(square + tiny_square, axis=1, keepdims=True)
        rows_new[k : k + 1, :] = as_row(rows)
        rows16[k : k + 1, :] = jnp.sum(square + tiny_square, axis=0, keepdims=True)
        rows16[4 + k : 5 + k, :] = jnp.sum(square * (1.0 / rows), axis=0, keepdims=True)
        scalars.append(jnp.sum(rows, axis=0, keepdims=True))
    rows16[8:12, :] = vec[0:4, :]
    rows16[12:16, :] = feed_shares[0:4, :]
    shares[0:16, :] = rows16[...].astype(bf16)
    row = lane_scalars(scalars, width) + feed_shares[4:5, :]
    high = row.astype(bf16).astype(f32)
    low = (row - high).astype(bf16).astype(f32)
    shares[16:, :] = jnp.concatenate([high, low, jnp.zeros((SHARE_ROWS - 18, width), f32)], axis=0).astype(bf16)


def attn_stats_call(even, odd, vec, stats, feed_shares, own_width):
    width = even.shape[1]
    return pl.pallas_call(
        attn_stats_kernel,
        out_shape=[near((4 * own_width, width), f32), near((4, own_width), f32), near((SHARE_ROWS, width), bf16)],
        scratch_shapes=[pltpu.VMEM((width, 1), f32), pltpu.VMEM((16, width), f32)],
        compiler_params=params(16),
        name="attn_stats",
    )(in_vmem(even), odd, in_vmem(vec), stats, in_vmem(feed_shares))


def attn_out_kernel(total, rows, grad_out, rows_out):
    own_width = grad_out.shape[1]
    for k in range(4):
        grad_out[k] = total[k * own_width : (k + 1) * own_width, :]
    rows_out[...] = rows[...]


def attn_out(total, rows):
    own_width, width = rows.shape[1], total.shape[1]
    return pl.pallas_call(
        attn_out_kernel,
        out_shape=[sds((4, own_width, width), f32), sds((4, own_width), f32)],
        compiler_params=params(8),
        cost_estimate=NO_COST,
        name="attn_out",
    )(*all_vmem((total, rows)))


def feed_stats_kernel(mine, other, wide_old, squares, up_grad_out, down_grad_out, wide_out, grads, wide_new, shares):
    width, hidden = up_grad_out.shape
    for part, rows in enumerate((width, hidden)):
        half = slice(part * width // 2, (part * width + rows) // 2)
        read_halves(mine.at[half], other.at[half], grads.at[part * width : part * width + rows])
    grad = grads[0:width, :]
    up_grad_out[...] = grad
    square = grad * grad
    columns = decay * wide_old[0:1, :] + (1.0 - decay) * jnp.mean(square + tiny_square, axis=0, keepdims=True)
    wide_new[0:1, :] = columns
    shares[0:1, :] = as_row(jnp.sum(square + tiny_square, axis=1, keepdims=True))
    shares[1:2, :] = as_row(jnp.sum(square * (1.0 / columns), axis=1, keepdims=True))
    grad = grads[width:, :]
    down_grad_out[...] = grad
    square = grad * grad
    rows = decay * as_column(wide_old[1:2, :]) + (1.0 - decay) * jnp.mean(
        square + tiny_square, axis=1, keepdims=True
    )
    wide_new[1:2, :] = as_row(rows)
    wide_out[...] = wide_new[...]
    shares[2:3, :] = jnp.sum(square + tiny_square, axis=0, keepdims=True)
    shares[3:4, :] = jnp.sum(square * (1.0 / rows), axis=0, keepdims=True)
    scalars = [jnp.sum(rows, axis=0, keepdims=True)]
    for k in range(2):
        scalars.append(jnp.sum(squares[4 + k : 5 + k, :], axis=1, keepdims=True))
    shares[4:5, :] = lane_scalars([0.0] * 4 + scalars, width)
    shares[5:8, :] = jnp.zeros((3, width), f32)


def feed_stats(even, odd, wide_old, squares):
    width, hidden = squares.shape[1], wide_old.shape[1]
    return pl.pallas_call(
        feed_stats_kernel,
        out_shape=[
            sds((width, hidden), f32),
            sds((hidden, width), f32),
            sds((2, hidden), f32),
            near((width + hidden, width), f32),
            near((2, hidden), f32),
            near((8, width), f32),
        ],
        compiler_params=params(16),
        cost_estimate=NO_COST,
        name="feed_stats",
    )(in_vmem(even), odd, wide_old, in_vmem(squares))


def update_kernel(
    hidden_all,
    attn_grad,
    attn_weight,
    attn_rows,
    stats,
    feed_grad,
    up_weight,
    down_weight,
    wide_new,
    narrow_old,
    squares,
    share,
    share1,
    share2,
    share3,
    vec,
    vec_moment,
    *refs,
):
    outs, made, sems = refs[0:11], refs[11:22], refs[22]
    attn_new, attn_new_low, up_new, up_new_low, down_new, down_new_low = made[0:6]
    attn_cols, narrow_new, vec_grad, vec_moment_new, vec_new = made[6:11]
    width = narrow_old.shape[1]
    own_width = attn_rows.shape[1]
    copies = []

    def leave(which, *place):
        source = made[which].at[place] if place else made[which]
        target = outs[which].at[place] if place else outs[which]
        copy = pltpu.make_async_copy(source, target, sems.at[len(copies)])
        copy.start()
        copies.append(copy)

    total = (share[...].astype(f32) + share1[...].astype(f32)) + (share2[...].astype(f32) + share3[...].astype(f32))
    scalars = total[16:17, :] + total[17:18, :]
    entries = float(width * hidden_all)
    rows = decay * narrow_old[0:1, :] + (1.0 - decay) * total[12:13, :] / hidden_all
    narrow_new[0:1, :] = rows
    cols = decay * narrow_old[1:2, :] + (1.0 - decay) * total[14:15, :] / hidden_all
    narrow_new[1:2, :] = cols
    mean_up = jnp.mean(rows, axis=1, keepdims=True)
    mean_down = lane_scalar(scalars, 4) / hidden_all

    def step_size(scaled, weight_square, count):
        clip = jnp.maximum(1.0, jnp.sqrt(scaled / count) / clip_limit)
        return learn_rate * jnp.sqrt(weight_square / count) / clip

    up_size = step_size(
        jnp.sum(total[13:14, :] / rows, axis=1, keepdims=True) * mean_up, lane_scalar(scalars, 5), entries
    )
    down_size = step_size(
        jnp.sum(total[15:16, :] / cols, axis=1, keepdims=True) * mean_down, lane_scalar(scalars, 6), entries
    )

    def block(which, here, grad, weight, row, col, mean, size):
        scale = row * col * (1.0 / mean)
        value = weight - size * (grad * lax.rsqrt(scale))
        made[which][here] = value
        made[which + 1][here] = value.astype(bf16)
        leave(which, *here)
        leave(which + 1, *here)

    pieces = 4
    row = as_column(rows)
    step = up_weight.shape[0] // pieces
    for n in range(pieces):
        here = slice(n * step, (n + 1) * step)
        block(2, (here, slice(None)), feed_grad[here, :], up_weight[here, :], row[here], wide_new[0:1, :], mean_up, up_size)
    row = as_column(wide_new[1:2, :])
    step = down_weight.shape[0] // pieces
    for n in range(pieces):
        here = slice(n * step, (n + 1) * step)
        below = slice(up_weight.shape[0] + n * step, up_weight.shape[0] + (n + 1) * step)
        block(4, (here, slice(None)), feed_grad[below, :], down_weight[here, :], row[here], cols, mean_down, down_size)
    leave(7)
    entries = float(width * width)
    for k in range(4):
        col = decay * stats[k, 1:2, :] + (1.0 - decay) * total[k : k + 1, :] / width
        attn_cols[k : k + 1, :] = col
        mean = lane_scalar(scalars, k) / width
        size = step_size(
            jnp.sum(total[4 + k : 5 + k, :] / col, axis=1, keepdims=True) * mean,
            jnp.sum(squares[k : k + 1, :], axis=1, keepdims=True),
            entries,
        )
        block(
            0, (k,), attn_grad[k * own_width : (k + 1) * own_width, :], attn_weight[k], as_column(attn_rows[k : k + 1, :]),
            col, mean, size,
        )
    leave(6)
    grads = total[8:12, :]
    vec_grad[...] = grads
    leave(8)
    moment = decay * vec_moment[...] + (1.0 - decay) * (grads * grads + tiny_square)
    vec_moment_new[...] = moment
    leave(9)
    scaled = grads * lax.rsqrt(moment)
    clip = jnp.maximum(1.0, jnp.sqrt(jnp.mean(scaled * scaled, axis=1, keepdims=True)) / clip_limit)
    held = vec[...]
    spread = jnp.sqrt(jnp.mean(held * held, axis=1, keepdims=True))
    vec_new[...] = held - learn_rate * spread * scaled / clip
    leave(10)
    for copy in copies:
        copy.wait()


def update(
    attn_grad, attn_weight, attn_rows, stats, feed_grad, up_weight, down_weight, wide_new, narrow_old, squares, shares,
    vec, vec_moment, hidden_all,
):
    _, own_width, width = attn_weight.shape
    hidden = up_weight.shape[1]
    outs = [((4, own_width, width), t) for t in (f32, bf16)]
    outs += [((width, hidden), t) for t in (f32, bf16)] + [((hidden, width), t) for t in (f32, bf16)]
    outs += [((4, width), f32), ((2, width), f32)] + [((4, width), f32)] * 3
    return pl.pallas_call(
        functools.partial(update_kernel, hidden_all),
        in_specs=[pl.BlockSpec(memory_space=pltpu.VMEM)] * 16,
        out_specs=[pl.BlockSpec(memory_space=pl.ANY)] * 11,
        out_shape=[pltpu.HBM(*out) for out in outs],
        scratch_shapes=[pltpu.VMEM(*out) for out in outs]
        + [pltpu.SemaphoreType.DMA((29,))],
        compiler_params=params(24),
        name="update",
    )(
        *all_vmem((attn_grad, attn_weight, attn_rows)), stats,
        *all_vmem((feed_grad, up_weight, down_weight, wide_new)), narrow_old, in_vmem(squares), in_vmem(shares[0]),
        *shares[1:], vec, vec_moment,
    )


def exchange(parts, steps):
    ranks = len(parts)
    moved = [
        lax.ppermute(part, "mp", [(i, target(i, step, ranks)) for i in range(ranks)])
        for part, step in zip(parts[1:], steps[1:])
    ]
    return [parts[0]] + moved


def on_device(
    tokens,
    cotangent,
    seq_starts,
    attn_weight,
    up_weight,
    down_weight,
    vec_params,
    attn_stats,
    ffn_narrow_stats,
    ffn_wide_stats,
    vec_moment,
):
    ranks = lax.axis_size("mp")
    local, width = tokens.shape
    own_width = width // ranks
    hidden_all = up_weight.shape[1] * ranks

    blocks = exchange([tokens] * ranks, TOKEN_STEPS)
    attn_low, up_low, down_low, mask, mask_t, squares = prepare(
        seq_starts, attn_weight, up_weight, down_weight, local * ranks
    )
    (
        x_all,
        query_feat,
        key_feat,
        value_low,
        mixed_low,
        inverse,
        own_sum,
        own_first,
        first_low,
        pre_act,
        hidden_low,
        *parts,
    ) = forward(blocks, attn_low, up_low, down_low, mask, vec_params)
    parts = exchange(parts, BRANCH_STEPS)
    weights_t, query_slope, key_slope, slope = slopes(query_feat, key_feat, mask_t, pre_act)
    own_first, slope = lax.optimization_barrier((own_first, slope))
    feats = (query_feat, key_feat, value_low, query_slope, key_slope, weights_t, mask, mask_t)
    mixing = (attn_low, mixed_low, inverse, *feats)
    feeding = (up_low, down_low, first_low, slope, hidden_low)
    block_near, d_second, sums, *d_branch = middle(
        parts, own_first, cotangent, vec_params, (*mixing, *feeding, own_sum, x_all)
    )
    turned_from, d_second = lax.optimization_barrier((x_all, d_second))
    x_slice, mixed_slice, block_out = own_columns(turned_from, mixed_low, block_near, own_width)
    slope, x_slice = lax.optimization_barrier((slope, x_slice))
    d_branch, d_pre, *parts = feed_back(
        exchange(d_branch, BACK_STEPS), slope, up_low, down_low, (*mixing, first_low, hidden_low, own_sum, d_second, sums, x_slice, mixed_slice)
    )
    staged = lax.axis_size("dp") == STAGED

    parts = exchange(parts, FIRST_STEPS)
    *feed_keep, up_send, down_send = feed_grads(first_low, d_pre, hidden_low, d_branch)
    if staged:
        up = fold_first(feed_keep[0], across(up_send, 1))
        down = fold_first(feed_keep[1], across(down_send, 1))
        parts[0], up, down = lax.optimization_barrier((parts[0], up, down))
        got_up, got_down = [[across(a, 2), across(b, 4)] for a, b in (up, down)]
    d_resid, sums, *d_attn = first_back(
        parts, d_second, own_sum, sums, vec_params, (*mixing, x_slice, mixed_slice)
    )
    blocks = exchange(d_attn, MIX_STEPS)
    if staged:
        d_resid, up, down = lax.optimization_barrier((d_resid, up, down))
        feed_a, feed_b = fold_feed((*up, *down), (*got_up, *got_down))
        blocks[0], feed_a, feed_b = lax.optimization_barrier((blocks[0], feed_a, feed_b))
        got_a, got_b = across(feed_a, 4), across(feed_b, 2)
    first = mix_first(blocks, attn_low, mixed_low, inverse, feats)
    *d_mix, vec_part, attn_keep, attn_send = mix_second(first, attn_low, feats, x_slice, mixed_slice, sums)
    if staged:
        feed_even = fold_feed_last(feed_a, got_a, feed_b, got_b)
        attn_send, feed_even = lax.optimization_barrier((attn_send, feed_even))
        received = across(attn_send, 1)
        feed_odd = across(feed_even, 1)
        vec_part, attn_a, attn_b = fold_first(attn_keep, received, vec_part)
        got_a, got_b = across(attn_a, 2), across(attn_b, 4)
    else:
        feed_even, feed_odd, attn_even, attn_odd, vec_part = lax.psum(
            (jnp.concatenate(feed_keep), jnp.concatenate([up_send, down_send]).astype(f32), attn_keep, attn_send[: 2 * own_width].astype(f32), vec_part), "dp"
        )
    up_grad, down_grad, wide_out, feed_near, wide_near, feed_shares = feed_stats(
        feed_even, feed_odd, ffn_wide_stats, squares
    )
    tokens_grad, own_attn, own_up, own_down = tokens_back(
        *d_mix, attn_low, d_resid, attn_weight, up_weight, down_weight, own_width
    )
    if staged:
        attn_a, tokens_grad = lax.optimization_barrier((attn_a, tokens_grad))
        vec_part, attn_a, attn_b = fold_second(attn_a, got_a, attn_b, got_b, vec_part)
        got_a, got_b = across(attn_a, 4), across(attn_b, 2)
        attn_a, feed_shares = lax.optimization_barrier((attn_a, feed_shares))
        vec_part, attn_even = fold_last(attn_a, got_a, attn_b, got_b, vec_part)
        attn_odd = across(attn_even, 1)
    attn_near, rows_near, shares = attn_stats_call(attn_even, attn_odd, vec_part, attn_stats, feed_shares, own_width)
    shares = exchange([shares] * ranks, SHARE_STEPS)
    attn_grad, attn_rows = attn_out(attn_near, rows_near)
    attn_near, attn_grad = lax.optimization_barrier((attn_near, attn_grad))
    (
        attn_new,
        attn_new_low,
        up_new,
        up_new_low,
        down_new,
        down_new_low,
        attn_cols,
        narrow_new,
        vec_grad,
        vec_moment_new,
        vec_new,
    ) = update(
        attn_near, own_attn, rows_near, attn_stats, feed_near, own_up, own_down, wide_near, ffn_narrow_stats,
        squares, shares, vec_params, vec_moment, hidden_all,
    )
    return (
        block_out,
        tokens_grad,
        attn_grad,
        attn_rows,
        attn_cols,
        attn_new,
        attn_new_low,
        up_grad,
        down_grad,
        narrow_new,
        wide_out,
        up_new,
        down_new,
        up_new_low,
        down_new_low,
        vec_grad,
        vec_moment_new,
        vec_new,
    )


def solution(mesh):
    in_specs = (
        P(("dp", "mp"), None),
        P(("dp", "mp"), None),
        P("dp", None),
        P(),
        P(None, "mp"),
        P("mp", None),
        P(),
        P(),
        P(),
        P(None, "mp"),
        P(),
    )
    out_specs = (
        P(("dp", "mp"), None),
        P(("dp", "mp"), None),
        P(None, "mp", None),
        P(None, "mp"),
        P(),
        P(None, "mp", None),
        P(None, "mp", None),
        P(None, "mp"),
        P("mp", None),
        P(),
        P(None, "mp"),
        P(None, "mp"),
        P("mp", None),
        P(None, "mp"),
        P("mp", None),
        P(),
        P(),
        P(),
    )
    return jax.shard_map(
        on_device, mesh=mesh, in_specs=in_specs, out_specs=out_specs, check_vma=False
    )
```

```python
import functools
import math

import jax
import jax.numpy as jnp
from jax import lax
from jax.experimental import pallas as pl
from jax.experimental.pallas import tpu as pltpu
from jax.sharding import PartitionSpec as P

HEADS = 12
STEP = 10

norm_eps = 1e-05
tiny_square = 1e-30
learn_rate = 0.3
clip_limit = 1.0
decay = 1.0 - float(STEP) ** (-0.8)

f32 = jnp.float32
bf16 = jnp.bfloat16

NN = (((1,), (0,)), ((), ()))
NT = (((1,), (1,)), ((), ()))
TN = (((0,), (0,)), ((), ()))


def mm(a, b, dims=NN):
    return lax.dot_general(a, b, dims, preferred_element_type=f32)


def params(mib):
    return pltpu.CompilerParams(vmem_limit_bytes=mib * 1024 * 1024)


def sds(shape, dtype):
    return jax.ShapeDtypeStruct(shape, dtype)


def in_hbm(array):
    return pltpu.with_memory_space_constraint(array, pltpu.HBM)


def in_vmem(array):
    return pltpu.with_memory_space_constraint(array, pltpu.VMEM)


def all_vmem(arrays):
    return [in_vmem(array) for array in arrays]


def near(shape, dtype):
    return pltpu.VMEM(shape, dtype)


NO_COST = pl.CostEstimate(flops=0, bytes_accessed=0, transcendentals=0)


def holding(kernel, count, held):
    def body(*refs):
        for ref in refs[count : count + held]:
            pltpu.touch(ref)
        kernel(*refs[:count], *refs[count + held :])

    return body


STAGED = 8
VEC_ROWS = 16
TOKEN_STEPS = (0, -2, -1, -3)
BRANCH_STEPS = (0, 2, 1, 3)
BACK_STEPS = (0, 2, 1, 3)
FIRST_STEPS = (0, 1, 2, 3)
MIX_STEPS = (0, 2, 1, 3)
SHARE_STEPS = (0, -1, -2, -3)


def target(rank, step, ranks):
    return rank ^ -step if step <= 0 else (rank + step) % ranks


def source(rank, step, ranks):
    return rank ^ -step if step <= 0 else (rank + ranks - step) % ranks


def rank_rows(rank, rows):
    return pl.ds(pl.multiple_of(rank * rows, rows), rows)


def half_rows(count, mine):
    rows = count // 2
    side = lax.rem(lax.axis_index("dp"), 2) if lax.axis_size("dp") == STAGED else 0
    return pl.ds(pl.multiple_of((side if mine else 1 - side) * rows, rows), rows)


def write_halves(total, keep, send):
    rows = total.shape[0] // 2
    keep[...] = total[half_rows(total.shape[0], True), :]
    send[0:rows, :] = total[half_rows(total.shape[0], False), :].astype(send.dtype)


def read_halves(mine, other, total):
    total[half_rows(total.shape[0], True), :] = mine[...].astype(total.dtype)
    total[half_rows(total.shape[0], False), :] = other[...].astype(total.dtype)


def two_parts(values):
    high = values.astype(bf16).astype(f32)
    low = (values - high).astype(bf16).astype(f32)
    both = jnp.concatenate([high, low], axis=0)
    return high + low, jnp.concatenate([both, jnp.zeros_like(both)], axis=0).astype(bf16)


def joined(block):
    block = block.astype(f32)
    return block[0:4, :] + block[4:8, :]


def add_vec(vec, block, vec_out, send=None):
    held, packed = two_parts(vec[0:4, :] + joined(block))
    vec_out[0:4, :] = held
    vec_out[4:8, :] = jnp.zeros_like(held)
    if send is not None:
        send[...] = packed


def fold_first_kernel(keep, received, *refs):
    send_a, send_b = refs[-2:]
    rows = keep.shape[0] // 2
    send_a[0:rows, :] = (keep[0:rows, :] + received[0:rows, :].astype(f32)).astype(bf16)
    send_b[...] = (keep[rows : 2 * rows, :] + received[rows : 2 * rows, :].astype(f32)).astype(bf16)
    if len(refs) > 2:
        add_vec(refs[0], received[2 * rows :, :], refs[1], send_a.at[rows:, :])


def fold_second_kernel(own_a, got_a, own_b, got_b, *refs):
    send_a, send_b = refs[-2:]
    rows = own_b.shape[0]
    send_a[0:rows, :] = (own_a[0:rows, :].astype(f32) + got_a[0:rows, :].astype(f32)).astype(bf16)
    send_b[...] = (own_b[...].astype(f32) + got_b[...].astype(f32)).astype(bf16)
    if len(refs) > 2:
        add_vec(refs[0], got_a[rows:, :], refs[1], send_a.at[rows:, :])


def fold_last_kernel(own_a, got_a, own_b, got_b, *refs):
    total = refs[-1]
    rows = own_b.shape[0]
    total[0:rows, :] = (own_a[0:rows, :].astype(f32) + got_a[0:rows, :].astype(f32)).astype(bf16)
    total[rows:, :] = (own_b[...].astype(f32) + got_b[...].astype(f32)).astype(bf16)
    if len(refs) > 1:
        add_vec(refs[0], got_a[rows:, :], refs[1])


def fold_call(kernel, name, inputs, vec, outs):
    width = inputs[0].shape[1]
    extra_in, extra_out = ([in_vmem(vec)], [near((8, width), f32)]) if vec is not None else ([], [])
    return pl.pallas_call(
        kernel,
        out_shape=extra_out + [near((rows, width), bf16) for rows in outs],
        compiler_params=params(8),
        cost_estimate=NO_COST,
        name=name,
    )(in_vmem(inputs[0]), *inputs[1:], *extra_in)


def fold_first(keep, received, vec=None):
    rows = keep.shape[0] // 2
    return fold_call(
        fold_first_kernel, "fold_first", (keep, received), vec, (rows if vec is None else rows + VEC_ROWS, rows)
    )


def fold_second(own_a, got_a, own_b, got_b, vec=None):
    return fold_call(
        fold_second_kernel, "fold_second", (own_a, got_a, own_b, got_b), vec, (own_a.shape[0], own_b.shape[0])
    )


def fold_last(own_a, got_a, own_b, got_b, vec=None):
    return fold_call(fold_last_kernel, "fold_last", (own_a, got_a, own_b, got_b), vec, (2 * own_b.shape[0],))


def fold_feed_kernel(*refs):
    own, got, (send_a, send_b) = refs[0:4], refs[4:8], refs[8:]
    rows = own[0].shape[0]
    for n, (block, other) in enumerate(zip(own, got)):
        send = (send_a, send_b)[n % 2]
        place = n // 2 * rows
        send[place : place + rows, :] = (block[...].astype(f32) + other[...].astype(f32)).astype(bf16)


def fold_feed(own, got):
    rows, width = own[0].shape
    return pl.pallas_call(
        fold_feed_kernel,
        out_shape=[near((2 * rows, width), bf16)] * 2,
        compiler_params=params(8),
        cost_estimate=NO_COST,
        name="fold_feed",
    )(*all_vmem(own), *got)


def fold_feed_last_kernel(own_a, got_a, own_b, got_b, total):
    rows = own_a.shape[0] // 2
    for n, (block, other) in enumerate(((own_a, got_a), (own_b, got_b))):
        for part in range(2):
            here = slice(part * rows, (part + 1) * rows)
            place = (2 * part + n) * rows
            total[place : place + rows, :] = (block[here, :].astype(f32) + other[here, :].astype(f32)).astype(bf16)


def fold_feed_last(own_a, got_a, own_b, got_b):
    rows, width = own_a.shape
    return pl.pallas_call(
        fold_feed_last_kernel,
        out_shape=near((2 * rows, width), bf16),
        compiler_params=params(8),
        cost_estimate=NO_COST,
        name="fold_feed_last",
    )(in_vmem(own_a), got_a, in_vmem(own_b), got_b)


def across(block, bit):
    return lax.ppermute(block, "dp", [(i, i ^ bit) for i in range(STAGED)])


def prepare_kernel(seqs, tokens_pack, starts, attn, up, down, attn_low, up_low, down_low, mask, mask_t, squares):
    step = pl.program_id(0)

    @pl.when(step == 0)
    def _():
        squares[...] = jnp.zeros_like(squares)

    for k in range(4):
        block = attn[k]
        attn_low[k] = block.astype(bf16)
        squares[k : k + 1, :] += jnp.sum(block * block, axis=0, keepdims=True)
    for k, (source, target) in enumerate(((up, up_low), (down, down_low))):
        block = source[...]
        target[...] = block.astype(bf16)
        squares[4 + k : 5 + k, :] += jnp.sum(block * block, axis=0, keepdims=True)

    def layout(index):
        seq = jnp.zeros_like(index)
        begin = jnp.zeros_like(index)
        length = jnp.ones_like(index)
        for s in range(seqs):
            start = starts[0, s]
            finish = starts[0, s + 1] if s + 1 < seqs else tokens_pack
            inside = index >= start
            seq = jnp.where(inside, s, seq)
            begin = jnp.where(inside, start, begin)
            length = jnp.where(inside, finish - start, length)
        angle = 0.5 * math.pi * (index - begin).astype(f32) / length.astype(f32)
        return seq, jnp.cos(angle), jnp.sin(angle)

    rows = mask.shape[0]
    row = lax.broadcasted_iota(jnp.int32, (rows, 128), 0) + step * rows
    col = lax.broadcasted_iota(jnp.int32, (8, tokens_pack), 1)
    row_seq, row_cos, row_sin = (a[:, 0:1] for a in layout(row))
    col_seq, col_cos, col_sin = (a[0:1, :] for a in layout(col))
    same = row_seq == col_seq
    value = row_cos * col_cos + row_sin * col_sin
    row, col = row[:, 0:1], col[0:1, :]
    mask[...] = jnp.where(same & (col <= row), value, 0.0)
    mask_t[...] = jnp.where(same & (row <= col), value, 0.0)


def prepare(seq_starts, attn_weight, up_weight, down_weight, tokens_pack):
    steps = 8
    seqs = seq_starts.shape[1]
    heads4, width, _ = attn_weight.shape
    hidden = up_weight.shape[1]
    a_rows, u_rows, d_rows, m_rows = width // steps, width // steps, hidden // steps, tokens_pack // steps
    return pl.pallas_call(
        functools.partial(prepare_kernel, seqs, tokens_pack),
        grid=(steps,),
        in_specs=[
            pl.BlockSpec(memory_space=pltpu.SMEM),
            pl.BlockSpec((4, a_rows, width), lambda i: (0, i, 0)),
            pl.BlockSpec((u_rows, hidden), lambda i: (i, 0)),
            pl.BlockSpec((d_rows, width), lambda i: (i, 0)),
        ],
        out_specs=[
            pl.BlockSpec((4, a_rows, width), lambda i: (0, i, 0)),
            pl.BlockSpec((u_rows, hidden), lambda i: (i, 0)),
            pl.BlockSpec((d_rows, width), lambda i: (i, 0)),
            pl.BlockSpec((m_rows, tokens_pack), lambda i: (i, 0)),
            pl.BlockSpec((m_rows, tokens_pack), lambda i: (i, 0)),
            pl.BlockSpec((8, width), lambda i: (0, 0)),
        ],
        out_shape=[
            near((4, width, width), bf16),
            near((width, hidden), bf16),
            near((hidden, width), bf16),
            near((tokens_pack, tokens_pack), f32),
            near((tokens_pack, tokens_pack), f32),
            near((8, width), f32),
        ],
        compiler_params=params(24),
        cost_estimate=pl.CostEstimate(flops=10_000_000, bytes_accessed=22_000_000, transcendentals=0),
        name="prepare",
    )(seq_starts, in_hbm(attn_weight), in_hbm(up_weight), in_hbm(down_weight))


def half_lanes(width):
    return lax.broadcasted_iota(jnp.int32, (1, width), 1) < width // 2


def norm_parts(values):
    centered = values - jnp.mean(values, axis=-1, keepdims=True)
    spread = lax.rsqrt(jnp.mean(centered * centered, axis=-1, keepdims=True) + norm_eps)
    return centered * spread, spread


def norm_back(grad, unit, spread, gain):
    scaled = grad * gain
    return spread * (
        scaled
        - jnp.mean(scaled, axis=-1, keepdims=True)
        - unit * jnp.mean(scaled * unit, axis=-1, keepdims=True)
    )


def causal_blocks(tokens, size):
    return [(i, min(size, tokens - i)) for i in range(0, tokens, size)]


def forward_kernel(
    local,
    x0,
    x1,
    x2,
    x3,
    attn_low,
    up_low,
    down_low,
    mask,
    vec,
    x_all,
    query_feat,
    key_feat,
    value_low,
    mixed_low,
    inverse,
    own_sum,
    own_first,
    first_low,
    pre_act,
    hidden_low,
    part0,
    part1,
    part2,
    part3,
    branch,
):
    rank = lax.axis_index("mp")
    tokens, width = x_all.shape
    ranks = tokens // local

    for step, block in zip(TOKEN_STEPS, (x0, x1, x2, x3)):
        x_all[rank_rows(source(rank, step, ranks), local), :] = block[...]

    piece = 256
    for c in range(0, width, piece):
        cols = slice(c, c + piece)
        for which, feat in ((0, query_feat), (1, key_feat)):
            raw = mm(x_all[...], attn_low[which, :, cols])
            feat[:, cols] = jax.nn.softplus(raw).astype(bf16)
        value_low[:, cols] = mm(x_all[...], attn_low[2, :, cols]).astype(bf16)

    pair = 2 * (width // HEADS)
    first_half = half_lanes(pair)
    for c in range(0, width, pair):
        cols = slice(c, c + pair)
        keys = key_feat[:, cols]
        values = value_low[:, cols]
        zero = jnp.zeros_like(keys)
        one = jnp.ones_like(values)
        sides = (first_half, ~first_half)
        own_keys = [jnp.where(own, keys, zero) for own in sides]
        own_values = [
            jnp.concatenate([jnp.where(own, values, zero), jnp.where(own, one, zero)], axis=1) for own in sides
        ]
        for i, rows in causal_blocks(tokens, 256):
            here = slice(i, i + rows)
            upto = i + rows
            queries = query_feat[here, cols]
            allowed = mask[here, :upto]
            scores = mm(queries, jnp.concatenate([block[:upto] for block in own_keys], axis=0), NT)
            weights = (scores * jnp.concatenate([allowed, allowed], axis=1)).astype(bf16)
            both = mm(weights, jnp.concatenate([block[:upto] for block in own_values], axis=0))
            inv = 1.0 / both[:, pair:]
            inverse[here, cols] = inv
            mixed_low[here, cols] = (both[:, :pair] * inv).astype(bf16)

    for i, rows in causal_blocks(tokens, 256):
        here = slice(i, i + rows)
        summed = x_all[here, :].astype(f32) + mm(mixed_low[here, :], attn_low[3])
        branch[here, :] = summed
        unit, _ = norm_parts(summed)
        first_low[here, :] = (unit * vec[0:1, :] + vec[1:2, :]).astype(bf16)
    own_sum[...] = branch[rank_rows(rank, local), :]
    unit, _ = norm_parts(own_sum[...])
    own_first[...] = unit * vec[0:1, :] + vec[1:2, :]

    hidden_count = up_low.shape[1]
    for c in range(0, hidden_count, piece):
        cols = slice(c, c + piece)
        pre = mm(first_low[...], up_low[:, cols])
        cdf = 0.5 * (1.0 + lax.erf(pre * math.sqrt(0.5)))
        hidden_low[:, cols] = (pre * cdf).astype(bf16)
        pre_act[:, cols] = pre

    branch[...] = mm(hidden_low[...], down_low[...])
    for step, part in zip(BRANCH_STEPS, (part0, part1, part2, part3)):
        part[...] = branch[rank_rows(target(rank, step, ranks), local), :].astype(part.dtype)


def forward(blocks, attn_low, up_low, down_low, mask, vec):
    local, width = blocks[0].shape
    tokens = mask.shape[0]
    hidden = up_low.shape[1]
    return pl.pallas_call(
        functools.partial(forward_kernel, local),
        out_shape=[near((tokens, width), bf16)] * 5
        + [near((tokens, width), f32), near((local, width), f32), near((local, width), f32)]
        + [near((tokens, width), bf16), near((tokens, hidden), f32), near((tokens, hidden), bf16)]
        + [near((local, width), f32)]
        + [near((local, width), bf16)] * 3,
        scratch_shapes=[pltpu.VMEM((tokens, width), f32)],
        compiler_params=params(16),
        cost_estimate=pl.CostEstimate(flops=8_000_000_000, bytes_accessed=20_000_000, transcendentals=2_000_000),
        name="forward",
    )(*blocks, *all_vmem((attn_low, up_low, down_low, mask)), vec)


def slopes_kernel(query_feat, key_feat, mask_t, pre_act, weights_t, query_slope, key_slope, slope):
    tokens, width = query_feat.shape
    piece = 256
    for c in range(0, width, piece):
        cols = slice(c, c + piece)
        for feat, grad in ((query_feat, query_slope), (key_feat, key_slope)):
            value = feat[:, cols].astype(f32)
            small = value * (1.0 - value * (0.5 - value * (1.0 / 6.0)))
            grad[:, cols] = jnp.where(value < 0.02, small, 1.0 - jnp.exp(-value)).astype(bf16)
    for c in range(0, pre_act.shape[1], piece):
        cols = slice(c, c + piece)
        pre = pre_act[:, cols]
        cdf = 0.5 * (1.0 + lax.erf(pre * math.sqrt(0.5)))
        slope[:, cols] = cdf + pre * (jnp.exp(-0.5 * pre * pre) * (1.0 / math.sqrt(2.0 * math.pi)))
    pair = 2 * (width // HEADS)
    first_half = half_lanes(pair)
    for head in range(HEADS):
        cols = slice(head // 2 * pair, (head // 2 + 1) * pair)
        own = first_half if head % 2 == 0 else ~first_half
        for i, rows in causal_blocks(tokens, 256):
            here = slice(i, i + rows)
            keys = key_feat[here, cols]
            scores = mm(jnp.where(own, keys, jnp.zeros_like(keys)), query_feat[i:, cols], NT)
            weights_t[head * tokens + i : head * tokens + i + rows, i:] = (scores * mask_t[here, i:]).astype(bf16)


def slopes(query_feat, key_feat, mask_t, pre_act):
    tokens, width = query_feat.shape
    return pl.pallas_call(
        slopes_kernel,
        out_shape=[near((HEADS * tokens, tokens), bf16)]
        + [near((tokens, width), bf16)] * 2
        + [near(pre_act.shape, f32)],
        compiler_params=params(16),
        cost_estimate=NO_COST,
        name="slopes",
    )(*all_vmem((query_feat, key_feat, mask_t, pre_act)))


def middle_kernel(part0, part1, part2, part3, own_first, cotangent, vec, block_out, d_second, sums, *d_branch):
    branch = part0[...] + part1[...].astype(f32) + part2[...].astype(f32) + part3[...].astype(f32)
    unit, spread = norm_parts(own_first[...] + branch)
    gain = vec[2:3, :]
    block_out[...] = unit * gain + vec[3:4, :]
    grad = cotangent[...].astype(f32)
    inner = norm_back(grad, unit, spread, gain)
    d_second[...] = inner
    for copy in d_branch:
        copy[...] = inner.astype(bf16)
    sums[...] = jnp.zeros_like(sums)
    sums[2:3, :] = jnp.sum(grad * unit, axis=0, keepdims=True)
    sums[3:4, :] = jnp.sum(grad, axis=0, keepdims=True)


def middle(parts, own_first, cotangent, vec, held):
    local, width = own_first.shape
    return pl.pallas_call(
        holding(middle_kernel, 7, len(held)),
        out_shape=[near((local, width), f32), near((local, width), f32), near((8, width), f32)]
        + [near((local, width), bf16)] * 4,
        compiler_params=params(8),
        name="middle",
    )(in_vmem(parts[0]), *parts[1:], in_vmem(own_first), cotangent, vec, *all_vmem(held))


def feed_back_kernel(
    local, d0, d1, d2, d3, slope, up_low, down_low, d_branch, d_pre, part0, part1, part2, part3, total
):
    rank = lax.axis_index("mp")
    tokens, width = d_branch.shape
    ranks = tokens // local

    for step, block in zip(BACK_STEPS, (d0, d1, d2, d3)):
        d_branch[rank_rows(source(rank, step, ranks), local), :] = block[...]
    piece = 256
    for c in range(0, d_pre.shape[1], piece):
        cols = slice(c, c + piece)
        d_pre[:, cols] = (mm(d_branch[...], down_low[cols, :], NT) * slope[:, cols]).astype(bf16)
    total[...] = mm(d_pre[...], up_low[...], NT)
    for step, part in zip(FIRST_STEPS, (part0, part1, part2, part3)):
        part[...] = total[rank_rows(target(rank, step, ranks), local), :].astype(part.dtype)


def feed_back(blocks, slope, up_low, down_low, held):
    local, width = blocks[0].shape
    tokens, hidden = slope.shape
    return pl.pallas_call(
        holding(functools.partial(feed_back_kernel, local), 7, len(held)),
        out_shape=[near((tokens, width), bf16), near((tokens, hidden), bf16), near((local, width), f32)]
        + [near((local, width), bf16)] * 3,
        scratch_shapes=[pltpu.VMEM((tokens, width), f32)],
        compiler_params=params(16),
        cost_estimate=pl.CostEstimate(flops=1_200_000_000, bytes_accessed=9_000_000, transcendentals=0),
        name="feed_back",
    )(in_vmem(blocks[0]), *blocks[1:], *all_vmem((slope, up_low, down_low, *held)))


def feed_grads_kernel(first_low, d_pre, hidden_low, d_branch, keep_up, keep_down, send_up, send_down):
    for left, right, keep, send in (
        (first_low, d_pre, keep_up, send_up),
        (hidden_low, d_branch, keep_down, send_down),
    ):
        keep[...] = mm(left[:, half_rows(left.shape[1], True)], right[...], TN)
        send[...] = mm(left[:, half_rows(left.shape[1], False)], right[...], TN).astype(bf16)


def feed_grads(first_low, d_pre, hidden_low, d_branch):
    width, hidden = first_low.shape[1], d_pre.shape[1]
    return pl.pallas_call(
        feed_grads_kernel,
        out_shape=[near((width // 2, hidden), f32), near((hidden // 2, width), f32)]
        + [near((width // 2, hidden), bf16), near((hidden // 2, width), bf16)],
        compiler_params=params(16),
        cost_estimate=NO_COST,
        name="feed_grads",
    )(*all_vmem((first_low, d_pre, hidden_low, d_branch)))


def first_back_kernel(part0, part1, part2, part3, d_second, own_sum, sums_in, vec, d_resid, sums, *d_attn):
    grad = d_second[...] + part0[...] + part1[...].astype(f32) + part2[...].astype(f32) + part3[...].astype(f32)
    unit, spread = norm_parts(own_sum[...])
    inner = norm_back(grad, unit, spread, vec[0:1, :])
    d_resid[...] = inner
    for copy in d_attn:
        copy[...] = inner.astype(bf16)
    sums[...] = sums_in[...]
    sums[0:1, :] = jnp.sum(grad * unit, axis=0, keepdims=True)
    sums[1:2, :] = jnp.sum(grad, axis=0, keepdims=True)


def first_back(parts, d_second, own_sum, sums, vec, held):
    local, width = own_sum.shape
    return pl.pallas_call(
        holding(first_back_kernel, 8, len(held)),
        out_shape=[near((local, width), f32), near((8, width), f32)] + [near((local, width), bf16)] * 4,
        compiler_params=params(8),
        name="first_back",
    )(in_vmem(parts[0]), *parts[1:], *all_vmem((d_second, own_sum, sums)), vec, *all_vmem(held))


def own_columns_kernel(x_all, mixed_low, block_near, x_slice, mixed_slice, block_out, turned):
    block_out[...] = block_near[...]
    rows = x_slice.shape[0]
    mine = pl.ds(pl.multiple_of(lax.axis_index("mp") * rows, rows), rows)
    for source, target in ((x_all, x_slice), (mixed_low, mixed_slice)):
        turned[...] = jnp.transpose(source[...])
        target[...] = turned[mine, :]


def own_columns(x_all, mixed_low, block_near, own_width):
    tokens, width = x_all.shape
    return pl.pallas_call(
        own_columns_kernel,
        out_shape=[near((own_width, tokens), bf16)] * 2 + [sds(block_near.shape, f32)],
        scratch_shapes=[pltpu.VMEM((width, tokens), bf16)],
        compiler_params=params(8),
        cost_estimate=NO_COST,
        name="own_columns",
    )(*all_vmem((x_all, mixed_low, block_near)))


def mix_heads(
    start, d_num, d_den, query_feat, key_feat, value_low, query_slope, key_slope, weights_t, mask, mask_t, d_query, d_key,
    d_value,
):
    tokens, width = query_feat.shape
    pair = 2 * (width // HEADS)
    first_half = half_lanes(pair)
    spans = causal_blocks(tokens, 256)
    for c in range(start, start + width // 2, pair):
        cols = slice(c, c + pair)
        queries = query_feat[:, cols]
        keys = key_feat[:, cols]
        values = value_low[:, cols]
        nums = d_num[:, cols]
        left = jnp.concatenate([nums, d_den[:, cols]], axis=1)
        zero = jnp.zeros_like(keys)
        minus = jnp.full_like(values, -1)
        sides = (first_half, ~first_half)
        own_query = [jnp.where(own, queries, zero) for own in sides]
        own_key = [jnp.where(own, keys, zero) for own in sides]
        own_num = [jnp.where(own, nums, zero) for own in sides]
        right = [
            jnp.concatenate([jnp.where(own, values, zero), jnp.where(own, minus, zero)], axis=1) for own in sides
        ]
        base = 2 * (c // pair) * tokens
        out = slice(c - start, c - start + pair)
        for i, rows in spans:
            here = slice(i, i + rows)
            upto = i + rows
            allowed = mask[here, :upto]
            d_scores = mm(left[here], jnp.concatenate([block[:upto] for block in right], axis=0), NT)
            d_scores = (d_scores * jnp.concatenate([allowed, allowed], axis=1)).astype(bf16)
            grad = mm(d_scores, jnp.concatenate([block[:upto] for block in own_key], axis=0))
            d_query[here, out] = (grad * query_slope[here, cols].astype(f32)).astype(bf16)
            weights = jnp.concatenate(
                [weights_t[base + half * tokens + i : base + half * tokens + i + rows, i:] for half in range(2)], axis=1
            )
            grad = mm(weights, jnp.concatenate([block[i:] for block in own_num], axis=0))
            d_value[here, out] = grad.astype(bf16)
            allowed = mask_t[here, i:]
            d_scores_t = mm(jnp.concatenate([block[here] for block in right], axis=0), left[i:], NT)
            d_scores_t = [(d_scores_t[half * rows : (half + 1) * rows] * allowed).astype(bf16) for half in range(2)]
            grad = mm(
                jnp.concatenate(d_scores_t, axis=1), jnp.concatenate([block[i:] for block in own_query], axis=0)
            )
            d_key[here, out] = (grad * key_slope[here, cols].astype(f32)).astype(bf16)


def mix_first_kernel(
    local,
    a0,
    a1,
    a2,
    a3,
    attn_low,
    mixed_low,
    inverse,
    query_feat,
    key_feat,
    value_low,
    query_slope,
    key_slope,
    weights_t,
    mask,
    mask_t,
    d_attn,
    d_num,
    d_den,
    d_query,
    d_key,
    d_value,
):
    rank = lax.axis_index("mp")
    tokens, width = d_attn.shape
    ranks = tokens // local
    for step, block in zip(MIX_STEPS, (a0, a1, a2, a3)):
        d_attn[rank_rows(source(rank, step, ranks), local), :] = block[...]
    piece = 768
    for c in range(0, width, piece):
        cols = slice(c, c + piece)
        d_mixed = mm(d_attn[...], attn_low[3, cols, :], NT) * inverse[:, cols]
        d_num[:, cols] = d_mixed.astype(bf16)
        d_den[:, cols] = (d_mixed * mixed_low[:, cols].astype(f32)).astype(bf16)
    mix_heads(
        0, d_num, d_den, query_feat, key_feat, value_low, query_slope, key_slope, weights_t, mask, mask_t, d_query,
        d_key, d_value,
    )


def mix_first(blocks, attn_low, mixed_low, inverse, feats):
    local, width = blocks[0].shape
    tokens = mixed_low.shape[0]
    return pl.pallas_call(
        functools.partial(mix_first_kernel, local),
        out_shape=[near((tokens, width), bf16)] * 3 + [near((tokens, width // 2), bf16)] * 3,
        compiler_params=params(16),
        cost_estimate=pl.CostEstimate(flops=6_000_000_000, bytes_accessed=18_000_000, transcendentals=0),
        name="mix_first",
    )(in_vmem(blocks[0]), *blocks[1:], *all_vmem((attn_low, mixed_low, inverse, *feats)))


def mix_second_kernel(
    d_attn,
    d_num,
    d_den,
    first_query,
    first_key,
    first_value,
    attn_low,
    query_feat,
    key_feat,
    value_low,
    query_slope,
    key_slope,
    weights_t,
    mask,
    mask_t,
    x_slice,
    mixed_slice,
    sums,
    d_query,
    d_key,
    d_value,
    vec,
    keep,
    send,
    attn_grad,
):
    width = d_attn.shape[1]
    own_width = x_slice.shape[0]
    half = width // 2
    for source, target in ((first_query, d_query), (first_key, d_key), (first_value, d_value)):
        target[:, 0:half] = source[...]
    mix_heads(
        half, d_num, d_den, query_feat, key_feat, value_low, query_slope, key_slope, weights_t, mask, mask_t,
        d_query.at[:, half:width], d_key.at[:, half:width], d_value.at[:, half:width],
    )
    for k, grad in enumerate((d_query, d_key, d_value)):
        attn_grad[k * own_width : (k + 1) * own_width, :] = mm(x_slice[...], grad[...])
    attn_grad[3 * own_width : 4 * own_width, :] = mm(mixed_slice[...], d_attn[...])
    write_halves(attn_grad, keep, send)
    held, packed = two_parts(sums[0:4, :])
    send[2 * own_width :, :] = packed
    vec[0:4, :] = held
    vec[4:8, :] = jnp.zeros_like(held)


def mix_second(first, attn_low, feats, x_slice, mixed_slice, sums):
    tokens, width = first[0].shape
    own_width = x_slice.shape[0]
    return pl.pallas_call(
        mix_second_kernel,
        out_shape=[near((tokens, width), bf16)] * 3
        + [
            near((8, width), f32),
            near((2 * own_width, width), f32),
            near((2 * own_width + VEC_ROWS, width), bf16),
        ],
        scratch_shapes=[pltpu.VMEM((4 * own_width, width), f32)],
        compiler_params=params(16),
        cost_estimate=pl.CostEstimate(flops=6_000_000_000, bytes_accessed=18_000_000, transcendentals=0),
        name="mix_second",
    )(*all_vmem((*first, attn_low, *feats, x_slice, mixed_slice, sums)))


def tokens_back_kernel(
    d_query, d_key, d_value, attn_low, d_resid, attn_weight, up_weight, down_weight, tokens_grad, own_attn, own_up, own_down,
    sems,
):
    local, own_width = d_resid.shape[0], own_attn.shape[1]
    rank = lax.axis_index("mp")
    columns = pl.ds(pl.multiple_of(rank * own_width, own_width), own_width)
    copies = [
        pltpu.make_async_copy(attn_weight.at[:, columns, :], own_attn, sems.at[0]),
        pltpu.make_async_copy(up_weight, own_up, sems.at[1]),
        pltpu.make_async_copy(down_weight, own_down, sems.at[2]),
    ]
    for copy in copies:
        copy.start()
    mine = pl.ds(pl.multiple_of(rank * local, local), local)
    tokens_grad[...] = (
        d_resid[...]
        + mm(d_query[mine, :], attn_low[0], NT)
        + mm(d_key[mine, :], attn_low[1], NT)
        + mm(d_value[mine, :], attn_low[2], NT)
    )
    for copy in copies:
        copy.wait()


def tokens_back(d_query, d_key, d_value, attn_low, d_resid, attn_weight, up_weight, down_weight, own_width):
    return pl.pallas_call(
        tokens_back_kernel,
        in_specs=[pl.BlockSpec(memory_space=pltpu.VMEM)] * 5 + [pl.BlockSpec(memory_space=pl.ANY)] * 3,
        out_shape=[
            sds(d_resid.shape, f32),
            near((4, own_width, d_resid.shape[1]), f32),
            near(up_weight.shape, f32),
            near(down_weight.shape, f32),
        ],
        scratch_shapes=[pltpu.SemaphoreType.DMA((3,))],
        compiler_params=params(16),
        cost_estimate=NO_COST,
        name="tokens_back",
    )(
        *all_vmem((d_query, d_key, d_value, attn_low, d_resid)), in_hbm(attn_weight), in_hbm(up_weight),
        in_hbm(down_weight),
    )


def as_row(column):
    return jnp.transpose(jnp.broadcast_to(column, (column.shape[0], 128)))[0:1, :]


def as_column(row):
    return jnp.transpose(jnp.broadcast_to(row, (128, row.shape[1])))[:, 0:1]


SHARE_ROWS = 32


def lane_scalars(values, width):
    lane = lax.broadcasted_iota(jnp.int32, (1, width), 1)
    row = jnp.zeros((1, width), f32)
    for k, value in enumerate(values):
        row = jnp.where(lane == k, value, row)
    return row


def lane_scalar(row, k):
    lane = lax.broadcasted_iota(jnp.int32, row.shape, 1)
    return jnp.sum(jnp.where(lane == k, row, 0.0), axis=1, keepdims=True)


def attn_stats_kernel(even, odd, vec, stats, feed_shares, total, rows_new, shares, columns, rows16):
    own_width, width = total.shape[0] // 4, total.shape[1]
    mine = pl.ds(pl.multiple_of(lax.axis_index("mp") * own_width, own_width), own_width)
    read_halves(even, odd, total)
    scalars = []
    for k in range(4):
        grad = total[k * own_width : (k + 1) * own_width, :]
        square = grad * grad
        columns[...] = as_column(stats[k, 0:1, :])
        rows = decay * columns[mine, :] + (1.0 - decay) * jnp.mean(square + tiny_square, axis=1, keepdims=True)
        rows_new[k : k + 1, :] = as_row(rows)
        rows16[k : k + 1, :] = jnp.sum(square + tiny_square, axis=0, keepdims=True)
        rows16[4 + k : 5 + k, :] = jnp.sum(square * (1.0 / rows), axis=0, keepdims=True)
        scalars.append(jnp.sum(rows, axis=0, keepdims=True))
    rows16[8:12, :] = vec[0:4, :]
    rows16[12:16, :] = feed_shares[0:4, :]
    shares[0:16, :] = rows16[...].astype(bf16)
    row = lane_scalars(scalars, width) + feed_shares[4:5, :]
    high = row.astype(bf16).astype(f32)
    low = (row - high).astype(bf16).astype(f32)
    shares[16:, :] = jnp.concatenate([high, low, jnp.zeros((SHARE_ROWS - 18, width), f32)], axis=0).astype(bf16)


def attn_stats_call(even, odd, vec, stats, feed_shares, own_width):
    width = even.shape[1]
    return pl.pallas_call(
        attn_stats_kernel,
        out_shape=[near((4 * own_width, width), f32), near((4, own_width), f32), near((SHARE_ROWS, width), bf16)],
        scratch_shapes=[pltpu.VMEM((width, 1), f32), pltpu.VMEM((16, width), f32)],
        compiler_params=params(16),
        name="attn_stats",
    )(in_vmem(even), odd, in_vmem(vec), stats, in_vmem(feed_shares))


def attn_out_kernel(total, rows, grad_out, rows_out):
    own_width = grad_out.shape[1]
    for k in range(4):
        grad_out[k] = total[k * own_width : (k + 1) * own_width, :]
    rows_out[...] = rows[...]


def attn_out(total, rows):
    own_width, width = rows.shape[1], total.shape[1]
    return pl.pallas_call(
        attn_out_kernel,
        out_shape=[sds((4, own_width, width), f32), sds((4, own_width), f32)],
        compiler_params=params(8),
        cost_estimate=NO_COST,
        name="attn_out",
    )(*all_vmem((total, rows)))


def feed_stats_kernel(mine, other, wide_old, squares, up_grad_out, down_grad_out, wide_out, grads, wide_new, shares):
    width, hidden = up_grad_out.shape
    for part, rows in enumerate((width, hidden)):
        half = slice(part * width // 2, (part * width + rows) // 2)
        read_halves(mine.at[half], other.at[half], grads.at[part * width : part * width + rows])
    grad = grads[0:width, :]
    up_grad_out[...] = grad
    square = grad * grad
    columns = decay * wide_old[0:1, :] + (1.0 - decay) * jnp.mean(square + tiny_square, axis=0, keepdims=True)
    wide_new[0:1, :] = columns
    shares[0:1, :] = as_row(jnp.sum(square + tiny_square, axis=1, keepdims=True))
    shares[1:2, :] = as_row(jnp.sum(square * (1.0 / columns), axis=1, keepdims=True))
    grad = grads[width:, :]
    down_grad_out[...] = grad
    square = grad * grad
    rows = decay * as_column(wide_old[1:2, :]) + (1.0 - decay) * jnp.mean(
        square + tiny_square, axis=1, keepdims=True
    )
    wide_new[1:2, :] = as_row(rows)
    wide_out[...] = wide_new[...]
    shares[2:3, :] = jnp.sum(square + tiny_square, axis=0, keepdims=True)
    shares[3:4, :] = jnp.sum(square * (1.0 / rows), axis=0, keepdims=True)
    scalars = [jnp.sum(rows, axis=0, keepdims=True)]
    for k in range(2):
        scalars.append(jnp.sum(squares[4 + k : 5 + k, :], axis=1, keepdims=True))
    shares[4:5, :] = lane_scalars([0.0] * 4 + scalars, width)
    shares[5:8, :] = jnp.zeros((3, width), f32)


def feed_stats(even, odd, wide_old, squares):
    width, hidden = squares.shape[1], wide_old.shape[1]
    return pl.pallas_call(
        feed_stats_kernel,
        out_shape=[
            sds((width, hidden), f32),
            sds((hidden, width), f32),
            sds((2, hidden), f32),
            near((width + hidden, width), f32),
            near((2, hidden), f32),
            near((8, width), f32),
        ],
        compiler_params=params(16),
        cost_estimate=NO_COST,
        name="feed_stats",
    )(in_vmem(even), odd, wide_old, in_vmem(squares))


def update_kernel(
    hidden_all,
    attn_grad,
    attn_weight,
    attn_rows,
    stats,
    feed_grad,
    up_weight,
    down_weight,
    wide_new,
    narrow_old,
    squares,
    share,
    share1,
    share2,
    share3,
    vec,
    vec_moment,
    *refs,
):
    outs, made, sems = refs[0:11], refs[11:22], refs[22]
    attn_new, attn_new_low, up_new, up_new_low, down_new, down_new_low = made[0:6]
    attn_cols, narrow_new, vec_grad, vec_moment_new, vec_new = made[6:11]
    width = narrow_old.shape[1]
    own_width = attn_rows.shape[1]
    copies = []

    def leave(which, *place):
        source = made[which].at[place] if place else made[which]
        target = outs[which].at[place] if place else outs[which]
        copy = pltpu.make_async_copy(source, target, sems.at[len(copies)])
        copy.start()
        copies.append(copy)

    total = (share[...].astype(f32) + share1[...].astype(f32)) + (share2[...].astype(f32) + share3[...].astype(f32))
    scalars = total[16:17, :] + total[17:18, :]
    entries = float(width * hidden_all)
    rows = decay * narrow_old[0:1, :] + (1.0 - decay) * total[12:13, :] / hidden_all
    narrow_new[0:1, :] = rows
    cols = decay * narrow_old[1:2, :] + (1.0 - decay) * total[14:15, :] / hidden_all
    narrow_new[1:2, :] = cols
    mean_up = jnp.mean(rows, axis=1, keepdims=True)
    mean_down = lane_scalar(scalars, 4) / hidden_all

    def step_size(scaled, weight_square, count):
        clip = jnp.maximum(1.0, jnp.sqrt(scaled / count) / clip_limit)
        return learn_rate * jnp.sqrt(weight_square / count) / clip

    up_size = step_size(
        jnp.sum(total[13:14, :] / rows, axis=1, keepdims=True) * mean_up, lane_scalar(scalars, 5), entries
    )
    down_size = step_size(
        jnp.sum(total[15:16, :] / cols, axis=1, keepdims=True) * mean_down, lane_scalar(scalars, 6), entries
    )

    def block(which, here, grad, weight, row, col, mean, size):
        scale = row * col * (1.0 / mean)
        value = weight - size * (grad * lax.rsqrt(scale))
        made[which][here] = value
        made[which + 1][here] = value.astype(bf16)
        leave(which, *here)
        leave(which + 1, *here)

    pieces = 4
    row = as_column(rows)
    step = up_weight.shape[0] // pieces
    for n in range(pieces):
        here = slice(n * step, (n + 1) * step)
        block(2, (here, slice(None)), feed_grad[here, :], up_weight[here, :], row[here], wide_new[0:1, :], mean_up, up_size)
    row = as_column(wide_new[1:2, :])
    step = down_weight.shape[0] // pieces
    for n in range(pieces):
        here = slice(n * step, (n + 1) * step)
        below = slice(up_weight.shape[0] + n * step, up_weight.shape[0] + (n + 1) * step)
        block(4, (here, slice(None)), feed_grad[below, :], down_weight[here, :], row[here], cols, mean_down, down_size)
    leave(7)
    entries = float(width * width)
    for k in range(4):
        col = decay * stats[k, 1:2, :] + (1.0 - decay) * total[k : k + 1, :] / width
        attn_cols[k : k + 1, :] = col
        mean = lane_scalar(scalars, k) / width
        size = step_size(
            jnp.sum(total[4 + k : 5 + k, :] / col, axis=1, keepdims=True) * mean,
            jnp.sum(squares[k : k + 1, :], axis=1, keepdims=True),
            entries,
        )
        block(
            0, (k,), attn_grad[k * own_width : (k + 1) * own_width, :], attn_weight[k], as_column(attn_rows[k : k + 1, :]),
            col, mean, size,
        )
    leave(6)
    grads = total[8:12, :]
    vec_grad[...] = grads
    leave(8)
    moment = decay * vec_moment[...] + (1.0 - decay) * (grads * grads + tiny_square)
    vec_moment_new[...] = moment
    leave(9)
    scaled = grads * lax.rsqrt(moment)
    clip = jnp.maximum(1.0, jnp.sqrt(jnp.mean(scaled * scaled, axis=1, keepdims=True)) / clip_limit)
    held = vec[...]
    spread = jnp.sqrt(jnp.mean(held * held, axis=1, keepdims=True))
    vec_new[...] = held - learn_rate * spread * scaled / clip
    leave(10)
    for copy in copies:
        copy.wait()


def update(
    attn_grad, attn_weight, attn_rows, stats, feed_grad, up_weight, down_weight, wide_new, narrow_old, squares, shares,
    vec, vec_moment, hidden_all,
):
    _, own_width, width = attn_weight.shape
    hidden = up_weight.shape[1]
    outs = [((4, own_width, width), t) for t in (f32, bf16)]
    outs += [((width, hidden), t) for t in (f32, bf16)] + [((hidden, width), t) for t in (f32, bf16)]
    outs += [((4, width), f32), ((2, width), f32)] + [((4, width), f32)] * 3
    return pl.pallas_call(
        functools.partial(update_kernel, hidden_all),
        in_specs=[pl.BlockSpec(memory_space=pltpu.VMEM)] * 16,
        out_specs=[pl.BlockSpec(memory_space=pl.ANY)] * 11,
        out_shape=[pltpu.HBM(*out) for out in outs],
        scratch_shapes=[pltpu.VMEM(*out) for out in outs]
        + [pltpu.SemaphoreType.DMA((29,))],
        compiler_params=params(24),
        name="update",
    )(
        *all_vmem((attn_grad, attn_weight, attn_rows)), stats,
        *all_vmem((feed_grad, up_weight, down_weight, wide_new)), narrow_old, in_vmem(squares), in_vmem(shares[0]),
        *shares[1:], vec, vec_moment,
    )


def exchange(parts, steps):
    ranks = len(parts)
    moved = [
        lax.ppermute(part, "mp", [(i, target(i, step, ranks)) for i in range(ranks)])
        for part, step in zip(parts[1:], steps[1:])
    ]
    return [parts[0]] + moved


def on_device(
    tokens,
    cotangent,
    seq_starts,
    attn_weight,
    up_weight,
    down_weight,
    vec_params,
    attn_stats,
    ffn_narrow_stats,
    ffn_wide_stats,
    vec_moment,
):
    ranks = lax.axis_size("mp")
    local, width = tokens.shape
    own_width = width // ranks
    hidden_all = up_weight.shape[1] * ranks

    blocks = exchange([tokens] * ranks, TOKEN_STEPS)
    attn_low, up_low, down_low, mask, mask_t, squares = prepare(
        seq_starts, attn_weight, up_weight, down_weight, local * ranks
    )
    (
        x_all,
        query_feat,
        key_feat,
        value_low,
        mixed_low,
        inverse,
        own_sum,
        own_first,
        first_low,
        pre_act,
        hidden_low,
        *parts,
    ) = forward(blocks, attn_low, up_low, down_low, mask, vec_params)
    parts = exchange(parts, BRANCH_STEPS)
    weights_t, query_slope, key_slope, slope = slopes(query_feat, key_feat, mask_t, pre_act)
    own_first, slope = lax.optimization_barrier((own_first, slope))
    feats = (query_feat, key_feat, value_low, query_slope, key_slope, weights_t, mask, mask_t)
    mixing = (attn_low, mixed_low, inverse, *feats)
    feeding = (up_low, down_low, first_low, slope, hidden_low)
    block_near, d_second, sums, *d_branch = middle(
        parts, own_first, cotangent, vec_params, (*mixing, *feeding, own_sum, x_all)
    )
    turned_from, d_second = lax.optimization_barrier((x_all, d_second))
    x_slice, mixed_slice, block_out = own_columns(turned_from, mixed_low, block_near, own_width)
    slope, x_slice = lax.optimization_barrier((slope, x_slice))
    d_branch, d_pre, *parts = feed_back(
        exchange(d_branch, BACK_STEPS), slope, up_low, down_low, (*mixing, first_low, hidden_low, own_sum, d_second, sums, x_slice, mixed_slice)
    )
    staged = lax.axis_size("dp") == STAGED

    parts = exchange(parts, FIRST_STEPS)
    *feed_keep, up_send, down_send = feed_grads(first_low, d_pre, hidden_low, d_branch)
    if staged:
        up = fold_first(feed_keep[0], across(up_send, 1))
        down = fold_first(feed_keep[1], across(down_send, 1))
        parts[0], up, down = lax.optimization_barrier((parts[0], up, down))
        got_up, got_down = [[across(a, 2), across(b, 4)] for a, b in (up, down)]
    d_resid, sums, *d_attn = first_back(
        parts, d_second, own_sum, sums, vec_params, (*mixing, x_slice, mixed_slice)
    )
    blocks = exchange(d_attn, MIX_STEPS)
    if staged:
        d_resid, up, down = lax.optimization_barrier((d_resid, up, down))
        feed_a, feed_b = fold_feed((*up, *down), (*got_up, *got_down))
        blocks[0], feed_a, feed_b = lax.optimization_barrier((blocks[0], feed_a, feed_b))
        got_a, got_b = across(feed_a, 4), across(feed_b, 2)
    first = mix_first(blocks, attn_low, mixed_low, inverse, feats)
    *d_mix, vec_part, attn_keep, attn_send = mix_second(first, attn_low, feats, x_slice, mixed_slice, sums)
    if staged:
        feed_even = fold_feed_last(feed_a, got_a, feed_b, got_b)
        received = across(attn_send, 1)
        attn_keep, feed_even = lax.optimization_barrier((attn_keep, feed_even))
        vec_part, attn_a, attn_b = fold_first(attn_keep, received, vec_part)
        feed_odd = across(feed_even, 1)
        got_a, got_b = across(attn_a, 2), across(attn_b, 4)
    else:
        feed_even, feed_odd, attn_even, attn_odd, vec_part = lax.psum(
            (jnp.concatenate(feed_keep), jnp.concatenate([up_send, down_send]).astype(f32), attn_keep, attn_send[: 2 * own_width].astype(f32), vec_part), "dp"
        )
    up_grad, down_grad, wide_out, feed_near, wide_near, feed_shares = feed_stats(
        feed_even, feed_odd, ffn_wide_stats, squares
    )
    tokens_grad, own_attn, own_up, own_down = tokens_back(
        *d_mix, attn_low, d_resid, attn_weight, up_weight, down_weight, own_width
    )
    if staged:
        attn_a, tokens_grad = lax.optimization_barrier((attn_a, tokens_grad))
        vec_part, attn_a, attn_b = fold_second(attn_a, got_a, attn_b, got_b, vec_part)
        got_a, got_b = across(attn_a, 4), across(attn_b, 2)
        attn_a, feed_shares = lax.optimization_barrier((attn_a, feed_shares))
        vec_part, attn_even = fold_last(attn_a, got_a, attn_b, got_b, vec_part)
        attn_odd = across(attn_even, 1)
    attn_near, rows_near, shares = attn_stats_call(attn_even, attn_odd, vec_part, attn_stats, feed_shares, own_width)
    shares = exchange([shares] * ranks, SHARE_STEPS)
    attn_grad, attn_rows = attn_out(attn_near, rows_near)
    attn_near, attn_grad = lax.optimization_barrier((attn_near, attn_grad))
    (
        attn_new,
        attn_new_low,
        up_new,
        up_new_low,
        down_new,
        down_new_low,
        attn_cols,
        narrow_new,
        vec_grad,
        vec_moment_new,
        vec_new,
    ) = update(
        attn_near, own_attn, rows_near, attn_stats, feed_near, own_up, own_down, wide_near, ffn_narrow_stats,
        squares, shares, vec_params, vec_moment, hidden_all,
    )
    return (
        block_out,
        tokens_grad,
        attn_grad,
        attn_rows,
        attn_cols,
        attn_new,
        attn_new_low,
        up_grad,
        down_grad,
        narrow_new,
        wide_out,
        up_new,
        down_new,
        up_new_low,
        down_new_low,
        vec_grad,
        vec_moment_new,
        vec_new,
    )


def solution(mesh):
    in_specs = (
        P(("dp", "mp"), None),
        P(("dp", "mp"), None),
        P("dp", None),
        P(),
        P(None, "mp"),
        P("mp", None),
        P(),
        P(),
        P(),
        P(None, "mp"),
        P(),
    )
    out_specs = (
        P(("dp", "mp"), None),
        P(("dp", "mp"), None),
        P(None, "mp", None),
        P(None, "mp"),
        P(),
        P(None, "mp", None),
        P(None, "mp", None),
        P(None, "mp"),
        P("mp", None),
        P(),
        P(None, "mp"),
        P(None, "mp"),
        P("mp", None),
        P(None, "mp"),
        P("mp", None),
        P(),
        P(),
        P(),
    )
    return jax.shard_map(
        on_device, mesh=mesh, in_specs=in_specs, out_specs=out_specs, check_vma=False
    )
```
